32 devices in a mesh: dp: 8 (over z, x), tensor: 4 (over y, core).
Axes of the slice: x: 2, y: 2, z: 4, core: 2. Of those that a mesh axis runs over, the one named last changes fastest.
Arguments:
- frames: bfloat16 [24000, 512], P(('dp', 'tensor')), may hold values from -6 to 6
- query_weight: bfloat16 [512, 512], P(None, 'tensor'), may hold values from -0.25 to 0.25
- query_bias: bfloat16 [512], P('tensor'), may hold values from -3 to 3
- key_weight: bfloat16 [512, 512], P(None, 'tensor'), may hold values from -0.25 to 0.25
- value_weight: bfloat16 [512, 512], P(None, 'tensor'), may hold values from -0.25 to 0.25
- value_bias: bfloat16 [512], P('tensor'), may hold values from -3 to 3
- out_weight: bfloat16 [512, 512], P('tensor'), may hold values from -1.5 to 1.5
- out_bias: bfloat16 [512], replicated, may hold values from -3 to 3
- first_gain: bfloat16 [512], replicated, may hold values from 0.099609375 to 1.8984375
- first_shift: bfloat16 [512], replicated, may hold values from -3 to 3
- expand_weight: bfloat16 [512, 2048], P(None, 'tensor'), may hold values from -0.25 to 0.25
- expand_bias: bfloat16 [2048], P('tensor'), may hold values from -3 to 3
- reduce_weight: bfloat16 [2048, 512], P('tensor'), may hold values from -0.125 to 0.125
- reduce_bias: bfloat16 [512], replicated, may hold values from -3 to 3
- second_gain: bfloat16 [512], replicated, may hold values from 0.099609375 to 1.8984375
- second_shift: bfloat16 [512], replicated, may hold values from -3 to 3
- span_start: int32 [16], P('dp'), may hold values from 0 to 749, as said below
- span_end: int32 [16], P('dp'), may hold values from 1 to 1500, as said below
- empty_flag: int32 [16], P('dp'), may hold values 0 or 1
- cotangent: bfloat16 [24000, 512], P(('dp', 'tensor')), may hold values from -6 to 6
Outputs:
- output: bfloat16 [24000, 512], P(('dp', 'tensor'))
- grad_frames: float32 [24000, 512], P(('dp', 'tensor'))
- grad_query_weight: float32 [512, 512], P(None, 'tensor')
- grad_query_bias: float32 [512], P('tensor')
- grad_key_weight: float32 [512, 512], P(None, 'tensor')
- grad_value_weight: float32 [512, 512], P(None, 'tensor')
- grad_value_bias: float32 [512], P('tensor')
- grad_out_weight: float32 [512, 512], P('tensor')
- grad_out_bias: float32 [512], replicated
- grad_first_gain: float32 [512], replicated
- grad_first_shift: float32 [512], replicated
- grad_expand_weight: float32 [512, 2048], P(None, 'tensor')
- grad_expand_bias: float32 [2048], P('tensor')
- grad_reduce_weight: float32 [2048, 512], P('tensor')
- grad_reduce_bias: float32 [512], replicated
- grad_second_gain: float32 [512], replicated
- grad_second_shift: float32 [512], replicated
The draws below stay inside these ranges and needn't reach their ends.
Inputs may be any that keep to these rules, and one draw needn't show every extreme that they name: `span_start`: some clip's span starts at frame 0, and another clip's at frame 1500 // 2 - 1. `span_end`: each span ends after it starts; some clip's span ends at frame 1, and another clip's at 1500.
All inputs are finite; a program needn't handle non-finite values. No bound on the sum of `empty_flag` on one device may be relied on, other than what follows from the above.
Results may differ from the reference program's by a relative error of at most 0.015.
Values may be sent and summed in bfloat16 or wider, within the bound.
No kernel may reach another device: no remote copies, remote signals or barrier semaphores. Data moves between devices by JAX's collectives and lax.ppermute only.
A program may use at most 128 MiB of HBM per device.

```python
import jax
import jax.numpy as jnp
from jax import lax

D = 512
HEADS = 8
FF = 2048
FRAMES = 1500
CLIPS = 16
TOKENS = 24000


def spans(key):
    first_key, second_key, third_key = jax.random.split(key, 3)
    starts = jax.random.randint(first_key, (CLIPS,), 0, FRAMES // 2)
    widths = jax.random.randint(second_key, (CLIPS,), 1, FRAMES // 2 + 1)
    opening = jax.random.randint(third_key, (), 0, CLIPS)
    latest = (opening + 1) % CLIPS
    closing = (opening + 2) % CLIPS
    slots = jnp.arange(CLIPS)
    starts = jnp.where(slots == opening, 0, starts)
    starts = jnp.where(slots == latest, FRAMES // 2 - 1, starts)
    ends = jnp.where(slots == opening, 1, starts + widths)
    ends = jnp.where(slots == closing, FRAMES, ends)
    return (starts, ends)


def draw_span_start(key, part):
    starts, ends = spans(key)
    return starts.astype(jnp.int32)


def draw_span_end(key, part):
    starts, ends = spans(key)
    return ends.astype(jnp.int32)


def set_ends(result, stream_key, least, largest):
    longest = result.shape.index(max(result.shape))
    spots = []
    for shift in (0, 1):
        where = [jax.random.randint(jax.random.fold_in(stream_key, axis), (), 0, length) for axis, length in enumerate(result.shape)]
        where[longest] = (where[longest] + shift) % result.shape[longest]
        spots.append(tuple(where))
    return result.at[spots[0]].set(least).at[spots[1]].set(largest)


def levels(rng, extent, cuts, least, high):
    def one(dim, shards_of):
        heights = jax.random.uniform(jax.random.fold_in(jax.random.fold_in(rng, 6), dim), (shards_of,), jnp.float32, least / len(cuts), high / len(cuts))
        return jnp.repeat(jnp.exp(heights), extent[dim] // shards_of).reshape((-1,) + (1,) * (len(extent) - dim - 1))

    level = one(*cuts[0])
    for cut in cuts[1:]:
        level = level * one(*cut)
    return level


def bell_draw(rng, extent, scale, limit, cuts=(), held_as=jnp.bfloat16):
    factor_of = levels(rng, extent, cuts, -0.22, 0.18) if cuts else 1.0
    entries = jax.random.normal(rng, extent, jnp.float32) * scale * factor_of
    return jnp.minimum(jnp.maximum(entries, -limit), limit).astype(held_as)


def setup_inputs(seed: int = 0) -> dict:
    key_list = jax.random.split(jax.random.key(seed), 21)
    return {
        "frames": bell_draw(key_list[0], (TOKENS, D), 1.0, 6.0, ((0, 32),)),
        "query_weight": bell_draw(key_list[1], (D, D), D ** -0.5, 0.25, ((1, 4),)),
        "query_bias": bell_draw(key_list[2], (D,), 0.5, 3.0, ((0, 4),)),
        "key_weight": bell_draw(key_list[3], (D, D), D ** -0.5, 0.25, ((1, 4),)),
        "value_weight": bell_draw(key_list[4], (D, D), D ** -0.5, 0.25, ((1, 4),)),
        "value_bias": bell_draw(key_list[5], (D,), 0.5, 3.0, ((0, 4),)),
        "out_weight": bell_draw(key_list[6], (D, D), 16 ** -0.5, 1.5, ((0, 4),)),
        "out_bias": bell_draw(key_list[7], (D,), 0.5, 3.0),
        "first_gain": jnp.clip(1.0 + 0.18 * jax.random.normal(key_list[8], (D,), jnp.float32), 0.099609375, 1.8984375).astype(jnp.bfloat16),
        "first_shift": bell_draw(key_list[9], (D,), 0.5, 3.0),
        "expand_weight": bell_draw(key_list[10], (D, FF), D ** -0.5, 0.25, ((1, 4),)),
        "expand_bias": bell_draw(key_list[11], (FF,), 0.5, 3.0, ((0, 4),)),
        "reduce_weight": bell_draw(key_list[12], (FF, D), FF ** -0.5, 0.125, ((0, 4),)),
        "reduce_bias": bell_draw(key_list[13], (D,), 0.5, 3.0),
        "second_gain": jnp.clip(1.0 + 0.18 * jax.random.normal(key_list[14], (D,), jnp.float32), 0.099609375, 1.8984375).astype(jnp.bfloat16),
        "second_shift": bell_draw(key_list[15], (D,), 0.5, 3.0),
        "span_start": draw_span_start(jax.random.fold_in(key_list[20], 71), 0),
        "span_end": draw_span_end(jax.random.fold_in(key_list[20], 71), 0),
        "empty_flag": set_ends((jax.random.randint(key_list[18], (CLIPS,), 0, 8) < 1).astype(jnp.int32), jax.random.fold_in(key_list[18], 1), 0, 1),
        "cotangent": bell_draw(key_list[19], (TOKENS, D), 1.0, 6.0, ((0, 32),)),
    }


EPS = 1e-05
HIGH = lax.Precision.HIGHEST

@jax.custom_vjp
def low(v):
    return lax.optimization_barrier(v.astype(jnp.bfloat16)).astype(jnp.float32)

@jax.custom_vjp
def low_back(v):
    return v

def low_keep(v):
    return (low(v), None)

def low_pass(kept, grad):
    return (grad,)

def back_keep(v):
    return (v, None)

def back_low(kept, grad):
    return (low(grad),)
low.defvjp(low_keep, low_pass)
low_back.defvjp(back_keep, back_low)

def layer_norm(values_in, gain, shift):
    center = lax.optimization_barrier(jnp.mean(values_in, axis=-1, keepdims=True))
    centered = values_in - center
    spread = lax.optimization_barrier(jnp.mean(centered * centered, axis=-1, keepdims=True))
    return centered * lax.rsqrt(spread + EPS) * gain + shift

def matmul(left, right):
    return jnp.dot(left, right, precision=HIGH, preferred_element_type=jnp.float32)

def reference(frames, query_weight, query_bias, key_weight, value_weight, value_bias, out_weight, out_bias, first_gain, first_shift, expand_weight, expand_bias, reduce_weight, reduce_bias, second_gain, second_shift, span_start, span_end, empty_flag, cotangent):
    positions = jnp.arange(FRAMES, dtype=jnp.int32)
    inside = (positions[None, :] >= span_start[:, None]) & (positions[None, :] < span_end[:, None])
    valid = jnp.logical_not(inside) & (empty_flag[:, None] == 0)
    counts = lax.optimization_barrier(jnp.sum(valid.astype(jnp.int32), axis=1))
    head_width = D // HEADS
    score_scale = float(head_width) ** (-0.5)
    shape = (CLIPS, FRAMES, HEADS, head_width)

    def attend_clip(item):
        query, keys, values, keep, count = item
        scores = jnp.einsum('qhd,khd->hqk', query, keys, precision=HIGH) * score_scale
        scores = low_back(scores)
        allowed = keep[None, None, :]
        masked = jnp.where(allowed, scores, -1e+30)
        top = jnp.where(count > 0, lax.optimization_barrier(jnp.max(masked, axis=-1, keepdims=True)), 0.0)
        expo = jnp.where(allowed, jnp.exp(jnp.where(allowed, scores - top, 0.0)), 0.0)
        total = jnp.where(count > 0, lax.optimization_barrier(jnp.sum(expo, axis=-1, keepdims=True)), 1.0)
        prob = low(expo / total)
        mixed = jnp.einsum('hqk,khd->qhd', prob, values, precision=HIGH)
        return low_back(low(mixed))
    checked = jax.checkpoint(attend_clip)

    def forward(frames_f, query_w, query_b, key_w, value_w, value_b, out_w, out_b, gain_one, shift_one, expand_w, expand_b, reduce_w, reduce_b, gain_two, shift_two):
        normed = low(layer_norm(frames_f, gain_one, shift_one))
        query = low_back(low(matmul(normed, query_w) + query_b))
        keys = low_back(low(matmul(normed, key_w)))
        values = low_back(low(matmul(normed, value_w) + value_b))
        mixed = lax.map(checked, (query.reshape(shape), keys.reshape(shape), values.reshape(shape), valid, counts))
        attended = low_back(matmul(mixed.reshape(CLIPS * FRAMES, D), out_w))
        hidden = frames_f + attended + out_b
        normed_two = low(layer_norm(hidden, gain_two, shift_two))
        inner = low_back(matmul(normed_two, expand_w) + expand_b)
        active = low(jax.nn.gelu(inner, approximate=False))
        return hidden + matmul(active, reduce_w) + reduce_b
    output, pullback = jax.vjp(forward, frames.astype(jnp.float32), query_weight.astype(jnp.float32), query_bias.astype(jnp.float32), key_weight.astype(jnp.float32), value_weight.astype(jnp.float32), value_bias.astype(jnp.float32), out_weight.astype(jnp.float32), out_bias.astype(jnp.float32), first_gain.astype(jnp.float32), first_shift.astype(jnp.float32), expand_weight.astype(jnp.float32), expand_bias.astype(jnp.float32), reduce_weight.astype(jnp.float32), reduce_bias.astype(jnp.float32), second_gain.astype(jnp.float32), second_shift.astype(jnp.float32))
    g_frames, g_query_w, g_query_b, g_key_w, g_value_w, g_value_b, g_out_w, g_out_b, g_gain_one, g_shift_one, g_expand_w, g_expand_b, g_reduce_w, g_reduce_b, g_gain_two, g_shift_two = pullback(cotangent.astype(jnp.float32))
    return (output.astype(jnp.bfloat16), g_frames, g_query_w, g_query_b, g_key_w, g_value_w, g_value_b, g_out_w, g_out_b, g_gain_one, g_shift_one, g_expand_w, g_expand_b, g_reduce_w, g_reduce_b, g_gain_two, g_shift_two)
```

```python
import functools

import jax
import jax.numpy as jnp
from jax import lax
from jax.experimental import pallas as pl
from jax.experimental.pallas import tpu as pltpu
from jax.sharding import PartitionSpec as P

BF = jnp.bfloat16
F32 = jnp.float32
D = 512
HEADS = 8
HEAD = D // HEADS
EPS = 1e-05
TENSOR = 4
CHUNK = 256
EXTRA = 16
NN = (((1,), (0,)), ((), ()))
NT = (((1,), (1,)), ((), ()))
TN = (((0,), (0,)), ((), ()))
TT = (((0,), (1,)), ((), ()))
VMEM = pl.BlockSpec(memory_space=pltpu.VMEM)
SMEM = pl.BlockSpec(memory_space=pltpu.SMEM)
ANY = pl.BlockSpec(memory_space=pl.ANY)


def dot(left, right, dims):
    return lax.dot_general(left, right, dims, preferred_element_type=F32)


def call(kernel, outs, in_specs, out_specs, scratch=()):
    return pl.pallas_call(
        kernel,
        out_shape=outs,
        in_specs=in_specs,
        out_specs=out_specs,
        scratch_shapes=list(scratch),
        compiler_params=pltpu.CompilerParams(vmem_limit_bytes=56 * 2**20),
    )


def row_keep(rows, half):
    return (lax.broadcasted_iota(jnp.int32, (rows, 1), 0) < half).astype(F32)


def norm_terms(rows_in):
    center = jnp.mean(rows_in, axis=-1, keepdims=True)
    centered = rows_in - center
    spread = jnp.mean(centered * centered, axis=-1, keepdims=True)
    scale = lax.rsqrt(spread + EPS)
    return centered * scale, scale


def norm_back(grad, gain, xhat, scale):
    e = grad * gain
    mean_e = jnp.mean(e, axis=-1, keepdims=True)
    mean_ex = jnp.mean(e * xhat, axis=-1, keepdims=True)
    return scale * (e - mean_e - xhat * mean_ex)


def valid_row(meta_ref, rows, half):
    lane = lax.broadcasted_iota(jnp.int32, (1, 2 * rows), 1)
    second = lane >= rows
    local = jnp.where(second, lane - rows, lane)
    core = meta_ref[3]
    position = local + half * jnp.where(second, 1 - core, core)
    inside = (position >= meta_ref[0]) & (position < meta_ref[1])
    return (local < half) & jnp.logical_not(inside) & (meta_ref[2] == 0)


def pair_columns(packs, first, last, row_from, row_to):
    return jnp.concatenate([p[row_from:row_to, first:last] for p in packs], axis=1)


def attention_forward(half, meta_ref, normed, packs, e_hbm, qT_ref, kT_ref, vT_ref, mixed_ref, inv_ref, s_buf, e_buf, sem):
    rows = qT_ref.shape[1]
    keys = kT_ref.shape[1]
    heads = qT_ref.shape[0] // HEAD
    local = packs[0].shape[1] // TENSOR
    ones16 = (lax.broadcasted_iota(jnp.int32, (EXTRA, keys), 0) == 0).astype(F32).astype(BF)

    def project(index, columns):
        first = index * local
        weight = pair_columns(packs, first, first + local, 0, D)
        return dot(weight, normed(columns), TT)

    def bias(index, columns):
        first = index * local
        row = pair_columns(packs, first, first + local, D, D + EXTRA)
        return dot(row, ones16[:, :columns], TN)

    qT_ref[...] = ((project(0, rows) + bias(0, rows)).astype(BF).astype(F32) * HEAD**-0.5).astype(BF)
    kT_ref[...] = project(1, keys).astype(BF)
    vT_ref[...] = (project(2, keys) + bias(2, keys)).astype(BF)

    valid = valid_row(meta_ref, rows, half)
    some = jnp.max(valid.astype(F32), axis=1, keepdims=True)
    mask_row = jnp.where(valid, 0.0, -1e30)
    first_row = lax.broadcasted_iota(jnp.int32, (EXTRA, keys), 0) == 0
    mask = jnp.where(first_row, mask_row, 0.0).astype(BF)

    wide = CHUNK
    blocks = [(h, c) for h in range(heads) for c in range(rows // wide)]
    tops = {}

    def score(i):
        h, c = blocks[i]
        q = jnp.concatenate([qT_ref[h * HEAD : (h + 1) * HEAD, c * wide : (c + 1) * wide], ones16[:, :wide]], axis=0)
        top = None
        for k in range(keys // CHUNK):
            span = slice(k * CHUNK, (k + 1) * CHUNK)
            s = dot(jnp.concatenate([kT_ref[h * HEAD : (h + 1) * HEAD, span], mask[:, span]], axis=0), q, TN)
            s_buf[i % 2, span, :] = s
            part = jnp.max(s.reshape(CHUNK // 8, 8, wide), axis=0)
            top = part if top is None else jnp.maximum(top, part)
        tops[i] = jnp.max(top, axis=0, keepdims=True)

    copies = []
    score(0)
    for i, (h, c) in enumerate(blocks):
        if i + 1 < len(blocks):
            score(i + 1)
        slot = h % 2
        columns = slice(c * wide, (c + 1) * wide)
        if c == 0 and h >= 2:
            copies[h - 2].wait()
        for k in range(keys // CHUNK):
            span = slice(k * CHUNK, (k + 1) * CHUNK)
            e_buf[slot, span, columns] = jnp.exp(s_buf[i % 2, span, :] - tops[i]).astype(BF)
        value = jnp.concatenate([vT_ref[h * HEAD : (h + 1) * HEAD, :], ones16 * 0 + 1], axis=0)
        o = dot(value, e_buf[slot, :, columns], NN)
        inv = some / o[HEAD : HEAD + 1, :]
        mixed_ref[h * HEAD : (h + 1) * HEAD, columns] = (o[:HEAD] * inv).astype(BF)
        inv_ref[h : h + 1, columns] = inv
        if c == rows // wide - 1:
            copy = pltpu.make_async_copy(e_buf.at[slot], e_hbm.at[h], sem.at[slot])
            copy.start()
            copies.append(copy)
    copies[-2].wait()
    copies[-1].wait()


def near_kernel(half, meta_ref, x_ref, xs_ref, gain_ref, shift_ref, pa0, pa1, n_ref, *rest):
    gain = gain_ref[...].astype(F32)
    shift = shift_ref[...].astype(F32)
    rows = x_ref.shape[0]
    keep = row_keep(rows, half)
    for part, ref in enumerate((x_ref, xs_ref)):
        xhat, _ = norm_terms(ref[...].astype(F32))
        n_ref[part * rows : (part + 1) * rows, :] = ((xhat * gain + shift) * keep).astype(BF)
    attention_forward(half, meta_ref, lambda count: n_ref[:count, :], (pa0, pa1), *rest)


def far_kernel(half, meta_ref, n_ref, pa0, pa1, *rest):
    attention_forward(half, meta_ref, lambda count: n_ref[:count, :], (pa0, pa1), *rest)


def phi_terms(inner):
    bell = jnp.exp(inner * inner * -0.5)
    x = jnp.abs(inner) * 0.7071067811865476
    t = 1.0 / (1.0 + 0.3275911 * x)
    poly = t * (0.254829592 + t * (-0.284496736 + t * (1.421413741 + t * (-1.453152027 + t * 1.061405429))))
    tail = 0.5 * poly * bell
    return jnp.where(inner >= 0, 1.0 - tail, tail), bell * 0.3989422804014327


def ff_pair(n2, cot, n2T, w1, w2, b1, act_buf, gi_buf, grads_ref, bias_ref):
    rows = n2.shape[0]
    ones = jnp.ones((EXTRA, rows), BF)
    branch = None
    back = None
    for s in range(2):
        width = w1[s].shape[1]
        for c in range(width // CHUNK):
            span = slice(c * CHUNK, (c + 1) * CHUNK)
            inner = dot(n2, w1[s][:, span], NN) + b1[s][:, span].astype(F32)
            grad = dot(cot, w2[s][span, :], NT)
            cdf, density = phi_terms(inner)
            act_buf[s, :, span] = (inner * cdf).astype(BF)
            gi_buf[s, :, span] = (grad * (cdf + inner * density)).astype(BF)
        act = act_buf[s]
        gi = gi_buf[s]
        part = dot(act, w2[s][...], NN)
        branch = part if branch is None else branch + part
        part = dot(gi, w1[s][...], NT)
        back = part if back is None else back + part
        grads_ref[s, :D, :] = dot(n2T, gi, NN).astype(BF)
        grads_ref[s, D:, :] = dot(act, cot, TN).astype(BF)
        bias_ref[s : s + 1, :] = dot(ones, gi, NN)[:1]
    return branch, back


def mid_kernel(half, x_ref, cot_ref, mixed0, mixed1, pa0, pa1, pa2, pa3, ob_ref, gain_ref, shift_ref, w10, w11, w20, w21, b10, b11,
               hidden_ref, n2_ref, branch_ref, back_ref, grads_ref, bias_ref, act_buf, gi_buf):
    local = pa0.shape[1] // TENSOR
    total = x_ref[...].astype(F32) + ob_ref[...].astype(F32)
    for m, packs in ((mixed0, (pa0, pa1)), (mixed1, (pa2, pa3))):
        total = total + dot(m[...], pair_columns(packs, 3 * local, 4 * local, 0, D), TT)
    hidden_ref[...] = total
    xhat, _ = norm_terms(total)
    n2 = (xhat * gain_ref[...].astype(F32) + shift_ref[...].astype(F32)).astype(BF)
    n2_ref[...] = n2
    branch, back = ff_pair(n2, cot_ref[...], n2.T, (w10, w11), (w20, w21), (b10, b11), act_buf, gi_buf, grads_ref, bias_ref)
    branch_ref[...] = branch
    back_ref[...] = back


def turn_kernel(half, hidden_ref, n2_ref, cot_ref, branch_in, back_in, mixed0, mixed1, pa0, pa1, pa2, pa3, rb_ref, gain_ref,
                w10, w11, w20, w21, b10, b11,
                out_ref, gh_ref, dT0, dT1, go_ref, grads_ref, bias_ref, small_ref, act_buf, gi_buf):
    local = pa0.shape[1] // TENSOR
    n2 = n2_ref[...]
    cot = cot_ref[...]
    branch, back = ff_pair(n2, cot, n2.T, (w10, w11), (w20, w21), (b10, b11), act_buf, gi_buf, grads_ref, bias_ref)
    hidden = hidden_ref[...]
    out_ref[...] = (hidden + branch_in[...] + branch + rb_ref[...].astype(F32)).astype(BF)[: out_ref.shape[0]]
    back = back + back_in[...]
    xhat, scale = norm_terms(hidden)
    cot_f = cot.astype(F32)
    grad_hidden = cot_f + norm_back(back, gain_ref[...].astype(F32), xhat, scale)
    gh_ref[...] = grad_hidden
    small_ref[0:1, :] = jnp.sum(grad_hidden, axis=0, keepdims=True)
    small_ref[1:2, :] = jnp.sum(back * xhat, axis=0, keepdims=True)
    small_ref[2:3, :] = jnp.sum(back, axis=0, keepdims=True)
    small_ref[3:4, :] = jnp.sum(cot_f, axis=0, keepdims=True)
    low = grad_hidden.astype(BF)
    for m, packs, dT, first in ((mixed0, (pa0, pa1), dT0, 0), (mixed1, (pa2, pa3), dT1, 2)):
        weight = pair_columns(packs, 3 * local, 4 * local, 0, D)
        dT[...] = dot(weight, low, TT).astype(BF)
        go = dot(m[...], low, NN).astype(BF)
        go_ref[first] = go[:local]
        go_ref[first + 1] = go[local:]


def attention_backward(e_hbm, n_ref, qT_ref, kT_ref, vT_ref, mixed_ref, dT_ref, inv_ref, dq_ref, dk_ref, dv_ref, grads_ref, bias_ref, e_buf, ds_buf, sem):
    rows = qT_ref.shape[1]
    keys = kT_ref.shape[1]
    heads = qT_ref.shape[0] // HEAD
    copies = [pltpu.make_async_copy(e_hbm.at[h], e_buf.at[h % 2], sem.at[h % 2]) for h in range(heads)]
    copies[0].start()
    which = lax.broadcasted_iota(jnp.int32, (EXTRA, rows), 0)
    ones2 = (lax.broadcasted_iota(jnp.int32, (EXTRA, CHUNK), 0) < 2).astype(F32).astype(BF)
    for h in range(heads):
        here = slice(h * HEAD, (h + 1) * HEAD)
        slot = h % 2
        if h + 1 < heads:
            copies[h + 1].start()
        copies[h].wait()
        d_low = (dT_ref[here, :].astype(F32) * inv_ref[h : h + 1, :]).astype(BF)
        delta = jnp.sum(d_low.astype(F32) * mixed_ref[here, :].astype(F32), axis=0, keepdims=True)
        high = (-delta).astype(BF).astype(F32)
        extra = jnp.where(which == 0, high, jnp.where(which == 1, -delta - high, 0.0)).astype(BF)
        d_more = jnp.concatenate([d_low, extra], axis=0)
        dv_ref[here, :] = dot(d_low, e_buf[slot], NT).astype(BF)
        for k in range(keys // CHUNK):
            span = slice(k * CHUNK, (k + 1) * CHUNK)
            v = jnp.concatenate([vT_ref[here, span], ones2], axis=0)
            ds_buf[slot, span, :] = (e_buf[slot, span, :].astype(F32) * dot(v, d_more, TN)).astype(BF)
        dq_ref[here, :] = (dot(kT_ref[here, :], ds_buf[slot], NN) * HEAD**-0.5).astype(BF)
        dk_ref[here, :] = dot(qT_ref[here, :], ds_buf[slot], NT).astype(BF)
    nT = n_ref[...].T
    local = grads_ref.shape[2] // 3
    ones = jnp.ones((EXTRA, rows), BF)
    for index, (ref, count) in enumerate(((dq_ref, rows), (dk_ref, keys), (dv_ref, keys))):
        grad = dot(nT[:, :count], ref[...], NT).astype(BF)
        grads_ref[0, :, index * local : (index + 1) * local] = grad[:, :local]
        grads_ref[1, :, index * local : (index + 1) * local] = grad[:, local:]
        sums = sum(dot(ones, ref[:, i * rows : (i + 1) * rows], NT) for i in range(count // rows))
        bias_ref[index : index + 1, :] = sums[:1]


def first_kernel(half, x_ref, xs_ref, pa0, pa1, pa2, pa3, dq0, dk0, dv0, dq1, dk1, dv1, own_ref, sib_ref, small_ref):
    rows = x_ref.shape[0]
    local = pa0.shape[1] // TENSOR
    gain_sum = 0.0
    shift_sum = 0.0
    for part, ref in enumerate((x_ref, xs_ref)):
        columns = slice(part * rows, (part + 1) * rows)
        total = None
        for dq, dk, dv, packs in ((dq0, dk0, dv0, (pa0, pa1)), (dq1, dk1, dv1, (pa2, pa3))):
            for index, source in ((0, dq), (1, dk), (2, dv)):
                if index == 0 and part == 1:
                    continue
                weight = pair_columns(packs, index * local, (index + 1) * local, 0, D)
                term = dot(source[:, columns], weight, TT)
                total = term if total is None else total + term
        if part == 0:
            own_ref[...] = total
        else:
            sib_ref[...] = total.astype(BF)
        xhat, _ = norm_terms(ref[...].astype(F32))
        gain_sum = gain_sum + jnp.sum(total * xhat, axis=0, keepdims=True)
        shift_sum = shift_sum + jnp.sum(total, axis=0, keepdims=True)
    small_ref[0:1, :] = gain_sum
    small_ref[1:2, :] = shift_sum


def last_kernel(x_ref, own_ref, got_ref, gh_ref, gain_ref, out_ref):
    grad = own_ref[...] + got_ref[...].astype(F32)
    xhat, scale = norm_terms(x_ref[...].astype(F32))
    out_ref[...] = (gh_ref[...] + norm_back(grad, gain_ref[...].astype(F32), xhat, scale))[: out_ref.shape[0]]


def swap(value, axis, size, bit):
    return lax.ppermute(value, axis, [(i, i ^ bit) for i in range(size)])


def dp_sum(value, size):
    place = lax.axis_index("dp")
    bit = 1
    while bit < size:
        half = value.shape[0] // 2
        upper = (place & bit) != 0
        send = lax.dynamic_slice_in_dim(value, jnp.where(upper, 0, half), half, 0)
        keep = lax.dynamic_slice_in_dim(value, jnp.where(upper, half, 0), half, 0)
        value = (keep.astype(F32) + swap(send, "dp", size, bit).astype(F32)).astype(BF)
        bit *= 2
    while bit > 1:
        bit //= 2
        upper = (place & bit) != 0
        got = swap(value, "dp", size, bit)
        value = jnp.where(upper, jnp.concatenate([got, value], 0), jnp.concatenate([value, got], 0))
    return value


def on_device(dp, frames, query_weight, query_bias, key_weight, value_weight, value_bias, out_weight, out_bias, first_gain, first_shift,
              expand_weight, expand_bias, reduce_weight, reduce_bias, second_gain, second_shift, span_start, span_end, empty_flag, cotangent):
    half = frames.shape[0]
    rows = -(-half // CHUNK) * CHUNK
    keys = 2 * rows
    local = query_weight.shape[1]
    pair = 2 * local
    pair_heads = pair // HEAD
    width = expand_weight.shape[1]
    device = lax.axis_index("tensor")
    clip = device // 2
    meta = jnp.stack([span_start[clip], span_end[clip], empty_flag[clip], device % 2]).astype(jnp.int32)

    def row(v):
        return v.reshape(1, -1)

    def across(v, bit):
        return swap(v, "tensor", TENSOR, bit)

    bias_row = jnp.concatenate([query_bias, jnp.zeros((local,), BF), value_bias, jnp.zeros((local,), BF)])
    pa0 = jnp.concatenate(
        [
            jnp.concatenate([query_weight, key_weight, value_weight, out_weight.T], axis=1),
            jnp.pad(row(bias_row), ((0, EXTRA - 1), (0, 0))),
        ],
        axis=0,
    )
    x = jnp.pad(frames, ((0, rows - half), (0, 0)))
    cot = jnp.pad(cotangent, ((0, rows - half), (0, 0)))
    xs = across(x, 1)
    pa1 = across(pa0, 1)
    pa2 = across(pa0, 2)
    pa3 = across(pa2, 1)
    pb0 = jnp.concatenate([expand_weight, reduce_weight, jnp.pad(row(expand_bias), ((0, EXTRA - 1), (0, 0)))], axis=0)
    pb1 = across(pb0, 1)
    pb2 = across(pb0, 2)
    pb3 = across(pb2, 1)

    def ff_parts(first, second):
        return (first[:D], second[:D], first[D : 2 * D], second[D : 2 * D], first[2 * D : 2 * D + 1], second[2 * D : 2 * D + 1])

    forward_outs = (
        jax.ShapeDtypeStruct((pair_heads, keys, rows), BF),
        jax.ShapeDtypeStruct((pair, rows), BF),
        jax.ShapeDtypeStruct((pair, keys), BF),
        jax.ShapeDtypeStruct((pair, keys), BF),
        jax.ShapeDtypeStruct((pair, rows), BF),
        jax.ShapeDtypeStruct((pair_heads, rows), F32),
    )
    forward_specs = [ANY] + [VMEM] * 5
    forward_scratch = (
        pltpu.VMEM((2, keys, CHUNK), F32),
        pltpu.VMEM((2, keys, rows), BF),
        pltpu.SemaphoreType.DMA((2,)),
    )
    normed, *near = call(
        functools.partial(near_kernel, half),
        (jax.ShapeDtypeStruct((keys, D), BF),) + forward_outs,
        [SMEM] + [VMEM] * 6,
        [VMEM] + forward_specs,
        forward_scratch,
    )(meta, x, xs, row(first_gain), row(first_shift), pa0, pa1)
    far = call(
        functools.partial(far_kernel, half), forward_outs, [SMEM] + [VMEM] * 3, forward_specs, forward_scratch
    )(meta, normed, pa2, pa3)
    e0, q0, k0, v0, mixed0, inv0 = near
    e1, q1, k1, v1, mixed1, inv1 = far

    ff_scratch = (pltpu.VMEM((2, rows, width), BF), pltpu.VMEM((2, rows, width), BF))
    whole = jax.ShapeDtypeStruct((rows, D), F32)
    ff_grads = jax.ShapeDtypeStruct((2, 2 * D, width), BF)
    ff_bias = jax.ShapeDtypeStruct((2, width), F32)
    hidden, n2, branch, back, g_near, gb_near = call(
        functools.partial(mid_kernel, half),
        (whole, jax.ShapeDtypeStruct((rows, D), BF), whole, whole, ff_grads, ff_bias),
        [VMEM] * 17,
        [VMEM] * 6,
        ff_scratch,
    )(x, cot, mixed0, mixed1, pa0, pa1, pa2, pa3, row(out_bias), row(second_gain), row(second_shift), *ff_parts(pb0, pb1))
    output, grad_hidden, dT0, dT1, go, g_far, gb_far, small_two = call(
        functools.partial(turn_kernel, half),
        (
            jax.ShapeDtypeStruct((half, D), BF),
            whole,
            jax.ShapeDtypeStruct((pair, rows), BF),
            jax.ShapeDtypeStruct((pair, rows), BF),
            jax.ShapeDtypeStruct((TENSOR, local, D), BF),
            ff_grads,
            ff_bias,
            jax.ShapeDtypeStruct((4, D), F32),
        ),
        [VMEM] * 19,
        [VMEM] * 8,
        ff_scratch,
    )(hidden, n2, cot, branch, back, mixed0, mixed1, pa0, pa1, pa2, pa3, row(reduce_bias), row(second_gain), *ff_parts(pb2, pb3))

    def ff_slot(grads, index):
        return jnp.concatenate([grads[index % 2], go[index]], axis=0)

    def tensor_sum(slots):
        near_sum = slots[0].astype(F32) + across(slots[1], 1).astype(F32)
        far_sum = (slots[2].astype(F32) + across(slots[3], 1).astype(F32)).astype(BF)
        return (near_sum + across(far_sum, 2).astype(F32)).astype(BF)

    ff_total = dp_sum(tensor_sum([ff_slot(g_near, 0), ff_slot(g_near, 1), ff_slot(g_far, 2), ff_slot(g_far, 3)]), dp)

    backward_outs = (
        jax.ShapeDtypeStruct((pair, rows), BF),
        jax.ShapeDtypeStruct((pair, keys), BF),
        jax.ShapeDtypeStruct((pair, keys), BF),
        jax.ShapeDtypeStruct((2, D, 3 * local), BF),
        jax.ShapeDtypeStruct((3, pair), F32),
    )
    backward = call(
        attention_backward,
        backward_outs,
        [ANY] + [VMEM] * 7,
        [VMEM] * 5,
        (pltpu.VMEM((2, keys, rows), BF), pltpu.VMEM((2, keys, rows), BF), pltpu.SemaphoreType.DMA((2,))),
    )
    dq1, dk1, dv1, gq_far, qb_far = backward(e1, normed, q1, k1, v1, mixed1, dT1, inv1)
    dq0, dk0, dv0, gq_near, qb_near = backward(e0, normed, q0, k0, v0, mixed0, dT0, inv0)

    own, sib, small_one = call(
        functools.partial(first_kernel, half),
        (whole, jax.ShapeDtypeStruct((rows, D), BF), jax.ShapeDtypeStruct((2, D), F32)),
        [VMEM] * 12,
        [VMEM] * 3,
    )(x, xs, pa0, pa1, pa2, pa3, dq0, dk0, dv0, dq1, dk1, dv1)
    grad_frames = call(last_kernel, jax.ShapeDtypeStruct((half, D), F32), [VMEM] * 5, VMEM)(
        x, own, across(sib, 1), grad_hidden, row(first_gain)
    )

    small_all = jnp.concatenate([small_two, small_one], axis=0).reshape(-1)
    line = 3 * local
    count = 6 * D + width + pair
    lines = -(-count // line)
    room = 8 * EXTRA

    def small_rows(bias_ff, bias_qkv, index):
        part = slice((index % 2) * local, (index % 2 + 1) * local)
        v = jnp.concatenate([small_all, bias_ff[index % 2], bias_qkv[0, part], bias_qkv[2, part]])
        return jnp.pad(v, (0, lines * line - count)).reshape(lines, line)

    def split(v):
        high = v.astype(BF)
        low = (v - high.astype(F32)).astype(BF)
        return high, low

    def q_slot(grads, bias_ff, bias_qkv, index):
        high, low = split(small_rows(bias_ff, bias_qkv, index))
        return jnp.concatenate([grads[index % 2], jnp.pad(jnp.concatenate([high, low]), ((0, room - 2 * lines), (0, 0)))], axis=0)

    q_total = dp_sum(
        tensor_sum(
            [
                q_slot(gq_near, gb_near, qb_near, 0),
                q_slot(gq_near, gb_near, qb_near, 1),
                q_slot(gq_far, gb_far, qb_far, 2),
                q_slot(gq_far, gb_far, qb_far, 3),
            ]
        ),
        dp,
    ).astype(F32)
    ff_total = ff_total.astype(F32)
    sums = (q_total[D : D + lines] + q_total[D + lines : D + 2 * lines]).reshape(-1)
    globals_ = sums[: 6 * D].reshape(6, D)
    bias_ff = sums[6 * D : 6 * D + width]
    bias_q = sums[6 * D + width : 6 * D + width + local]
    bias_v = sums[6 * D + width + local : 6 * D + width + pair]
    return (
        output,
        grad_frames,
        q_total[:D, :local],
        bias_q,
        q_total[:D, local : 2 * local],
        q_total[:D, 2 * local :],
        bias_v,
        ff_total[2 * D :],
        globals_[0],
        globals_[4],
        globals_[5],
        ff_total[:D],
        bias_ff,
        ff_total[D : 2 * D],
        globals_[3],
        globals_[1],
        globals_[2],
    )


def solution(mesh):
    dp = mesh.shape["dp"]
    assert mesh.shape["tensor"] == TENSOR and dp & (dp - 1) == 0
    split = P(("dp", "tensor"), None)
    column = P(None, "tensor")
    return jax.shard_map(
        functools.partial(on_device, dp),
        mesh=mesh,
        in_specs=(
            split, column, P("tensor"), column, column, P("tensor"), P("tensor", None), P(), P(), P(),
            column, P("tensor"), P("tensor", None), P(), P(), P(), P("dp"), P("dp"), P("dp"), split,
        ),
        out_specs=(
            split, split, column, P("tensor"), column, column, P("tensor"), P("tensor", None), P(), P(), P(),
            column, P("tensor"), P("tensor", None), P(), P(), P(),
        ),
        check_vma=False,
    )
```

```python
import functools

import jax
import jax.numpy as jnp
from jax import lax
from jax.experimental import pallas as pl
from jax.experimental.pallas import tpu as pltpu
from jax.sharding import PartitionSpec as P

BF = jnp.bfloat16
F32 = jnp.float32
D = 512
HEADS = 8
HEAD = D // HEADS
EPS = 1e-05
TENSOR = 4
CHUNK = 256
EXTRA = 16
NN = (((1,), (0,)), ((), ()))
NT = (((1,), (1,)), ((), ()))
TN = (((0,), (0,)), ((), ()))
TT = (((0,), (1,)), ((), ()))
VMEM = pl.BlockSpec(memory_space=pltpu.VMEM)
SMEM = pl.BlockSpec(memory_space=pltpu.SMEM)
ANY = pl.BlockSpec(memory_space=pl.ANY)


def dot(left, right, dims):
    return lax.dot_general(left, right, dims, preferred_element_type=F32)


class Fetched:
    def __init__(self, source, buffer, sem):
        self.buffer, self.shape, self.waited = buffer, buffer.shape, False
        self.copy = pltpu.make_async_copy(source, buffer, sem)
        self.copy.start()

    def __getitem__(self, index):
        if not self.waited:
            self.copy.wait()
            self.waited = True
        return self.buffer[index]


class Stored:
    def __init__(self, target, buffer, sem):
        self.buffer, self.shape, self.dtype, self.sent = buffer, buffer.shape, buffer.dtype, False
        self.copy = pltpu.make_async_copy(buffer, target, sem)

    def __getitem__(self, index):
        return self.buffer[index]

    def __setitem__(self, index, value):
        self.buffer[index] = value

    def flush(self):
        if not self.sent:
            self.copy.start()
            self.sent = True


HBM = pl.BlockSpec(memory_space=pltpu.HBM)
SPEC = {"f": HBM, "h": HBM, "s": SMEM, "v": VMEM}


class Line:
    def __init__(self):
        self.waits = ()

    def run(self, kernel, outs, ins, args, scratch=(), us=8, vmem=20):
        waits = self.waits
        outs = [o if isinstance(o, tuple) else (o, "v") for o in outs]
        kinds = list(ins)
        skip, last = len(kinds), len(outs)
        moved = [i for i, k in enumerate(kinds) if k == "f"]
        built = [i for i, (_, k) in enumerate(outs) if k == "f"]
        buffers = [pltpu.VMEM(args[i].shape, args[i].dtype) for i in moved] + [pltpu.VMEM(outs[i][0].shape, outs[i][0].dtype) for i in built]

        def body(*refs):
            inputs = list(refs[:skip])
            rest = refs[skip + len(waits) :]
            results, zeros, rest = list(rest[:last]), rest[last], rest[last + 1 :]
            held, sems, rest = rest[: len(buffers)], rest[len(buffers)], rest[len(buffers) + 1 :]
            for n, i in enumerate(moved):
                inputs[i] = Fetched(inputs[i], held[n], sems.at[n])
            for n, i in enumerate(built, len(moved)):
                results[i] = Stored(results[i], held[n], sems.at[n])
            zeros[...] = jnp.zeros((8, 128), F32)
            kernel(*inputs, *results, *rest)
            for i in built:
                results[i].flush()
            for i in moved:
                if not inputs[i].waited:
                    inputs[i].copy.wait()
            for i in built:
                results[i].copy.wait()

        *got, zeros = pl.pallas_call(
            body,
            out_shape=tuple(pltpu.HBM(o.shape, o.dtype) if k in "fh" else o for o, k in outs) + (jax.ShapeDtypeStruct((8, 128), F32),),
            in_specs=[SPEC[k] for k in kinds] + [ANY] * len(waits),
            out_specs=[SPEC[k] for _, k in outs] + [VMEM],
            scratch_shapes=buffers + [pltpu.SemaphoreType.DMA((len(buffers) + 1,))] + list(scratch),
            compiler_params=pltpu.CompilerParams(vmem_limit_bytes=vmem * 2**20),
            cost_estimate=pl.CostEstimate(flops=int(us * 4.4e9), bytes_accessed=2**20, transcendentals=0),
        )(*(pltpu.with_memory_space_constraint(a, pltpu.HBM) if k in "fh" else a for a, k in zip(args, kinds)), *waits)
        self.waits = (zeros,)
        return got

    def touch(self, value):
        waits = self.waits
        got = (
            pl.pallas_call(
                lambda given, *rest: None,
                out_shape=jax.ShapeDtypeStruct(value.shape, value.dtype),
                in_specs=[ANY] * (1 + len(waits)),
                out_specs=ANY,
                input_output_aliases={0: 0},
                compiler_params=pltpu.CompilerParams(vmem_limit_bytes=2**20),
                cost_estimate=pl.CostEstimate(flops=10**6, bytes_accessed=1024, transcendentals=0),
            )(value, *waits)
        )
        self.waits = self.waits + (got,)
        return got

    def plus(self, left, right):
        def body(a, b, out):
            out[...] = (a[...].astype(F32) + b[...].astype(F32)).astype(out.dtype)

        return self.run(body, [jax.ShapeDtypeStruct(left.shape, left.dtype)], "vv", (left, right), us=1, vmem=6)[0]


def shaped(*shape, dtype=BF):
    return jax.ShapeDtypeStruct(shape, dtype)


def norm_terms(rows_in):
    center = jnp.mean(rows_in, axis=-1, keepdims=True)
    centered = rows_in - center
    spread = jnp.mean(centered * centered, axis=-1, keepdims=True)
    scale = lax.rsqrt(spread + EPS)
    return centered * scale, scale


def norm_back(grad, gain, xhat, scale):
    e = grad * gain
    mean_e = jnp.mean(e, axis=-1, keepdims=True)
    mean_ex = jnp.mean(e * xhat, axis=-1, keepdims=True)
    return scale * (e - mean_e - xhat * mean_ex)


def valid_row(start_ref, end_ref, empty_ref, rows, half):
    lane = lax.broadcasted_iota(jnp.int32, (1, 2 * rows), 1)
    second = lane >= rows
    local = jnp.where(second, lane - rows, lane)
    device = lax.axis_index("tensor")
    clip = device // 2
    core = device % 2
    position = local + half * jnp.where(second, 1 - core, core)
    inside = (position >= start_ref[clip]) & (position < end_ref[clip])
    return (local < half) & jnp.logical_not(inside) & (empty_ref[clip] == 0)


def attention_forward(half, start_ref, end_ref, empty_ref, n_ref, pack, e_hbm, qT_ref, kT_ref, vT_ref, mixed_ref, inv_ref, s_buf, e_buf, sem):
    rows = qT_ref.shape[1]
    keys = kT_ref.shape[1]
    local = qT_ref.shape[0]
    heads = local // HEAD
    first_row = lax.broadcasted_iota(jnp.int32, (EXTRA, keys), 0) == 0
    ones16 = first_row.astype(F32).astype(BF)

    def project(first, last, count):
        product = dot(pack[:D, first * local : last * local], n_ref[:count, :], TT)
        return product + dot(pack[D:, first * local : last * local], ones16[:, :count], TN)

    qT_ref[...] = (project(0, 1, rows).astype(BF).astype(F32) * HEAD**-0.5).astype(BF)
    both = project(1, 3, keys).astype(BF)
    kT_ref[...] = both[:local]
    vT_ref[...] = both[local:]

    valid = valid_row(start_ref, end_ref, empty_ref, rows, half)
    some = jnp.max(valid.astype(F32), axis=1, keepdims=True)
    mask = jnp.where(first_row, jnp.where(valid, 0.0, -1e30), 0.0).astype(BF)

    blocks = [(h, c) for h in range(heads) for c in range(rows // CHUNK)]
    tops = {}

    def score(i):
        h, c = blocks[i]
        q = jnp.concatenate([qT_ref[h * HEAD : (h + 1) * HEAD, c * CHUNK : (c + 1) * CHUNK], ones16[:, :CHUNK]], axis=0)
        top = None
        for k in range(keys // CHUNK):
            span = slice(k * CHUNK, (k + 1) * CHUNK)
            s = dot(jnp.concatenate([kT_ref[h * HEAD : (h + 1) * HEAD, span], mask[:, span]], axis=0), q, TN)
            s_buf[i % 2, span, :] = s
            part = jnp.max(s.reshape(CHUNK // 8, 8, CHUNK), axis=0)
            top = part if top is None else jnp.maximum(top, part)
        tops[i] = jnp.max(top, axis=0, keepdims=True)

    copies = []
    score(0)
    for i, (h, c) in enumerate(blocks):
        if i + 1 < len(blocks):
            score(i + 1)
        columns = slice(c * CHUNK, (c + 1) * CHUNK)
        for k in range(keys // CHUNK):
            span = slice(k * CHUNK, (k + 1) * CHUNK)
            e_buf[h, c, span, :] = jnp.exp(s_buf[i % 2, span, :] - tops[i]).astype(BF)
        value = jnp.concatenate([vT_ref[h * HEAD : (h + 1) * HEAD, :], jnp.ones((EXTRA, keys), BF)], axis=0)
        o = dot(value, e_buf[h, c], NN)
        inv = some / o[HEAD : HEAD + 1, :]
        mixed_ref[h * HEAD : (h + 1) * HEAD, columns] = o[:HEAD] * inv
        inv_ref[h : h + 1, columns] = inv
        copy = pltpu.make_async_copy(e_buf.at[h, c], e_hbm.at[h, c], sem.at[i])
        copy.start()
        copies.append(copy)
    for copy in copies:
        copy.wait()


def ff_pack(first, w1_ref, w2_ref, b1_ref, out_ref):
    out_ref[:D, :] = w1_ref[:, first : first + CHUNK]
    for part in range(2):
        out_ref[D + part * CHUNK : D + (part + 1) * CHUNK, :] = w2_ref[first : first + CHUNK, part * CHUNK : (part + 1) * CHUNK]
    out_ref[2 * D :, :] = jnp.broadcast_to(b1_ref[...].reshape(1, -1)[:, first : first + CHUNK], (EXTRA, CHUNK))


def pack_kernel(wq, wk, wv, wo, bq, bv, g1, s1, ob, g2, s2, rb, pack_ref, small_ref):
    local = wq.shape[1]
    for index, ref in enumerate((wq, wk, wv)):
        pack_ref[:D, index * local : (index + 1) * local] = ref[...]
    pack_ref[:D, 3 * local :] = wo[...].T
    pack_ref[D:, :] = jnp.zeros((EXTRA, 4 * local), BF)
    pack_ref[D : D + 1, :local] = bq[...].reshape(1, local)
    pack_ref[D : D + 1, 2 * local : 3 * local] = bv[...].reshape(1, local)
    for index, ref in enumerate((g1, s1, ob, g2, s2, rb)):
        small_ref[index : index + 1, :] = ref[...].astype(F32).reshape(1, D)


def start_kernel(half, start_ref, end_ref, empty_ref, x_ref, xs_ref, small_ref, pack, w1_ref, w2_ref, b1_ref, n_ref, ff_ref, *rest):
    rows = n_ref.shape[0] // 2
    gain = small_ref[0:1, :]
    shift = small_ref[1:2, :]
    for part, ref in enumerate((x_ref, xs_ref)):
        xhat, _ = norm_terms(ref[...].astype(F32))
        n_ref[part * rows : part * rows + half, :] = (xhat * gain + shift).astype(BF)
        n_ref[part * rows + half : (part + 1) * rows, :] = jnp.zeros((rows - half, D), BF)
    ff_pack(0, w1_ref, w2_ref, b1_ref, ff_ref)
    attention_forward(half, start_ref, end_ref, empty_ref, n_ref, pack, *rest)


def far_kernel(half, start_ref, end_ref, empty_ref, n_ref, pack, w1_ref, w2_ref, b1_ref, ff_ref, *rest):
    ff_pack(CHUNK, w1_ref, w2_ref, b1_ref, ff_ref)
    attention_forward(half, start_ref, end_ref, empty_ref, n_ref, pack, *rest)


def out_kernel(half, x_ref, m0, m1, m2, m3, pa0, pa1, pa2, pa3, small_ref, hidden_ref, n2_ref):
    local = m0.shape[0]
    mixed = jnp.concatenate([m[...].astype(BF) for m in (m0, m1, m2, m3)], axis=0)
    weight = jnp.concatenate([p[:D, 3 * local :] for p in (pa0, pa1, pa2, pa3)], axis=1)
    hidden_ref[...] = dot(mixed, weight, TT) + small_ref[2:3, :]
    hidden_ref[:half, :] += x_ref[...].astype(F32)
    xhat, _ = norm_terms(hidden_ref[...])
    n2_ref[...] = (xhat * small_ref[3:4, :] + small_ref[4:5, :]).astype(BF)


def phi_terms(inner):
    bell = jnp.exp(inner * inner * -0.5)
    x = jnp.abs(inner) * 0.7071067811865476
    t = 1.0 / (1.0 + 0.3275911 * x)
    poly = t * (0.254829592 + t * (-0.284496736 + t * (1.421413741 + t * (-1.453152027 + t * 1.061405429))))
    tail = 0.5 * poly * bell
    return jnp.where(inner >= 0, 1.0 - tail, tail), bell * 0.3989422804014327


def padded(cot_ref, rows):
    half = cot_ref.shape[0]
    return jnp.concatenate([cot_ref[...].astype(F32), jnp.zeros((rows - half, D), F32)], axis=0)


def ff_slots(n2, cot, packs, branch_ref, back_ref, keep_ref, send_ref, bias_ref, act_buf, gi_buf):
    n2T = n2.T
    ones = jnp.ones((EXTRA, n2.shape[0]), BF)

    def weights(s):
        p = packs[s]
        return p[:D, :], jnp.concatenate([p[D : D + CHUNK, :], p[D + CHUNK : 2 * D, :]], axis=1)

    def enter(s):
        w1, w2 = weights(s)
        return dot(n2, w1, NN) + packs[s][2 * D : 2 * D + 1, :].astype(F32), dot(cot, w2, NT)

    ahead = enter(0)
    for s in range(TENSOR):
        inner, grad = ahead
        if s + 1 < TENSOR:
            ahead = enter(s + 1)
        cdf, density = phi_terms(inner)
        act_buf[s] = (inner * cdf).astype(BF)
        gi_buf[s] = (grad * (cdf + inner * density)).astype(BF)
        w1, w2 = weights(s)
        branch_ref[...] += dot(act_buf[s], w2, NN)
        back_ref[...] += dot(gi_buf[s], w1, NT)
        grads = send_ref if s % 2 else keep_ref
        grads[s // 2, :D, :] = dot(n2T, gi_buf[s], NN).astype(BF)
        second = dot(act_buf[s], cot, TN).astype(BF)
        grads[s // 2, D : D + CHUNK, :] = second[:, :CHUNK]
        grads[s // 2, D + CHUNK : 2 * D, :] = second[:, CHUNK:]
        bias_ref[s : s + 1, :] = dot(ones, gi_buf[s], NN)[:1]


def ff_kernel(n2_ref, cot_ref, p0, p1, p2, p3, branch_ref, back_ref, keep_ref, send_ref, bias_ref, act_buf, gi_buf):
    branch_ref[...] = jnp.zeros(branch_ref.shape, F32)
    back_ref[...] = jnp.zeros(back_ref.shape, F32)
    cot = padded(cot_ref, n2_ref.shape[0]).astype(BF)
    ff_slots(n2_ref[...], cot, (p0, p1, p2, p3), branch_ref, back_ref, keep_ref, send_ref, bias_ref, act_buf, gi_buf)


def turn_kernel(n2_ref, cot_ref, p0, p1, p2, p3, branch_in, back_in, hidden_ref, m0, m1, m2, m3, pa0, pa1, pa2, pa3, small_in,
                out_ref, gh_ref, dT0, dT1, dT2, dT3, keep_ref, send_ref, bias_ref, small_ref, act_buf, gi_buf, branch_buf, back_buf):
    local = m0.shape[0]
    cot_f = padded(cot_ref, n2_ref.shape[0])
    branch_buf[...] = branch_in[...]
    back_buf[...] = back_in[...]
    ff_slots(n2_ref[...], cot_f.astype(BF), (p0, p1, p2, p3), branch_buf, back_buf, keep_ref, send_ref, bias_ref, act_buf, gi_buf)
    hidden = hidden_ref[...]
    back = back_buf[...]
    xhat, scale = norm_terms(hidden)
    grad_hidden = cot_f + norm_back(back, small_in[3:4, :], xhat, scale)
    gh_ref[...] = grad_hidden
    small_ref[0:1, :] = jnp.sum(grad_hidden, axis=0, keepdims=True)
    small_ref[1:2, :] = jnp.sum(back * xhat, axis=0, keepdims=True)
    small_ref[2:3, :] = jnp.sum(back, axis=0, keepdims=True)
    small_ref[3:4, :] = jnp.sum(cot_f, axis=0, keepdims=True)
    out_ref[...] = (hidden + branch_buf[...] + small_in[5:6, :])[: out_ref.shape[0]].astype(BF)
    low = grad_hidden.astype(BF)
    weight = jnp.concatenate([p[:D, 3 * local :] for p in (pa0, pa1, pa2, pa3)], axis=1)
    grads_T = dot(weight, low, TT).astype(BF)
    for s, ref in enumerate((dT0, dT1, dT2, dT3)):
        ref[...] = grads_T[s * local : (s + 1) * local]
    mixed = jnp.concatenate([m[...].astype(BF) for m in (m0, m1, m2, m3)], axis=0)
    grad = dot(mixed, low, NN).astype(BF)
    for s in range(TENSOR):
        grads = send_ref if s % 2 else keep_ref
        for part in range(2):
            first = 2 * D + part * local
            grads[s // 2, first : first + local, :] = grad[s * local : (s + 1) * local, part * CHUNK : (part + 1) * CHUNK]


def attention_backward(e_hbm, dT_ref, inv_ref, mixed_ref, vT_ref, qT_ref, kT_ref, n_ref, dq_ref, dk_ref, dv_ref, grad_ref, bias_ref,
                       e_buf, ds_buf, sem):
    rows = qT_ref.shape[1]
    keys = kT_ref.shape[1]
    local = qT_ref.shape[0]
    heads = local // HEAD
    blocks = [(h, c) for h in range(heads) for c in range(rows // CHUNK)]
    copies = [pltpu.make_async_copy(e_hbm.at[h, c], e_buf.at[h, c], sem.at[i]) for i, (h, c) in enumerate(blocks)]
    for copy in copies:
        copy.start()
    which = lax.broadcasted_iota(jnp.int32, (EXTRA, CHUNK), 0)
    ones2 = (lax.broadcasted_iota(jnp.int32, (EXTRA, CHUNK), 0) < 2).astype(F32).astype(BF)
    lows = {}

    def enter(i):
        h, c = blocks[i]
        here = slice(h * HEAD, (h + 1) * HEAD)
        columns = slice(c * CHUNK, (c + 1) * CHUNK)
        low = (dT_ref[here, columns].astype(F32) * inv_ref[h : h + 1, columns]).astype(BF)
        delta = jnp.sum(low.astype(F32) * mixed_ref[here, columns], axis=0, keepdims=True)
        high = (-delta).astype(BF).astype(F32)
        extra = jnp.where(which == 0, high, jnp.where(which == 1, -delta - high, 0.0)).astype(BF)
        more = jnp.concatenate([low, extra], axis=0)
        lows[i] = low
        copies[i].wait()
        for k in range(keys // CHUNK):
            span = slice(k * CHUNK, (k + 1) * CHUNK)
            v = jnp.concatenate([vT_ref[here, span], ones2], axis=0)
            ds_buf[i % 2, span, :] = (e_buf[h, c, span, :].astype(F32) * dot(v, more, TN)).astype(BF)

    dv = None
    dk = None
    enter(0)
    for i, (h, c) in enumerate(blocks):
        if i + 1 < len(blocks):
            enter(i + 1)
        here = slice(h * HEAD, (h + 1) * HEAD)
        columns = slice(c * CHUNK, (c + 1) * CHUNK)
        part = dot(lows[i], e_buf[h, c], NT)
        dv = part if c == 0 else dv + part
        dq_ref[here, columns] = (dot(kT_ref[here, :], ds_buf[i % 2], NN) * HEAD**-0.5).astype(BF)
        part = dot(qT_ref[here, columns], ds_buf[i % 2], NT)
        dk = part if c == 0 else dk + part
        if c == rows // CHUNK - 1:
            dv_ref[here, :] = dv.astype(BF)
            dk_ref[here, :] = dk.astype(BF)
    nT = n_ref[...].T
    ones = jnp.ones((EXTRA, rows), BF)
    for index, (ref, count) in enumerate(((dq_ref, rows), (dk_ref, keys), (dv_ref, keys))):
        columns = slice(index * local, (index + 1) * local)
        grad_ref[:, columns] = dot(nT[:, :count], ref[...], NT).astype(BF)
        sums = sum(dot(ones, ref[:, i * rows : (i + 1) * rows], NT) for i in range(count // rows))
        bias_ref[0:1, columns] = sums[:1]


def first_kernel(half, x_ref, xs_ref, pa0, pa1, pa2, pa3, *rest):
    sources = rest[:12]
    small_two, b0, b1, b2, b3, f0, f1, own_ref, sib_ref, small_ref = rest[12:]
    local = pa0.shape[1] // TENSOR
    rows = own_ref.shape[0]
    device = lax.axis_index("tensor")
    small_ref[...] = jnp.zeros(small_ref.shape, F32)
    gain_sum = 0.0
    shift_sum = 0.0
    for part, ref in enumerate((x_ref, xs_ref)):
        columns = slice(part * rows, (part + 1) * rows)
        total = None
        for slot, p in enumerate((pa0, pa1, pa2, pa3)):
            for index in range(part, 3):
                term = dot(sources[slot * 3 + index][:, columns], p[:D, index * local : (index + 1) * local], TT)
                total = term if total is None else total + term
        if part == 0:
            own_ref[...] = total
        else:
            sib_ref[...] = total.astype(BF)
        xhat, _ = norm_terms(ref[...].astype(F32))
        gain_sum = gain_sum + jnp.sum(total[:half] * xhat, axis=0, keepdims=True)
        shift_sum = shift_sum + jnp.sum(total, axis=0, keepdims=True)
    small_ref[0:4, :] = small_two[...]
    small_ref[4:5, :] = gain_sum
    small_ref[5:6, :] = shift_sum
    for slot, b in enumerate((b0, b1, b2, b3)):
        owner = jnp.bitwise_xor(device, slot)
        small_ref[pl.ds(8 + owner, 1), :] = jnp.concatenate([f[slot : slot + 1, :] for f in (f0, f1)], axis=1)
        small_ref[pl.ds(12 + owner, 1), : 3 * local] = b[...]


def last_kernel(x_ref, own_ref, got_ref, gh_ref, small_ref, out_ref):
    half = out_ref.shape[0]
    grad = own_ref[:half, :] + got_ref[:half, :].astype(F32)
    xhat, scale = norm_terms(x_ref[...].astype(F32))
    out_ref[...] = gh_ref[:half, :] + norm_back(grad, small_ref[0:1, :], xhat, scale)


def upper_half():
    return lax.rem(lax.axis_index("dp"), 2)


def total_kernel(parts, send_ref, keep_ref, sum_buf):
    sum_buf[...] = sum(ref[...].astype(F32) for ref in parts)
    rows = keep_ref.shape[0]
    upper = upper_half()
    keep_ref[...] = sum_buf[pl.ds(pl.multiple_of(upper * rows, rows), rows), :].astype(BF)
    send_ref[...] = sum_buf[pl.ds(pl.multiple_of((1 - upper) * rows, rows), rows), :].astype(BF)


def merge(kept, got, buf):
    rows = kept.shape[0]
    upper = upper_half()
    buf[pl.ds(pl.multiple_of(upper * rows, rows), rows), :] = kept[...].astype(F32)
    buf[pl.ds(pl.multiple_of((1 - upper) * rows, rows), rows), :] = got[...].astype(F32)


def finish_ff_kernel(kept0, got0, kept1, got1, expand_ref, reduce_ref, out_ref, buf0, buf1):
    local = out_ref.shape[0]
    for index, (kept, got, buf) in enumerate(((kept0, got0, buf0), (kept1, got1, buf1))):
        merge(kept, got, buf)
        lanes = slice(index * CHUNK, (index + 1) * CHUNK)
        expand_ref[:, lanes] = buf[:D, :]
        for part in range(2):
            reduce_ref[lanes, part * CHUNK : (part + 1) * CHUNK] = buf[D + part * CHUNK : D + (part + 1) * CHUNK, :]
    for part in range(2):
        first = 2 * D + part * local
        out_ref[:, part * CHUNK : (part + 1) * CHUNK] = buf1[first : first + local, :]


def finish_qkv_kernel(kept, got, q_ref, k_ref, v_ref, buf):
    merge(kept, got, buf)
    local = q_ref.shape[1]
    for index, ref in enumerate((q_ref, k_ref, v_ref)):
        ref[...] = buf[:, index * local : (index + 1) * local]


class Doubling:
    def __init__(self, line, along, size, send, keep):
        self.line, self.along, self.size, self.part, self.bit = line, along, size, keep, 1
        self.pending = along(send, 1)

    def step(self):
        self.part = self.line.plus(self.part, self.pending)
        self.bit *= 2
        self.pending = self.along(self.part, self.bit if self.bit < self.size else 1)

    def finish(self):
        while self.bit < self.size:
            self.step()
        return self.part, self.pending


def swap(value, axis, size, bit):
    return lax.ppermute(value, axis, [(i, i ^ bit) for i in range(size)])


def on_device(dp, frames, query_weight, query_bias, key_weight, value_weight, value_bias, out_weight, out_bias, first_gain, first_shift,
              expand_weight, expand_bias, reduce_weight, reduce_bias, second_gain, second_shift, span_start, span_end, empty_flag, cotangent):
    half = frames.shape[0]
    rows = -(-half // CHUNK) * CHUNK
    keys = 2 * rows
    local = query_weight.shape[1]
    heads = local // HEAD
    blocks = rows // CHUNK
    line = Line()

    def across(v, bit):
        return swap(v, "tensor", TENSOR, bit)

    def along(v, bit):
        return swap(v, "dp", dp, bit)

    xs = across(frames, 1)
    pa0, small = line.run(
        pack_kernel, (shaped(D + EXTRA, 4 * local), shaped(8, D, dtype=F32)), "f" * 12,
        (query_weight, key_weight, value_weight, out_weight, query_bias, value_bias,
         first_gain, first_shift, out_bias, second_gain, second_shift, reduce_bias), us=2,
    )
    pa2 = across(pa0, 2)
    pa1 = across(pa0, 1)

    forward_outs = (
        (shaped(heads, blocks, keys, CHUNK), "h"), shaped(local, rows), shaped(local, keys), shaped(local, keys),
        shaped(local, rows, dtype=F32), shaped(heads, rows, dtype=F32),
    )
    forward_scratch = (
        pltpu.VMEM((2, keys, CHUNK), F32),
        pltpu.VMEM((heads, blocks, keys, CHUNK), BF),
        pltpu.SemaphoreType.DMA((heads * blocks,)),
    )
    spans = (span_start, span_end, empty_flag)
    ff_weights = (expand_weight, reduce_weight, expand_bias)
    ff_shape = shaped(2 * D + EXTRA, CHUNK)
    normed, ff0, *s0 = line.run(
        functools.partial(start_kernel, half), (shaped(keys, D), ff_shape) + forward_outs, "sssfvvvfff",
        spans + (frames, xs, small, pa0) + ff_weights, forward_scratch, us=8,
    )
    ff0_far = across(ff0, 2)
    ff0_near = across(ff0, 1)
    s1 = line.run(
        functools.partial(attention_forward, half), forward_outs, "sssvv",
        spans + (normed, pa1), forward_scratch, us=7,
    )
    pa2 = line.touch(pa2)
    pa3 = across(pa2, 1)
    ff1, *s2 = line.run(
        functools.partial(far_kernel, half), (ff_shape,) + forward_outs, "sssvvfff",
        spans + (normed, pa2) + ff_weights, forward_scratch, us=7,
    )
    ff1_far = across(ff1, 2)
    s3 = line.run(
        functools.partial(attention_forward, half), forward_outs, "sssvv",
        spans + (normed, pa3), forward_scratch, us=7,
    )
    slots = (s0, s1, s2, s3)
    mixed = tuple(s[4] for s in slots)
    packs = (pa0, pa1, pa2, pa3)
    ff0_far = line.touch(ff0_far)
    ff0_cross = across(ff0_far, 1)
    whole = shaped(rows, D, dtype=F32)
    hidden, n2 = line.run(
        functools.partial(out_kernel, half), (whole, shaped(rows, D)), "f" + "v" * 9,
        (frames,) + mixed + packs + (small,), us=8,
    )
    ff1_near = across(ff1, 1)
    ff_scratch = (pltpu.VMEM((TENSOR, rows, CHUNK), BF), pltpu.VMEM((TENSOR, rows, CHUNK), BF))
    bias_shape = shaped(TENSOR, CHUNK, dtype=F32)
    branch, back, keep_a, send_a, bias_a = line.run(
        ff_kernel, (whole, whole, shaped(2, 2 * D, CHUNK), shaped(2, 2 * D, CHUNK), bias_shape), "vfvvvv",
        (n2, cotangent, ff0, ff0_near, ff0_far, ff0_cross), ff_scratch, us=8,
    )
    got_a = across(send_a, 1)
    ff1_far = line.touch(ff1_far)
    ff1_cross = across(ff1_far, 1)
    sum_a = line.plus(keep_a, got_a)
    y_a = across(sum_a[1], 2)
    size_b = 2 * D + 2 * local
    output, grad_hidden, *dT, keep_b, send_b, bias_b, small_two = line.run(
        turn_kernel,
        ((shaped(half, D), "f"), (whole, "f")) + (shaped(local, rows),) * TENSOR + (shaped(2, size_b, CHUNK), shaped(2, size_b, CHUNK), bias_shape, shaped(4, D, dtype=F32)),
        "vf" + "v" * 16,
        (n2, cotangent, ff1, ff1_near, ff1_far, ff1_cross, branch, back, hidden) + mixed + packs + (small,),
        ff_scratch + (pltpu.VMEM((rows, D), F32), pltpu.VMEM((rows, D), F32)), us=12, vmem=30,
    )
    got_b = across(send_b, 1)

    backward_outs = (
        shaped(local, rows), shaped(local, keys), shaped(local, keys), shaped(D, 3 * local), shaped(1, 3 * local, dtype=F32),
    )

    def backward(slot):
        e, q, k, v, m, inv = slots[slot]
        return line.run(
            attention_backward, backward_outs, "h" + "v" * 7,
            (e, dT[slot], inv, m, v, q, k, normed),
            (
                pltpu.VMEM((heads, blocks, keys, CHUNK), BF), pltpu.VMEM((2, keys, CHUNK), BF),
                pltpu.SemaphoreType.DMA((heads * blocks,)),
            ),
            us=8,
        )

    def total(*parts):
        def body(*refs):
            total_kernel(refs[: len(parts)], *refs[len(parts) :])

        size, columns = parts[0].shape
        piece = shaped(size // 2, columns)
        return line.run(
            body, (piece, piece), "v" * len(parts), parts, (pltpu.VMEM((size, columns), F32),), us=1
        )

    *d3, g3, b3 = backward(3)
    got_3 = across(g3, 1)
    sum_b = line.plus(keep_b, got_b)
    y_b = across(sum_b[1], 2)
    chain_a = Doubling(line, along, dp, *total(sum_a[0], y_a))
    *d2, g2, b2 = backward(2)
    sum_q = line.plus(g2, got_3)
    y_q = across(sum_q, 2)
    chain_a.step()
    *d1, g1, b1 = backward(1)
    got_1 = across(g1, 1)
    chain_b = Doubling(line, along, dp, *total(sum_b[0], y_b))
    chain_a.step()
    *d0, g0, b0 = backward(0)
    chain_q = Doubling(line, along, dp, *total(g0, got_1, y_q))
    chain_b.step()
    chain_a.finish()
    own, sib, sums = line.run(
        functools.partial(first_kernel, half), (whole, shaped(rows, D), shaped(16, D, dtype=F32)), "f" + "v" * 24,
        (frames, xs) + packs + (*d0, *d1, *d2, *d3, small_two, b0, b1, b2, b3, bias_a, bias_b), us=6,
    )
    got = across(sib, 1)
    pending = across(sums, 1)
    chain_q.step()
    chain_b.step()
    sums = line.plus(sums, pending)
    pending = across(sums, 2)
    (grad_frames,) = line.run(
        last_kernel, ((shaped(half, D, dtype=F32), "f"),), "fvvfv", (frames, own, got, grad_hidden, small), us=4
    )
    sums = line.plus(sums, pending)
    pending = along(sums, 1)
    chain_q.step()
    chain_b.finish()
    bit = 2
    while bit < dp:
        sums = line.plus(sums, pending)
        pending = along(sums, bit)
        bit *= 2
        chain_q.step() if chain_q.bit < dp else None
    chain_q.finish()
    grad_expand, grad_reduce, grad_out = line.run(
        finish_ff_kernel, tuple((shaped(*o, dtype=F32), "f") for o in ((D, 2 * CHUNK), (2 * CHUNK, D), (local, D))),
        "vvvv", chain_a.finish() + chain_b.finish(),
        (pltpu.VMEM((2 * D, CHUNK), F32), pltpu.VMEM((size_b, CHUNK), F32)), us=2,
    )
    sums = line.plus(sums, pending)
    grad_q, grad_k, grad_v = line.run(
        finish_qkv_kernel, ((shaped(D, local, dtype=F32), "f"),) * 3, "vv", chain_q.finish(),
        (pltpu.VMEM((D, 3 * local), F32),), us=1,
    )
    device = lax.axis_index("tensor")
    bias_ff = lax.dynamic_slice_in_dim(sums, 8 + device, 1, 0).reshape(-1)
    bias_qkv = lax.dynamic_slice_in_dim(sums, 12 + device, 1, 0).reshape(-1)
    return (
        output,
        grad_frames,
        grad_q,
        bias_qkv[:local],
        grad_k,
        grad_v,
        bias_qkv[2 * local : 3 * local],
        grad_out,
        sums[0],
        sums[4],
        sums[5],
        grad_expand,
        bias_ff,
        grad_reduce,
        sums[3],
        sums[1],
        sums[2],
    )


def solution(mesh):
    dp = mesh.shape["dp"]
    assert mesh.shape["tensor"] == TENSOR and dp & (dp - 1) == 0
    split = P(("dp", "tensor"), None)
    column = P(None, "tensor")
    return jax.shard_map(
        functools.partial(on_device, dp),
        mesh=mesh,
        in_specs=(
            split, column, P("tensor"), column, column, P("tensor"), P("tensor", None), P(), P(), P(),
            column, P("tensor"), P("tensor", None), P(), P(), P(), P("dp"), P("dp"), P("dp"), split,
        ),
        out_specs=(
            split, split, column, P("tensor"), column, column, P("tensor"), P("tensor", None), P(), P(), P(),
            column, P("tensor"), P("tensor", None), P(), P(), P(),
        ),
        check_vma=False,
    )
```

```python
import functools

import jax
import jax.numpy as jnp
from jax import lax
from jax.experimental import pallas as pl
from jax.experimental.pallas import tpu as pltpu
from jax.sharding import PartitionSpec as P

BF = jnp.bfloat16
F32 = jnp.float32
D = 512
HEADS = 8
HEAD = D // HEADS
EPS = 1e-05
TENSOR = 4
CHUNK = 256
EXTRA = 16
NN = (((1,), (0,)), ((), ()))
NT = (((1,), (1,)), ((), ()))
TN = (((0,), (0,)), ((), ()))
TT = (((0,), (1,)), ((), ()))
VMEM = pl.BlockSpec(memory_space=pltpu.VMEM)
SMEM = pl.BlockSpec(memory_space=pltpu.SMEM)
ANY = pl.BlockSpec(memory_space=pl.ANY)


def dot(left, right, dims):
    return lax.dot_general(left, right, dims, preferred_element_type=F32)


class Fetched:
    def __init__(self, source, buffer, sem):
        self.buffer, self.shape, self.waited = buffer, buffer.shape, False
        self.copy = pltpu.make_async_copy(source, buffer, sem)
        self.copy.start()

    def __getitem__(self, index):
        if not self.waited:
            self.copy.wait()
            self.waited = True
        return self.buffer[index]


class Stored:
    def __init__(self, target, buffer, sem):
        self.buffer, self.shape, self.dtype, self.sent = buffer, buffer.shape, buffer.dtype, False
        self.copy = pltpu.make_async_copy(buffer, target, sem)

    def __getitem__(self, index):
        return self.buffer[index]

    def __setitem__(self, index, value):
        self.buffer[index] = value

    def flush(self):
        if not self.sent:
            self.copy.start()
            self.sent = True


HBM = pl.BlockSpec(memory_space=pltpu.HBM)
SPEC = {"f": HBM, "h": HBM, "s": HBM, "v": VMEM}


class Line:
    def __init__(self):
        self.waits = ()

    def run(self, kernel, outs, ins, args, scratch=(), us=8, vmem=20):
        waits = self.waits
        outs = [o if isinstance(o, tuple) else (o, "v") for o in outs]
        kinds = list(ins)
        skip, last = len(kinds), len(outs)
        moved = [i for i, k in enumerate(kinds) if k in "fs"]
        built = [i for i, (_, k) in enumerate(outs) if k == "f"]
        space = {"f": pltpu.VMEM, "s": pltpu.SMEM}
        buffers = [space[kinds[i]](args[i].shape, args[i].dtype) for i in moved] + [pltpu.VMEM(outs[i][0].shape, outs[i][0].dtype) for i in built]

        def body(*refs):
            inputs = list(refs[:skip])
            rest = refs[skip + len(waits) :]
            results, zeros, rest = list(rest[:last]), rest[last], rest[last + 1 :]
            held, sems, rest = rest[: len(buffers)], rest[len(buffers)], rest[len(buffers) + 1 :]
            for n, i in enumerate(moved):
                inputs[i] = Fetched(inputs[i], held[n], sems.at[n])
            for n, i in enumerate(built, len(moved)):
                results[i] = Stored(results[i], held[n], sems.at[n])
            zeros[...] = jnp.zeros((8, 128), F32)
            kernel(*inputs, *results, *rest)
            for i in built:
                results[i].flush()
            for i in moved:
                if not inputs[i].waited:
                    inputs[i].copy.wait()
            for i in built:
                results[i].copy.wait()

        *got, zeros = pl.pallas_call(
            body,
            out_shape=tuple(pltpu.HBM(o.shape, o.dtype) if k in "fh" else o for o, k in outs) + (jax.ShapeDtypeStruct((8, 128), F32),),
            in_specs=[SPEC[k] for k in kinds] + [ANY] * len(waits),
            out_specs=[SPEC[k] for _, k in outs] + [VMEM],
            scratch_shapes=buffers + [pltpu.SemaphoreType.DMA((len(buffers) + 1,))] + list(scratch),
            compiler_params=pltpu.CompilerParams(vmem_limit_bytes=vmem * 2**20),
            cost_estimate=pl.CostEstimate(flops=10**6, bytes_accessed=2**10, transcendentals=0),
        )(*(pltpu.with_memory_space_constraint(a, pltpu.HBM) if k in "fhs" else a for a, k in zip(args, kinds)), *waits)
        self.waits = (zeros,)
        return got

    def touch(self, value):
        waits = self.waits
        got = (
            pl.pallas_call(
                lambda given, *rest: None,
                out_shape=jax.ShapeDtypeStruct(value.shape, value.dtype),
                in_specs=[ANY] * (1 + len(waits)),
                out_specs=ANY,
                input_output_aliases={0: 0},
                compiler_params=pltpu.CompilerParams(vmem_limit_bytes=2**20),
                cost_estimate=pl.CostEstimate(flops=10**6, bytes_accessed=1024, transcendentals=0),
            )(value, *waits)
        )
        self.waits = self.waits + (got,)
        return got

    def tick(self, *jobs):
        args, outs, scratch, plans = [], [], [], []

        def place(part):
            array, first, rows = part if isinstance(part, tuple) else (part, 0, part.shape[0])
            args.append(array)
            return len(args) - 1, first, rows

        for kind, *rest in jobs:
            pieces = [[place(part) for part in piece] for piece in ([[p] for p in rest[:2]] if kind == "merge" else rest[0])]
            rows = sum(piece[0][2] for piece in pieces)
            like = args[pieces[0][0][0]]
            columns = like.shape[1:]
            plans.append((kind, pieces, len(outs), len(scratch), rest[-1]))
            if kind == "halves":
                outs += [shaped(rows // 2, *columns)] * 2
            else:
                outs.append(jax.ShapeDtypeStruct((rows, *columns), like.dtype))
            if kind != "sum":
                scratch.append(pltpu.VMEM((rows, *columns), F32))

        def body(*refs):
            ins, results, buffers = refs[: len(args)], refs[len(args) : len(args) + len(outs)], refs[len(args) + len(outs) :]
            for kind, pieces, out, held, bit in plans:
                if kind == "merge":
                    kept, got = (ins[piece[0][0]] for piece in pieces)
                    merge(kept, got, buffers[held], bit)
                    results[out][...] = buffers[held][...].astype(results[out].dtype)
                    continue
                target = buffers[held] if kind == "halves" else results[out]
                at = 0
                for piece in pieces:
                    count = piece[0][2]
                    total = sum(ins[i][first : first + count].astype(F32) for i, first, _ in piece)
                    target[at : at + count] = total.astype(target.dtype)
                    at += count
                if kind == "halves":
                    half = at // 2
                    upper = place_of(bit)
                    results[out][...] = target[pl.ds(pl.multiple_of((1 - upper) * half, half), half), :].astype(BF)
                    results[out + 1][...] = target[pl.ds(pl.multiple_of(upper * half, half), half), :].astype(BF)

        return self.run(body, outs, "v" * len(args), args, scratch, us=1, vmem=16)


def shaped(*shape, dtype=BF):
    return jax.ShapeDtypeStruct(shape, dtype)


def norm_terms(rows_in):
    center = jnp.mean(rows_in, axis=-1, keepdims=True)
    centered = rows_in - center
    spread = jnp.mean(centered * centered, axis=-1, keepdims=True)
    scale = lax.rsqrt(spread + EPS)
    return centered * scale, scale


def norm_back(grad, gain, xhat, scale):
    e = grad * gain
    mean_e = jnp.mean(e, axis=-1, keepdims=True)
    mean_ex = jnp.mean(e * xhat, axis=-1, keepdims=True)
    return scale * (e - mean_e - xhat * mean_ex)


def valid_row(start_ref, end_ref, empty_ref, rows, half):
    lane = lax.broadcasted_iota(jnp.int32, (1, 2 * rows), 1)
    second = lane >= rows
    local = jnp.where(second, lane - rows, lane)
    device = lax.axis_index("tensor")
    clip = device // 2
    core = device % 2
    position = local + half * jnp.where(second, 1 - core, core)
    inside = (position >= start_ref[clip]) & (position < end_ref[clip])
    return (local < half) & jnp.logical_not(inside) & (empty_ref[clip] == 0)


def attention_forward(half, start_ref, end_ref, empty_ref, n_ref, pack, e_hbm, qT_ref, kT_ref, vT_ref, mixed_ref, inv_ref, s_buf, e_buf, sem):
    rows = qT_ref.shape[1]
    keys = kT_ref.shape[1]
    local = qT_ref.shape[0]
    heads = local // HEAD
    first_row = lax.broadcasted_iota(jnp.int32, (EXTRA, keys), 0) == 0
    ones16 = first_row.astype(F32).astype(BF)

    def project(first, last, count):
        product = dot(pack[:D, first * local : last * local], n_ref[:count, :], TT)
        return product + dot(pack[D:, first * local : last * local], ones16[:, :count], TN)

    qT_ref[...] = (project(0, 1, rows).astype(BF).astype(F32) * HEAD**-0.5).astype(BF)
    both = project(1, 3, keys).astype(BF)
    kT_ref[...] = both[:local]
    vT_ref[...] = both[local:]

    valid = valid_row(start_ref, end_ref, empty_ref, rows, half)
    some = jnp.max(valid.astype(F32), axis=1, keepdims=True)
    mask = jnp.where(first_row, jnp.where(valid, 0.0, -1e30), 0.0).astype(BF)

    blocks = [(h, c) for h in range(heads) for c in range(rows // CHUNK)]
    tops = {}

    def score(i):
        h, c = blocks[i]
        q = jnp.concatenate([qT_ref[h * HEAD : (h + 1) * HEAD, c * CHUNK : (c + 1) * CHUNK], ones16[:, :CHUNK]], axis=0)
        top = None
        for k in range(keys // CHUNK):
            span = slice(k * CHUNK, (k + 1) * CHUNK)
            s = dot(jnp.concatenate([kT_ref[h * HEAD : (h + 1) * HEAD, span], mask[:, span]], axis=0), q, TN)
            s_buf[i % 2, span, :] = s
            part = jnp.max(s.reshape(CHUNK // 8, 8, CHUNK), axis=0)
            top = part if top is None else jnp.maximum(top, part)
        tops[i] = jnp.max(top, axis=0, keepdims=True)

    copies = []
    score(0)
    for i, (h, c) in enumerate(blocks):
        if i + 1 < len(blocks):
            score(i + 1)
        columns = slice(c * CHUNK, (c + 1) * CHUNK)
        for k in range(keys // CHUNK):
            span = slice(k * CHUNK, (k + 1) * CHUNK)
            e_buf[h, c, span, :] = jnp.exp(s_buf[i % 2, span, :] - tops[i]).astype(BF)
        value = jnp.concatenate([vT_ref[h * HEAD : (h + 1) * HEAD, :], jnp.ones((EXTRA, keys), BF)], axis=0)
        o = dot(value, e_buf[h, c], NN)
        inv = some / o[HEAD : HEAD + 1, :]
        mixed_ref[h * HEAD : (h + 1) * HEAD, columns] = o[:HEAD] * inv
        inv_ref[h : h + 1, columns] = inv
        copy = pltpu.make_async_copy(e_buf.at[h, c], e_hbm.at[h, c], sem.at[i])
        copy.start()
        copies.append(copy)
    for copy in copies:
        copy.wait()


def ff_pack(first, w1_ref, w2_ref, b1_ref, out_ref):
    out_ref[:D, :] = w1_ref[:, first : first + CHUNK]
    for part in range(2):
        out_ref[D + part * CHUNK : D + (part + 1) * CHUNK, :] = w2_ref[first : first + CHUNK, part * CHUNK : (part + 1) * CHUNK]
    out_ref[2 * D :, :] = jnp.broadcast_to(b1_ref[...].reshape(1, -1)[:, first : first + CHUNK], (out_ref.shape[0] - 2 * D, CHUNK))


def pack_kernel(wq, wk, wv, wo, bq, bv, g1, s1, ob, g2, s2, rb, pack_ref, small_ref):
    local = wq.shape[1]
    for index, ref in enumerate((wq, wk, wv)):
        pack_ref[:D, index * local : (index + 1) * local] = ref[...]
    pack_ref[:D, 3 * local :] = wo[...].T
    pack_ref[D:, :] = jnp.zeros((EXTRA, 4 * local), BF)
    pack_ref[D : D + 1, :local] = bq[...].reshape(1, local)
    pack_ref[D : D + 1, 2 * local : 3 * local] = bv[...].reshape(1, local)
    for index, ref in enumerate((g1, s1, ob, g2, s2, rb)):
        small_ref[index : index + 1, :] = ref[...].astype(F32).reshape(1, D)


def start_kernel(half, start_ref, end_ref, empty_ref, x_ref, xs_ref, small_ref, pack, w1_ref, w2_ref, b1_ref, n_ref, ff_ref, *rest):
    rows = n_ref.shape[0] // 2
    gain = small_ref[0:1, :]
    shift = small_ref[1:2, :]
    for part, ref in enumerate((x_ref, xs_ref)):
        xhat, _ = norm_terms(ref[...].astype(F32))
        n_ref[part * rows : part * rows + half, :] = (xhat * gain + shift).astype(BF)
        n_ref[part * rows + half : (part + 1) * rows, :] = jnp.zeros((rows - half, D), BF)
    attention_forward(half, start_ref, end_ref, empty_ref, n_ref, pack, *rest)
    ff_pack(0, w1_ref, w2_ref, b1_ref, ff_ref)


def far_kernel(half, start_ref, end_ref, empty_ref, n_ref, pack, w1_ref, w2_ref, b1_ref, ff_ref, *rest):
    attention_forward(half, start_ref, end_ref, empty_ref, n_ref, pack, *rest)
    ff_pack(CHUNK, w1_ref, w2_ref, b1_ref, ff_ref)


def out_kernel(half, x_ref, m0, m1, m2, m3, pa0, pa1, pa2, pa3, small_ref, hidden_ref, n2_ref):
    local = m0.shape[0]
    mixed = jnp.concatenate([m[...].astype(BF) for m in (m0, m1, m2, m3)], axis=0)
    weight = jnp.concatenate([p[:D, 3 * local :] for p in (pa0, pa1, pa2, pa3)], axis=1)
    hidden_ref[...] = dot(mixed, weight, TT) + small_ref[2:3, :]
    hidden_ref[:half, :] += x_ref[...].astype(F32)
    xhat, _ = norm_terms(hidden_ref[...])
    n2_ref[...] = (xhat * small_ref[3:4, :] + small_ref[4:5, :]).astype(BF)


def phi_terms(inner):
    bell = jnp.exp(inner * inner * -0.5)
    x = jnp.abs(inner) * 0.7071067811865476
    t = 1.0 / (1.0 + 0.3275911 * x)
    poly = t * (0.254829592 + t * (-0.284496736 + t * (1.421413741 + t * (-1.453152027 + t * 1.061405429))))
    tail = 0.5 * poly * bell
    return jnp.where(inner >= 0, 1.0 - tail, tail), bell * 0.3989422804014327


def padded(cot_ref, rows):
    half = cot_ref.shape[0]
    return jnp.concatenate([cot_ref[...].astype(F32), jnp.zeros((rows - half, D), F32)], axis=0)


def ff_slots(n2, cot, packs, branch_ref, back_ref, grad_refs, bias_ref, act_buf, gi_buf):
    n2T = n2.T
    ones = jnp.ones((EXTRA, n2.shape[0]), BF)

    def weights(s):
        p = packs[s]
        return p[:D, :], jnp.concatenate([p[D : D + CHUNK, :], p[D + CHUNK : 2 * D, :]], axis=1)

    def enter(s):
        w1, w2 = weights(s)
        return dot(n2, w1, NN) + packs[s][2 * D : 2 * D + 1, :].astype(F32), dot(cot, w2, NT)

    ahead = enter(0)
    for s in range(TENSOR):
        inner, grad = ahead
        if s + 1 < TENSOR:
            ahead = enter(s + 1)
        cdf, density = phi_terms(inner)
        act_buf[s] = (inner * cdf).astype(BF)
        gi_buf[s] = (grad * (cdf + inner * density)).astype(BF)
        w1, w2 = weights(s)
        branch_ref[...] += dot(act_buf[s], w2, NN)
        back_ref[...] += dot(gi_buf[s], w1, NT)
        grad_refs[s][:D, :] = dot(n2T, gi_buf[s], NN).astype(BF)
        second = dot(act_buf[s], cot, TN).astype(BF)
        grad_refs[s][D : D + CHUNK, :] = second[:, :CHUNK]
        grad_refs[s][D + CHUNK : 2 * D, :] = second[:, CHUNK:]
        bias_ref[s : s + 1, :] = dot(ones, gi_buf[s], NN)[:1]


def ff_kernel(n2_ref, cot_ref, p0, p1, p2, p3, branch_ref, back_ref, g0, g1, g2, g3, bias_ref, act_buf, gi_buf):
    branch_ref[...] = jnp.zeros(branch_ref.shape, F32)
    back_ref[...] = jnp.zeros(back_ref.shape, F32)
    cot = padded(cot_ref, n2_ref.shape[0]).astype(BF)
    ff_slots(n2_ref[...], cot, (p0, p1, p2, p3), branch_ref, back_ref, (g0, g1, g2, g3), bias_ref, act_buf, gi_buf)


def turn_kernel(n2_ref, cot_ref, p0, p1, p2, p3, branch_in, back_in, hidden_ref, m0, m1, m2, m3, pa0, pa1, pa2, pa3, small_in,
                out_ref, gh_ref, dT0, dT1, dT2, dT3, g0, g1, g2, g3, o0, o2, o_send, bias_ref, small_ref, act_buf, gi_buf, branch_buf, back_buf):
    local = m0.shape[0]
    cot_f = padded(cot_ref, n2_ref.shape[0])
    branch_buf[...] = branch_in[...]
    back_buf[...] = back_in[...]
    ff_slots(n2_ref[...], cot_f.astype(BF), (p0, p1, p2, p3), branch_buf, back_buf, (g0, g1, g2, g3), bias_ref, act_buf, gi_buf)
    hidden = hidden_ref[...]
    back = back_buf[...]
    xhat, scale = norm_terms(hidden)
    grad_hidden = cot_f + norm_back(back, small_in[3:4, :], xhat, scale)
    gh_ref[...] = grad_hidden
    small_ref[0:1, :] = jnp.sum(grad_hidden, axis=0, keepdims=True)
    small_ref[1:2, :] = jnp.sum(back * xhat, axis=0, keepdims=True)
    small_ref[2:3, :] = jnp.sum(back, axis=0, keepdims=True)
    small_ref[3:4, :] = jnp.sum(cot_f, axis=0, keepdims=True)
    out_ref[...] = (hidden + branch_buf[...] + small_in[5:6, :])[: out_ref.shape[0]].astype(BF)
    low = grad_hidden.astype(BF)
    weight = jnp.concatenate([p[:D, 3 * local :] for p in (pa0, pa1, pa2, pa3)], axis=1)
    grads_T = dot(weight, low, TT).astype(BF)
    for s, ref in enumerate((dT0, dT1, dT2, dT3)):
        ref[...] = grads_T[s * local : (s + 1) * local]
    mixed = jnp.concatenate([m[...].astype(BF) for m in (m0, m1, m2, m3)], axis=0)
    grad = dot(mixed, low, NN).astype(BF)
    for s, (ref, first) in enumerate(((o0, 0), (o_send, 0), (o2, 0), (o_send, 2 * local))):
        for part in range(2):
            at = first + part * local
            ref[at : at + local, :] = grad[s * local : (s + 1) * local, part * CHUNK : (part + 1) * CHUNK]


def attention_backward(e_hbm, dT_ref, inv_ref, mixed_ref, vT_ref, qT_ref, kT_ref, n_ref, dq_ref, dk_ref, dv_ref, grad_ref, bias_ref,
                       e_buf, ds_buf, sem):
    rows = qT_ref.shape[1]
    keys = kT_ref.shape[1]
    local = qT_ref.shape[0]
    heads = local // HEAD
    blocks = [(h, c) for h in range(heads) for c in range(rows // CHUNK)]
    copies = [pltpu.make_async_copy(e_hbm.at[h, c], e_buf.at[h, c], sem.at[i]) for i, (h, c) in enumerate(blocks)]
    for copy in copies:
        copy.start()
    which = lax.broadcasted_iota(jnp.int32, (EXTRA, CHUNK), 0)
    ones2 = (lax.broadcasted_iota(jnp.int32, (EXTRA, CHUNK), 0) < 2).astype(F32).astype(BF)
    lows = {}

    def enter(i):
        h, c = blocks[i]
        here = slice(h * HEAD, (h + 1) * HEAD)
        columns = slice(c * CHUNK, (c + 1) * CHUNK)
        low = (dT_ref[here, columns].astype(F32) * inv_ref[h : h + 1, columns]).astype(BF)
        delta = jnp.sum(low.astype(F32) * mixed_ref[here, columns], axis=0, keepdims=True)
        high = (-delta).astype(BF).astype(F32)
        extra = jnp.where(which == 0, high, jnp.where(which == 1, -delta - high, 0.0)).astype(BF)
        more = jnp.concatenate([low, extra], axis=0)
        lows[i] = low
        copies[i].wait()
        for k in range(keys // CHUNK):
            span = slice(k * CHUNK, (k + 1) * CHUNK)
            v = jnp.concatenate([vT_ref[here, span], ones2], axis=0)
            ds_buf[i % 2, span, :] = (e_buf[h, c, span, :].astype(F32) * dot(v, more, TN)).astype(BF)

    dv = None
    dk = None
    enter(0)
    for i, (h, c) in enumerate(blocks):
        if i + 1 < len(blocks):
            enter(i + 1)
        here = slice(h * HEAD, (h + 1) * HEAD)
        columns = slice(c * CHUNK, (c + 1) * CHUNK)
        part = dot(lows[i], e_buf[h, c], NT)
        dv = part if c == 0 else dv + part
        dq_ref[here, columns] = (dot(kT_ref[here, :], ds_buf[i % 2], NN) * HEAD**-0.5).astype(BF)
        part = dot(qT_ref[here, columns], ds_buf[i % 2], NT)
        dk = part if c == 0 else dk + part
        if c == rows // CHUNK - 1:
            dv_ref[here, :] = dv.astype(BF)
            dk_ref[here, :] = dk.astype(BF)
    nT = n_ref[...].T
    ones = jnp.ones((EXTRA, rows), BF)
    for index, (ref, count) in enumerate(((dq_ref, rows), (dk_ref, keys), (dv_ref, keys))):
        columns = slice(index * local, (index + 1) * local)
        grad_ref[:, columns] = dot(nT[:, :count], ref[...], NT).astype(BF)
        sums = sum(dot(ones, ref[:, i * rows : (i + 1) * rows], NT) for i in range(count // rows))
        bias_ref[0:1, columns] = sums[:1]


def first_kernel(half, x_ref, xs_ref, pa0, pa1, pa2, pa3, *rest):
    sources = rest[:12]
    small_two, b0, b1, b2, b3, f0, f1, own_ref, sib_ref, small_ref = rest[12:]
    local = pa0.shape[1] // TENSOR
    rows = own_ref.shape[0]
    device = lax.axis_index("tensor")
    small_ref[...] = jnp.zeros(small_ref.shape, F32)
    gain_sum = 0.0
    shift_sum = 0.0
    for part, ref in enumerate((x_ref, xs_ref)):
        columns = slice(part * rows, (part + 1) * rows)
        total = None
        for slot, p in enumerate((pa0, pa1, pa2, pa3)):
            for index in range(part, 3):
                term = dot(sources[slot * 3 + index][:, columns], p[:D, index * local : (index + 1) * local], TT)
                total = term if total is None else total + term
        if part == 0:
            own_ref[...] = total
        else:
            sib_ref[...] = total.astype(BF)
        xhat, _ = norm_terms(ref[...].astype(F32))
        gain_sum = gain_sum + jnp.sum(total[:half] * xhat, axis=0, keepdims=True)
        shift_sum = shift_sum + jnp.sum(total, axis=0, keepdims=True)
    small_ref[0:4, :] = small_two[...]
    small_ref[4:5, :] = gain_sum
    small_ref[5:6, :] = shift_sum
    for slot, b in enumerate((b0, b1, b2, b3)):
        owner = jnp.bitwise_xor(device, slot)
        small_ref[pl.ds(8 + owner, 1), :] = jnp.concatenate([f[slot : slot + 1, :] for f in (f0, f1)], axis=1)
        small_ref[pl.ds(12 + owner, 1), : 3 * local] = b[...]


def last_kernel(x_ref, own_ref, got_ref, gh_ref, small_ref, out_ref):
    half = out_ref.shape[0]
    grad = own_ref[:half, :] + got_ref[:half, :].astype(F32)
    xhat, scale = norm_terms(x_ref[...].astype(F32))
    out_ref[...] = gh_ref[:half, :] + norm_back(grad, small_ref[0:1, :], xhat, scale)


def place_of(bit):
    return lax.rem(lax.div(lax.axis_index("dp"), bit), 2)


def merge(kept, got, buf, bit=1):
    rows = kept.shape[0]
    upper = place_of(bit)
    buf[pl.ds(pl.multiple_of(upper * rows, rows), rows), :] = kept[...].astype(F32)
    buf[pl.ds(pl.multiple_of((1 - upper) * rows, rows), rows), :] = got[...].astype(F32)


def finish_ff_kernel(first, kept, got, expand_ref, reduce_ref, out_ref, second):
    local = out_ref.shape[0]
    merge(kept, got, second)
    for index, ref in enumerate((first, second)):
        lanes = slice(index * CHUNK, (index + 1) * CHUNK)
        expand_ref[:, lanes] = ref[:D, :].astype(F32)
        for part in range(2):
            rows = slice(D + part * CHUNK, D + (part + 1) * CHUNK)
            reduce_ref[lanes, part * CHUNK : (part + 1) * CHUNK] = ref[rows, :].astype(F32)
    for part in range(2):
        rows = slice(2 * D + part * local, 2 * D + (part + 1) * local)
        out_ref[:, part * CHUNK : (part + 1) * CHUNK] = second[rows, :]


def finish_qkv_kernel(kept, got, sums_ref, more_ref, q_ref, k_ref, v_ref, bias_q, bias_v, bias_ff, s0, s1, s2, s3, s4, s5, buf, sums):
    merge(kept, got, buf)
    local = q_ref.shape[1]
    for index, ref in enumerate((q_ref, k_ref, v_ref)):
        ref[...] = buf[:, index * local : (index + 1) * local]
        ref.flush()
    sums[...] = sums_ref[...] + more_ref[...]
    device = lax.axis_index("tensor")
    for index, ref in enumerate((s0, s1, s2, s3, s4, s5)):
        ref[...] = sums[index : index + 1, :].reshape(D)
    bias_ff[...] = sums[pl.ds(8 + device, 1), :].reshape(D)
    both = sums[pl.ds(12 + device, 1), :]
    bias_q[...] = both[:, :local].reshape(local)
    bias_v[...] = both[:, 2 * local : 3 * local].reshape(local)


class Chain:
    def __init__(self, along, size, halvings, pieces):
        bits = [1 << i for i in range(size.bit_length() - 1)]
        halvings = min(halvings, len(bits))
        self.along = along
        self.plan = [("half", b) for b in bits[:halvings]] + [("full", b) for b in bits[halvings:]]
        self.plan += [("back", b) for b in reversed(bits[:halvings])]
        self.at = -1
        self.pieces = pieces

    def left(self):
        return len(self.plan) - 1 - self.at

    def last(self):
        return tuple(self.pieces[0])

    def due(self):
        kind, bit = self.plan[self.at + 1]
        if kind == "half":
            return "halves", self.pieces, bit
        if self.at >= 0 and self.plan[self.at][0] == "back":
            return ("merge",) + tuple(self.pieces[0]) + (self.plan[self.at][1],)
        return "sum", self.pieces

    def taken(self, *results):
        self.at += 1
        send, keep = results if len(results) == 2 else results * 2
        self.pieces = [(keep, self.along(send, self.plan[self.at][1]))]


def swap(value, axis, size, bit):
    return lax.ppermute(value, axis, [(i, i ^ bit) for i in range(size)])


def on_device(dp, frames, query_weight, query_bias, key_weight, value_weight, value_bias, out_weight, out_bias, first_gain, first_shift,
              expand_weight, expand_bias, reduce_weight, reduce_bias, second_gain, second_shift, span_start, span_end, empty_flag, cotangent):
    half = frames.shape[0]
    rows = -(-half // CHUNK) * CHUNK
    keys = 2 * rows
    local = query_weight.shape[1]
    heads = local // HEAD
    blocks = rows // CHUNK
    line = Line()

    def across(v, bit):
        return swap(v, "tensor", TENSOR, bit)

    def along(v, bit):
        return swap(v, "dp", dp, bit)

    xs = across(frames, 1)
    pa0, small = line.run(
        pack_kernel, (shaped(D + EXTRA, 4 * local), shaped(8, D, dtype=F32)), "f" * 12,
        (query_weight, key_weight, value_weight, out_weight, query_bias, value_bias,
         first_gain, first_shift, out_bias, second_gain, second_shift, reduce_bias), us=2,
    )
    pa2 = across(pa0, 2)
    pa1 = across(pa0, 1)

    forward_outs = (
        (shaped(heads, blocks, keys, CHUNK), "h"), shaped(local, rows), shaped(local, keys), shaped(local, keys),
        shaped(local, rows, dtype=F32), shaped(heads, rows, dtype=F32),
    )
    forward_scratch = (
        pltpu.VMEM((2, keys, CHUNK), F32),
        pltpu.VMEM((heads, blocks, keys, CHUNK), BF),
        pltpu.SemaphoreType.DMA((heads * blocks,)),
    )
    spans = (span_start, span_end, empty_flag)
    ff_weights = (expand_weight, reduce_weight, expand_bias)
    ff0_shape = shaped(2 * D + 3 * EXTRA, CHUNK)
    ff1_shape = shaped(2 * D + 4 * EXTRA, CHUNK)
    normed, ff0, *s0 = line.run(
        functools.partial(start_kernel, half), (shaped(keys, D), ff0_shape) + forward_outs, "sssfvvvfff",
        spans + (frames, xs, small, pa0) + ff_weights, forward_scratch, us=8,
    )
    ff0_far = across(ff0, 2)
    ff0_near = across(ff0, 1)
    s1 = line.run(
        functools.partial(attention_forward, half), forward_outs, "sssvv",
        spans + (normed, pa1), forward_scratch, us=7,
    )
    pa2 = line.touch(pa2)
    pa3 = across(pa2, 1)
    ff1, *s2 = line.run(
        functools.partial(far_kernel, half), (ff1_shape,) + forward_outs, "sssvvfff",
        spans + (normed, pa2) + ff_weights, forward_scratch, us=7,
    )
    ff1_far = across(ff1, 2)
    s3 = line.run(
        functools.partial(attention_forward, half), forward_outs, "sssvv",
        spans + (normed, pa3), forward_scratch, us=7,
    )
    slots = (s0, s1, s2, s3)
    mixed = tuple(s[4] for s in slots)
    packs = (pa0, pa1, pa2, pa3)
    ff0_far = line.touch(ff0_far)
    ff0_cross = across(ff0_far, 1)
    whole = shaped(rows, D, dtype=F32)
    hidden, n2 = line.run(
        functools.partial(out_kernel, half), (whole, shaped(rows, D)), "f" + "v" * 9,
        (frames,) + mixed + packs + (small,), us=8,
    )
    ff1_near = across(ff1, 1)
    ff_scratch = (pltpu.VMEM((TENSOR, rows, CHUNK), BF), pltpu.VMEM((TENSOR, rows, CHUNK), BF))
    bias_shape = shaped(TENSOR, CHUNK, dtype=F32)
    ff_grads = (shaped(2 * D, CHUNK),) * TENSOR
    branch, back, a0, a1, a2, a3, bias_a = line.run(
        ff_kernel, (whole, whole) + ff_grads + (bias_shape,), "vfvvvv",
        (n2, cotangent, ff0, ff0_near, ff0_far, ff0_cross), ff_scratch, us=8,
    )
    got_a1 = across(a1, 1)
    got_a3 = across(a3, 1)
    ff1_far = line.touch(ff1_far)
    ff1_cross = across(ff1_far, 1)
    spare = jnp.zeros((EXTRA, CHUNK), BF)
    (far_a,) = line.tick(("sum", [(a2, got_a3), (spare,)]))
    y_a = across(far_a, 2)
    size_b = 2 * D + 2 * local
    output, grad_hidden, *rest = line.run(
        turn_kernel,
        ((shaped(half, D), "f"), (whole, "f")) + (shaped(local, rows),) * TENSOR + ff_grads
        + (shaped(2 * local, CHUNK), shaped(2 * local, CHUNK), shaped(4 * local, CHUNK), bias_shape, shaped(4, D, dtype=F32)),
        "vf" + "v" * 16,
        (n2, cotangent, ff1, ff1_near, ff1_far, ff1_cross, branch, back, hidden) + mixed + packs + (small,),
        ff_scratch + (pltpu.VMEM((rows, D), F32), pltpu.VMEM((rows, D), F32)), us=12, vmem=30,
    )
    dT, (f0, f1, f2, f3, o0, o2, o_send, bias_b, small_two) = rest[:TENSOR], rest[TENSOR:]
    got_f1 = across(f1, 1)
    got_f3 = across(f3, 1)
    got_o = across(o_send, 1)

    backward_outs = (
        shaped(local, rows), shaped(local, keys), shaped(local, keys), shaped(D, 3 * local), shaped(1, 3 * local, dtype=F32),
    )

    def backward(slot):
        e, q, k, v, m, inv = slots[slot]
        return line.run(
            attention_backward, backward_outs, "h" + "v" * 7,
            (e, dT[slot], inv, m, v, q, k, normed),
            (
                pltpu.VMEM((heads, blocks, keys, CHUNK), BF), pltpu.VMEM((2, keys, CHUNK), BF),
                pltpu.SemaphoreType.DMA((heads * blocks,)),
            ),
            us=8,
        )

    def chain(halvings, pieces):
        return Chain(along, dp, halvings, pieces)

    *d3, g3, b3 = backward(3)
    chain_a = chain(1, [(a0, got_a1, (y_a, 0, 2 * D))])
    pair = 2 * local
    far_b, send_3, *halves = line.tick(
        ("sum", [(f2, got_f3), (o2, (got_o, pair, pair))]), ("sum", [(g3,)]), chain_a.due()
    )
    y_b = across(far_b, 2)
    got_3 = across(send_3, 1)
    chain_a.taken(*halves)
    *d2, g2, b2 = backward(2)
    far_q, *whole_a = line.tick(("sum", [(g2, got_3)]), chain_a.due())
    y_q = across(far_q, 2)
    chain_a.taken(*whole_a)
    *d1, g1, b1 = backward(1)
    chain_b = chain(2, [(f0, got_f1, (y_b, 0, 2 * D)), (o0, (got_o, 0, pair), (y_b, 2 * D, pair))])
    middle = D // 2
    upper_1, lower_1, whole_a, *halves = line.tick(
        ("sum", [((g1, 0, middle),)]), ("sum", [((g1, middle, middle),)]), chain_a.due(), chain_b.due()
    )
    got_1 = (across(upper_1, 1), across(lower_1, 1))
    chain_a.taken(whole_a)
    chain_b.taken(*halves)
    *d0, g0, b0 = backward(0)
    chain_q = chain(1, [((g0, i * middle, middle), got_1[i], (y_q, i * middle, middle)) for i in range(2)])
    send_q, keep_q, *halves = line.tick(chain_q.due(), chain_b.due())
    chain_q.taken(send_q, keep_q)
    chain_b.taken(*halves)
    own, sib, sums = line.run(
        functools.partial(first_kernel, half), (whole, shaped(rows, D), shaped(16, D, dtype=F32)), "f" + "v" * 24,
        (frames, xs) + packs + (*d0, *d1, *d2, *d3, small_two, b0, b1, b2, b3, bias_a, bias_b), us=6,
    )
    part_q, part_b, part_a, sums, sib = line.tick(
        chain_q.due(), chain_b.due(), chain_a.due(), ("sum", [(sums,)]), ("sum", [(sib,)])
    )
    chain_q.taken(part_q)
    chain_b.taken(part_b)
    chain_a.taken(part_a)
    pending = across(sums, 1)
    got = across(sib, 1)
    (sums,) = line.tick(("sum", [(sums, pending)]))
    pending = across(sums, 2)
    (grad_frames,) = line.run(
        last_kernel, ((shaped(half, D, dtype=F32), "f"),), "fvvfv", (frames, own, got, grad_hidden, small), us=4
    )
    bits = [1 << i for i in range(dp.bit_length() - 1)]
    whole_a = None
    turn = 0
    while bits or any(c.left() for c in (chain_a, chain_b, chain_q)):
        rounds = ([chain_q], [chain_b, chain_a]) if turn % 2 == 0 else ([chain_b, chain_a],)
        for index, chains in enumerate(rounds):
            due = [c for c in chains if c.left()]
            with_sums = index == 0 and bits
            with_a = turn > 0 and whole_a is None and not chain_a.left()
            jobs = [c.due() for c in due] + [("sum", [(sums, pending)])] * bool(with_sums)
            jobs += [("merge",) + chain_a.last() + (1,)] * with_a
            if not jobs:
                continue
            made = list(line.tick(*jobs))
            for c in due:
                c.taken(made.pop(0))
            if with_sums:
                sums = made.pop(0)
                pending = along(sums, bits.pop(0))
            if with_a:
                whole_a = made.pop(0)
        turn += 1
    grad_expand, grad_reduce, grad_out = line.run(
        finish_ff_kernel, tuple((shaped(*o, dtype=F32), "f") for o in ((D, 2 * CHUNK), (2 * CHUNK, D), (local, D))),
        "vvv", (whole_a,) + chain_b.last(), (pltpu.VMEM((size_b, CHUNK), F32),), us=2,
    )
    vector = (shaped(D, dtype=F32), "f")
    short = (shaped(local, dtype=F32), "f")
    grad_q, grad_k, grad_v, bias_q, bias_v, bias_ff, *globals_ = line.run(
        finish_qkv_kernel, ((shaped(D, local, dtype=F32), "f"),) * 3 + (short, short, vector) + (vector,) * 6, "vvvv",
        chain_q.last() + (sums, pending), (pltpu.VMEM((D, 3 * local), F32), pltpu.VMEM(sums.shape, F32)), us=1,
    )
    return (
        output, grad_frames, grad_q, bias_q, grad_k, grad_v, bias_v, grad_out, globals_[0], globals_[4], globals_[5],
        grad_expand, bias_ff, grad_reduce, globals_[3], globals_[1], globals_[2],
    )


def solution(mesh):
    dp = mesh.shape["dp"]
    assert mesh.shape["tensor"] == TENSOR and dp & (dp - 1) == 0
    split = P(("dp", "tensor"), None)
    column = P(None, "tensor")
    return jax.shard_map(
        functools.partial(on_device, dp),
        mesh=mesh,
        in_specs=(
            split, column, P("tensor"), column, column, P("tensor"), P("tensor", None), P(), P(), P(),
            column, P("tensor"), P("tensor", None), P(), P(), P(), P("dp"), P("dp"), P("dp"), split,
        ),
        out_specs=(
            split, split, column, P("tensor"), column, column, P("tensor"), P("tensor", None), P(), P(), P(),
            column, P("tensor"), P("tensor", None), P(), P(), P(),
        ),
        check_vma=False,
    )
```

```python
import functools

import jax
import jax.numpy as jnp
from jax import lax
from jax.experimental import pallas as pl
from jax.experimental.pallas import tpu as pltpu
from jax.sharding import PartitionSpec as P

BF = jnp.bfloat16
F32 = jnp.float32
D = 512
HEADS = 8
HEAD = D // HEADS
EPS = 1e-05
TENSOR = 4
CHUNK = 256
EXTRA = 16
LANES = 128
NN = (((1,), (0,)), ((), ()))
NT = (((1,), (1,)), ((), ()))
TN = (((0,), (0,)), ((), ()))
TT = (((0,), (1,)), ((), ()))
VMEM = pl.BlockSpec(memory_space=pltpu.VMEM)
SMEM = pl.BlockSpec(memory_space=pltpu.SMEM)
ANY = pl.BlockSpec(memory_space=pl.ANY)


def dot(left, right, dims):
    return lax.dot_general(left, right, dims, preferred_element_type=F32)


class Fetched:
    def __init__(self, source, buffer, sem):
        self.buffer, self.shape, self.waited = buffer, buffer.shape, False
        self.copy = pltpu.make_async_copy(source, buffer, sem)
        self.copy.start()

    def __getitem__(self, index):
        if not self.waited:
            self.copy.wait()
            self.waited = True
        return self.buffer[index]


class Stored:
    def __init__(self, target, buffer, sem):
        self.buffer, self.shape, self.dtype, self.sent = buffer, buffer.shape, buffer.dtype, False
        self.copy = pltpu.make_async_copy(buffer, target, sem)

    def __getitem__(self, index):
        return self.buffer[index]

    def __setitem__(self, index, value):
        self.buffer[index] = value

    def flush(self):
        if not self.sent:
            self.copy.start()
            self.sent = True


HBM = pl.BlockSpec(memory_space=pltpu.HBM)
SPEC = {"f": HBM, "h": HBM, "s": HBM, "v": VMEM, "V": VMEM}
PINNED = {"f": pltpu.HBM, "h": pltpu.HBM, "s": pltpu.HBM, "V": pltpu.VMEM}


class Rows:
    def __init__(self, *refs):
        self.refs, self.at = refs, [0]
        for ref in refs:
            self.at.append(self.at[-1] + ref.shape[0])

    def spans(self, rows):
        first, last, _ = rows.indices(self.at[-1])
        for ref, low, high in zip(self.refs, self.at, self.at[1:]):
            if max(first, low) < min(last, high):
                yield ref, slice(max(first, low) - low, min(last, high) - low), slice(max(first, low) - first, min(last, high) - first)

    def __getitem__(self, index):
        parts = [ref[here, index[1]] for ref, here, _ in self.spans(index[0])]
        return parts[0] if len(parts) == 1 else jnp.concatenate(parts, axis=0)

    def __setitem__(self, index, value):
        for ref, here, there in self.spans(index[0]):
            ref[here, index[1]] = value[there]


class Line:
    def __init__(self):
        self.waits = ()

    def run(self, kernel, outs, ins, args, scratch=(), us=8, vmem=12):
        waits = self.waits
        outs = [o if isinstance(o, tuple) else (o, "v") for o in outs]
        kinds = list(ins)
        skip, last = len(kinds), len(outs)
        moved = [i for i, k in enumerate(kinds) if k in "fs"]
        built = [i for i, (_, k) in enumerate(outs) if k == "f"]
        space = {"f": pltpu.VMEM, "s": pltpu.SMEM}
        buffers = [space[kinds[i]](args[i].shape, args[i].dtype) for i in moved] + [pltpu.VMEM(outs[i][0].shape, outs[i][0].dtype) for i in built]

        def body(*refs):
            inputs = list(refs[:skip])
            rest = refs[skip + len(waits) :]
            results, zeros, rest = list(rest[:last]), rest[last], rest[last + 1 :]
            held, sems, rest = rest[: len(buffers)], rest[len(buffers)], rest[len(buffers) + 1 :]
            for n, i in enumerate(moved):
                inputs[i] = Fetched(inputs[i], held[n], sems.at[n])
            for n, i in enumerate(built, len(moved)):
                results[i] = Stored(results[i], held[n], sems.at[n])
            zeros[...] = jnp.zeros((8, 128), F32)
            kernel(*inputs, *results, *rest)
            for i in built:
                results[i].flush()
            for i in moved:
                if not inputs[i].waited:
                    inputs[i].copy.wait()
            for i in built:
                results[i].copy.wait()

        *got, zeros = pl.pallas_call(
            body,
            out_shape=tuple(PINNED[k](o.shape, o.dtype) if k in PINNED else o for o, k in outs) + (jax.ShapeDtypeStruct((8, 128), F32),),
            in_specs=[SPEC[k] for k in kinds] + [ANY] * len(waits),
            out_specs=[SPEC[k] for _, k in outs] + [VMEM],
            scratch_shapes=buffers + [pltpu.SemaphoreType.DMA((len(buffers) + 1,))] + list(scratch),
            compiler_params=pltpu.CompilerParams(vmem_limit_bytes=vmem * 2**20),
            cost_estimate=pl.CostEstimate(flops=10**6, bytes_accessed=2**10, transcendentals=0),
        )(*(pltpu.with_memory_space_constraint(a, PINNED[k]) if k in PINNED else a for a, k in zip(args, kinds)), *waits)
        self.waits = (zeros,)
        return got

    def touch(self, value):
        waits = self.waits
        got = (
            pl.pallas_call(
                lambda given, *rest: None,
                out_shape=jax.ShapeDtypeStruct(value.shape, value.dtype),
                in_specs=[ANY] * (1 + len(waits)),
                out_specs=ANY,
                input_output_aliases={0: 0},
                compiler_params=pltpu.CompilerParams(vmem_limit_bytes=2**20),
                cost_estimate=pl.CostEstimate(flops=10**6, bytes_accessed=1024, transcendentals=0),
            )(value, *waits)
        )
        self.waits = self.waits + (got,)
        return got

    def tick(self, *jobs):
        args, outs, scratch, plans = [], [], [], []

        def place(part):
            array, first, rows = part if isinstance(part, tuple) else (part, 0, part.shape[0])
            args.append(array)
            return len(args) - 1, first, rows

        for kind, *rest in jobs:
            pieces = [[place(part) for part in piece] for piece in ([[p] for p in rest[:2]] if kind == "merge" else rest[0])]
            rows = sum(piece[0][2] for piece in pieces)
            like = args[pieces[0][0][0]]
            columns = like.shape[1:]
            plans.append((kind, pieces, len(outs), len(scratch), rest[-1]))
            if kind == "halves":
                outs += [shaped(rows // 2, *columns)] * 2
            else:
                outs.append(jax.ShapeDtypeStruct((rows, *columns), like.dtype))
            if kind != "sum":
                scratch.append(pltpu.VMEM((rows, *columns), F32))

        def body(*refs):
            ins, results, buffers = refs[: len(args)], refs[len(args) : len(args) + len(outs)], refs[len(args) + len(outs) :]
            for kind, pieces, out, held, bit in plans:
                if kind == "merge":
                    kept, got = (ins[piece[0][0]] for piece in pieces)
                    merge(kept, got, buffers[held], bit)
                    results[out][...] = buffers[held][...].astype(results[out].dtype)
                    continue
                target = buffers[held] if kind == "halves" else results[out]
                at = 0
                for piece in pieces:
                    count = piece[0][2]
                    total = sum(ins[i][first : first + count].astype(F32) for i, first, _ in piece)
                    target[at : at + count] = total.astype(target.dtype)
                    at += count
                if kind == "halves":
                    half = at // 2
                    upper = place_of(bit)
                    results[out][...] = target[pl.ds(pl.multiple_of((1 - upper) * half, half), half), :].astype(BF)
                    results[out + 1][...] = target[pl.ds(pl.multiple_of(upper * half, half), half), :].astype(BF)

        return self.run(body, outs, "v" * len(args), args, scratch, us=1, vmem=6)


def shaped(*shape, dtype=BF):
    return jax.ShapeDtypeStruct(shape, dtype)


def norm_terms(rows_in):
    center = jnp.mean(rows_in, axis=-1, keepdims=True)
    centered = rows_in - center
    spread = jnp.mean(centered * centered, axis=-1, keepdims=True)
    scale = lax.rsqrt(spread + EPS)
    return centered * scale, scale


def norm_back(grad, gain, xhat, scale):
    e = grad * gain
    mean_e = jnp.mean(e, axis=-1, keepdims=True)
    mean_ex = jnp.mean(e * xhat, axis=-1, keepdims=True)
    return scale * (e - mean_e - xhat * mean_ex)


def valid_row(start_ref, end_ref, empty_ref, rows, half):
    lane = lax.broadcasted_iota(jnp.int32, (1, 2 * rows), 1)
    second = lane >= rows
    local = jnp.where(second, lane - rows, lane)
    device = lax.axis_index("tensor")
    clip = device // 2
    core = device % 2
    position = local + half * jnp.where(second, 1 - core, core)
    inside = (position >= start_ref[clip]) & (position < end_ref[clip])
    return (local < half) & jnp.logical_not(inside) & (empty_ref[clip] == 0)


def attention_forward(half, start_ref, end_ref, empty_ref, nT_ref, pack, e_ref, qT_ref, kT_ref, vT_ref, mixed_ref, inv_ref, s_buf):
    rows = qT_ref.shape[1]
    keys = kT_ref.shape[1]
    local = qT_ref.shape[0]
    heads = local // HEAD
    first_row = lax.broadcasted_iota(jnp.int32, (EXTRA, keys), 0) == 0
    ones16 = first_row.astype(F32).astype(BF)

    def project(first, last, count):
        product = dot(pack[:D, first * local : last * local], nT_ref[:, :count], TN)
        bias = dot(pack[D:, first * local : last * local], ones16[:, :LANES], TN)
        return product + jnp.concatenate([bias] * (count // LANES), axis=1)

    qT_ref[...] = (project(0, 1, rows).astype(BF).astype(F32) * HEAD**-0.5).astype(BF)
    both = project(1, 3, keys).astype(BF)
    kT_ref[...] = both[:local]
    vT_ref[...] = both[local:]

    valid = valid_row(start_ref, end_ref, empty_ref, rows, half)
    some = jnp.max(valid.astype(F32), axis=1, keepdims=True)
    mask = jnp.where(first_row, jnp.where(valid, 0.0, -1e30), 0.0).astype(BF)

    blocks = [(h, c) for h in range(heads) for c in range(rows // CHUNK)]
    tops = {}

    def score(i):
        h, c = blocks[i]
        q = jnp.concatenate([qT_ref[h * HEAD : (h + 1) * HEAD, c * CHUNK : (c + 1) * CHUNK], ones16[:, :CHUNK]], axis=0)
        top = None
        for k in range(keys // CHUNK):
            span = slice(k * CHUNK, (k + 1) * CHUNK)
            s = dot(jnp.concatenate([kT_ref[h * HEAD : (h + 1) * HEAD, span], mask[:, span]], axis=0), q, TN)
            s_buf[i % 2, span, :] = s
            part = jnp.max(s.reshape(CHUNK // 8, 8, CHUNK), axis=0)
            top = part if top is None else jnp.maximum(top, part)
        tops[i] = jnp.max(top, axis=0, keepdims=True)

    score(0)
    for i, (h, c) in enumerate(blocks):
        if i + 1 < len(blocks):
            score(i + 1)
        columns = slice(c * CHUNK, (c + 1) * CHUNK)
        for k in range(keys // CHUNK):
            span = slice(k * CHUNK, (k + 1) * CHUNK)
            e_ref[h, c, span, :] = jnp.exp(s_buf[i % 2, span, :] - tops[i]).astype(BF)
        value = jnp.concatenate([vT_ref[h * HEAD : (h + 1) * HEAD, :], jnp.ones((EXTRA, keys), BF)], axis=0)
        o = dot(value, e_ref[h, c], NN)
        inv = some / o[HEAD : HEAD + 1, :]
        mixed_ref[h * HEAD : (h + 1) * HEAD, columns] = o[:HEAD] * inv
        inv_ref[h : h + 1, columns] = inv


def ff_pack(first, w1_ref, w2_ref, b1_ref, out_ref):
    out_ref[:D, :] = w1_ref[:, first : first + CHUNK]
    for part in range(2):
        out_ref[D + part * CHUNK : D + (part + 1) * CHUNK, :] = w2_ref[first : first + CHUNK, part * CHUNK : (part + 1) * CHUNK]
    out_ref[2 * D :, :] = jnp.broadcast_to(b1_ref[...].reshape(1, -1)[:, first : first + CHUNK], (out_ref.shape[0] - 2 * D, CHUNK))


def pack_kernel(wq, wk, wv, wo, bq, bv, g1, s1, ob, g2, s2, rb, pack_ref, small_ref):
    local = wq.shape[1]
    for index, ref in enumerate((wq, wk, wv)):
        pack_ref[:D, index * local : (index + 1) * local] = ref[...]
    pack_ref[:D, 3 * local :] = wo[...].T
    pack_ref[D:, :] = jnp.zeros((EXTRA, 4 * local), BF)
    pack_ref[D : D + 1, :local] = bq[...].reshape(1, local)
    pack_ref[D : D + 1, 2 * local : 3 * local] = bv[...].reshape(1, local)
    for index, ref in enumerate((g1, s1, ob, g2, s2, rb)):
        small_ref[index : index + 1, :] = ref[...].astype(F32).reshape(1, D)


def start_kernel(half, start_ref, end_ref, empty_ref, x_ref, xs_ref, small_ref, pack, w1_ref, w2_ref, b1_ref, nT_ref, ff_ref, pad_ref, *rest):
    *rest, n_buf = rest
    rows = n_buf.shape[0]
    pad_ref[half:, :] = jnp.zeros((rows - half, D), BF)
    pad_ref[:half, :] = x_ref[...]
    gain = small_ref[0:1, :]
    shift = small_ref[1:2, :]
    for part, ref in enumerate((x_ref, xs_ref)):
        xhat, _ = norm_terms(ref[...].astype(F32))
        n_buf[:half, :] = (xhat * gain + shift).astype(BF)
        n_buf[half:, :] = jnp.zeros((rows - half, D), BF)
        nT_ref[:, part * rows : (part + 1) * rows] = n_buf[...].T
    attention_forward(half, start_ref, end_ref, empty_ref, nT_ref, pack, *rest)
    ff_pack(0, w1_ref, w2_ref, b1_ref, ff_ref)


def far_kernel(half, start_ref, end_ref, empty_ref, nT_ref, pack, w1_ref, w2_ref, b1_ref, ff_ref, *rest):
    attention_forward(half, start_ref, end_ref, empty_ref, nT_ref, pack, *rest)
    ff_pack(CHUNK, w1_ref, w2_ref, b1_ref, ff_ref)


def near_kernel(half, start_ref, end_ref, empty_ref, nT_ref, pack, cot_ref, pad_ref, *rest):
    attention_forward(half, start_ref, end_ref, empty_ref, nT_ref, pack, *rest)
    pad_ref[half:, :] = jnp.zeros((pad_ref.shape[0] - half, D), BF)
    pad_ref[:half, :] = cot_ref[...]


def out_kernel(x_ref, m0, m1, m2, m3, pa0, pa1, pa2, pa3, small_ref, hidden_ref, n2_ref, n2T_ref):
    local = m0.shape[0]
    mixed = jnp.concatenate([m[...].astype(BF) for m in (m0, m1, m2, m3)], axis=0)
    weight = jnp.concatenate([p[:D, 3 * local :] for p in (pa0, pa1, pa2, pa3)], axis=1)
    hidden = dot(mixed, weight, TT) + small_ref[2:3, :] + x_ref[...].astype(F32)
    hidden_ref[...] = hidden
    xhat, _ = norm_terms(hidden)
    n2 = (xhat * small_ref[3:4, :] + small_ref[4:5, :]).astype(BF)
    n2_ref[...] = n2
    n2T_ref[...] = n2.T


def phi_terms(inner):
    bell = jnp.exp(inner * inner * -0.5)
    x = jnp.abs(inner) * 0.7071067811865476
    t = 1.0 / (1.0 + 0.3275911 * x)
    poly = t * (0.254829592 + t * (-0.284496736 + t * (1.421413741 + t * (-1.453152027 + t * 1.061405429))))
    tail = 0.5 * poly * bell
    return jnp.where(inner >= 0, 1.0 - tail, tail), bell * 0.3989422804014327


def ff_slots(n2, n2T, cot, packs, back_ref, grad_refs, act_refs, bias_ref, act_buf, gi_buf):
    parts = 3
    piece = n2.shape[0] // parts
    units = [(s, r) for s in range(len(packs)) for r in range(parts)]

    def enter(s, r):
        p = packs[s]
        at = slice(r * piece, (r + 1) * piece)
        w2 = jnp.concatenate([p[D : D + CHUNK, :], p[D + CHUNK : 2 * D, :]], axis=1)
        return dot(n2[at], p[:D, :], NN) + p[2 * D : 2 * D + 1, :].astype(F32), dot(cot[at], w2, NT)

    ahead = enter(*units[0])
    for i, (s, r) in enumerate(units):
        inner, grad = ahead
        if i + 1 < len(units):
            ahead = enter(*units[i + 1])
        at = slice(r * piece, (r + 1) * piece)
        lanes = slice(s * CHUNK, (s + 1) * CHUNK)
        cdf, density = phi_terms(inner)
        act = (inner * cdf).astype(BF)
        act_buf[at, lanes] = act
        act_refs[s][at, :] = act
        gi_buf[at, lanes] = (grad * (cdf + inner * density)).astype(BF)
    w1 = jnp.concatenate([p[:D, :] for p in packs], axis=1)
    back = dot(gi_buf[...], w1, NT)
    back_ref[...] = back
    first = dot(n2T, gi_buf[...], NN).astype(BF)
    second = dot(act_buf[...], cot, TN).astype(BF)
    sums = dot(jnp.ones((EXTRA, n2.shape[0]), BF), gi_buf[...], NN)
    for s, ref in enumerate(grad_refs):
        at = slice(s * CHUNK, (s + 1) * CHUNK)
        ref[:D, :] = first[:, at]
        ref[D : D + CHUNK, :] = second[at, :CHUNK]
        ref[D + CHUNK : 2 * D, :] = second[at, CHUNK:]
        bias_ref[s : s + 1, :] = sums[:1, at]


def ff_kernel(n2_ref, n2T_ref, cot_ref, p0, p1, back_in, back_ref, g0, g1, act0, act1, bias_ref, act_buf, gi_buf):
    ff_slots(n2_ref[...], n2T_ref[...], cot_ref[...], (p0, p1), back_ref, (g0, g1), (act0, act1), bias_ref, act_buf, gi_buf)
    back_ref[...] += back_in[...]


def ff_first_kernel(n2_ref, n2T_ref, cot_ref, p0, c0, c1, c2, c3, back_ref, g0, d0, d1, d2, d3, act0, act1, bias_ref, act_buf, gi_buf):
    ff_slots(n2_ref[...], n2T_ref[...], cot_ref[...], (p0, Rows(c0, c1, c2, c3)), back_ref, (g0, Rows(d0, d1, d2, d3)), (act0, act1),
             bias_ref, act_buf, gi_buf)


def turn_kernel(n2_ref, n2T_ref, cot_ref, p0, p1, p2, p3, back_in, hidden_ref, m0, m1, m2, m3, pa0, pa1, pa2, pa3, small_in,
                gh_ref, dT0, dT1, dT2, dT3, g0, g1, g2, g3, o0, o2, o_send, act0, act1, act2, act3, bias_ref, small_ref,
                act_buf, gi_buf, back_buf):
    local = m0.shape[0]
    ff_slots(n2_ref[...], n2T_ref[...], cot_ref[...], (p0, p1, p2, p3), back_buf, (g0, g1, g2, g3), (act0, act1, act2, act3), bias_ref,
             act_buf, gi_buf)
    cot_f = cot_ref[...].astype(F32)
    back = back_buf[...] + back_in[...]
    xhat, scale = norm_terms(hidden_ref[...])
    grad_hidden = cot_f + norm_back(back, small_in[3:4, :], xhat, scale)
    gh_ref[...] = grad_hidden
    small_ref[0:1, :] = jnp.sum(grad_hidden, axis=0, keepdims=True)
    small_ref[1:2, :] = jnp.sum(back * xhat, axis=0, keepdims=True)
    small_ref[2:3, :] = jnp.sum(back, axis=0, keepdims=True)
    small_ref[3:4, :] = jnp.sum(cot_f, axis=0, keepdims=True)
    low = grad_hidden.astype(BF)
    weight = jnp.concatenate([p[:D, 3 * local :] for p in (pa0, pa1, pa2, pa3)], axis=1)
    grads_T = dot(weight, low, TT).astype(BF)
    for s, ref in enumerate((dT0, dT1, dT2, dT3)):
        ref[...] = grads_T[s * local : (s + 1) * local]
    mixed = jnp.concatenate([m[...].astype(BF) for m in (m0, m1, m2, m3)], axis=0)
    grad = dot(mixed, low, NN).astype(BF)
    for s, (ref, first) in enumerate(((o0, 0), (o_send, 0), (o2, 0), (o_send, 2 * local))):
        for part in range(2):
            at = first + part * local
            ref[at : at + local, :] = grad[s * local : (s + 1) * local, part * CHUNK : (part + 1) * CHUNK]


def attention_backward(e_ref, dT_ref, inv_ref, mixed_ref, vT_ref, qT_ref, kT_ref, nT_ref, dq_ref, dk_ref, dv_ref, grad_ref, bias_ref,
                       ds_buf):
    rows = qT_ref.shape[1]
    keys = kT_ref.shape[1]
    local = qT_ref.shape[0]
    heads = local // HEAD
    blocks = [(h, c) for h in range(heads) for c in range(rows // CHUNK)]
    which = lax.broadcasted_iota(jnp.int32, (EXTRA, CHUNK), 0)
    ones2 = (lax.broadcasted_iota(jnp.int32, (EXTRA, CHUNK), 0) < 2).astype(F32).astype(BF)
    lows = {}

    def enter(i):
        h, c = blocks[i]
        here = slice(h * HEAD, (h + 1) * HEAD)
        columns = slice(c * CHUNK, (c + 1) * CHUNK)
        low = (dT_ref[here, columns].astype(F32) * inv_ref[h : h + 1, columns]).astype(BF)
        delta = jnp.sum(low.astype(F32) * mixed_ref[here, columns], axis=0, keepdims=True)
        high = (-delta).astype(BF).astype(F32)
        extra = jnp.where(which == 0, high, jnp.where(which == 1, -delta - high, 0.0)).astype(BF)
        more = jnp.concatenate([low, extra], axis=0)
        lows[i] = low
        for k in range(keys // CHUNK):
            span = slice(k * CHUNK, (k + 1) * CHUNK)
            v = jnp.concatenate([vT_ref[here, span], ones2], axis=0)
            ds_buf[i % 2, span, :] = (e_ref[h, c, span, :].astype(F32) * dot(v, more, TN)).astype(BF)

    dv = None
    dk = None
    enter(0)
    for i, (h, c) in enumerate(blocks):
        if i + 1 < len(blocks):
            enter(i + 1)
        here = slice(h * HEAD, (h + 1) * HEAD)
        columns = slice(c * CHUNK, (c + 1) * CHUNK)
        part = dot(lows[i], e_ref[h, c], NT)
        dv = part if c == 0 else dv + part
        dq_ref[here, columns] = (dot(kT_ref[here, :], ds_buf[i % 2], NN) * HEAD**-0.5).astype(BF)
        part = dot(qT_ref[here, columns], ds_buf[i % 2], NT)
        dk = part if c == 0 else dk + part
        if c == rows // CHUNK - 1:
            dv_ref[here, :] = dv.astype(BF)
            dk_ref[here, :] = dk.astype(BF)
    ones = jnp.ones((EXTRA, rows), BF)
    for index, (ref, count) in enumerate(((dq_ref, rows), (dk_ref, keys), (dv_ref, keys))):
        columns = slice(index * local, (index + 1) * local)
        grad_ref[:, columns] = dot(nT_ref[:, :count], ref[...], NT).astype(BF)
        sums = sum(dot(ones, ref[:, i * rows : (i + 1) * rows], NT) for i in range(count // rows))
        bias_ref[0:1, columns] = sums[:1]


def first_kernel(half, x_ref, xs_ref, pa0, pa1, pa2, pa3, *rest):
    sources = rest[:12]
    small_two, b0, b1, b2, b3, f00, f01, f1, own_ref, sib_ref, small_ref = rest[12:]
    local = pa0.shape[1] // TENSOR
    rows = own_ref.shape[0]
    device = lax.axis_index("tensor")
    small_ref[...] = jnp.zeros(small_ref.shape, F32)
    gain_sum = 0.0
    shift_sum = 0.0
    for part, ref in enumerate((x_ref, xs_ref)):
        columns = slice(part * rows, (part + 1) * rows)
        total = None
        for slot, p in enumerate((pa0, pa1, pa2, pa3)):
            for index in range(part, 3):
                term = dot(sources[slot * 3 + index][:, columns], p[:D, index * local : (index + 1) * local], TT)
                total = term if total is None else total + term
        if part == 0:
            own_ref[...] = total
        else:
            sib_ref[...] = total.astype(BF)
        xhat, _ = norm_terms(ref[:half, :].astype(F32))
        gain_sum = gain_sum + jnp.sum(total[:half] * xhat, axis=0, keepdims=True)
        shift_sum = shift_sum + jnp.sum(total, axis=0, keepdims=True)
    small_ref[0:4, :] = small_two[...]
    small_ref[4:5, :] = gain_sum
    small_ref[5:6, :] = shift_sum
    for slot, b in enumerate((b0, b1, b2, b3)):
        owner = jnp.bitwise_xor(device, slot)
        small_ref[pl.ds(8 + owner, 1), :] = jnp.concatenate(
            [(f00, f01)[slot // 2][slot % 2 : slot % 2 + 1, :], f1[slot : slot + 1, :]], axis=1
        )
        small_ref[pl.ds(12 + owner, 1), : 3 * local] = b[...]


def branch_kernel(hidden_ref, small_ref, *rest):
    *refs, out_ref = rest
    acts, packs = refs[: 2 * TENSOR], refs[2 * TENSOR :]
    packs = packs[:3] + [Rows(*packs[3:7])] + packs[7:]
    act = jnp.concatenate([a[...] for a in acts], axis=1)
    weight = jnp.concatenate(
        [jnp.concatenate([p[D : D + CHUNK, :], p[D + CHUNK : 2 * D, :]], axis=1) for p in packs], axis=0
    )
    total = hidden_ref[...] + dot(act, weight, NN) + small_ref[5:6, :]
    out_ref[...] = total[: out_ref.shape[0]].astype(BF)


def last_kernel(x_ref, own_ref, got_ref, gh_ref, small_ref, out_ref):
    half = out_ref.shape[0]
    grad = own_ref[:half, :] + got_ref[:half, :].astype(F32)
    xhat, scale = norm_terms(x_ref[:half, :].astype(F32))
    out_ref[...] = gh_ref[:half, :] + norm_back(grad, small_ref[0:1, :], xhat, scale)


def place_of(bit):
    return lax.rem(lax.div(lax.axis_index("dp"), bit), 2)


def merge(kept, got, buf, bit=1):
    rows = kept.shape[0]
    upper = place_of(bit)
    buf[pl.ds(pl.multiple_of(upper * rows, rows), rows), :] = kept[...].astype(F32)
    buf[pl.ds(pl.multiple_of((1 - upper) * rows, rows), rows), :] = got[...].astype(F32)


def finish_ff_kernel(first, kept, got, expand_ref, reduce_ref, out_ref, second):
    local = out_ref.shape[0]
    merge(kept, got, second)
    for index, ref in enumerate((first, second)):
        lanes = slice(index * CHUNK, (index + 1) * CHUNK)
        expand_ref[:, lanes] = ref[:D, :].astype(F32)
        for part in range(2):
            rows = slice(D + part * CHUNK, D + (part + 1) * CHUNK)
            reduce_ref[lanes, part * CHUNK : (part + 1) * CHUNK] = ref[rows, :].astype(F32)
    for part in range(2):
        rows = slice(2 * D + part * local, 2 * D + (part + 1) * local)
        out_ref[:, part * CHUNK : (part + 1) * CHUNK] = second[rows, :]


def finish_qkv_kernel(kept, got, sums_ref, more_ref, q_ref, k_ref, v_ref, bias_q, bias_v, bias_ff, s0, s1, s2, s3, s4, s5, buf, sums):
    merge(kept, got, buf)
    local = q_ref.shape[1]
    for index, ref in enumerate((q_ref, k_ref, v_ref)):
        ref[...] = buf[:, index * local : (index + 1) * local]
        ref.flush()
    sums[...] = sums_ref[...] + more_ref[...]
    device = lax.axis_index("tensor")
    for index, ref in enumerate((s0, s1, s2, s3, s4, s5)):
        ref[...] = sums[index : index + 1, :].reshape(D)
    bias_ff[...] = sums[pl.ds(8 + device, 1), :].reshape(D)
    both = sums[pl.ds(12 + device, 1), :]
    bias_q[...] = both[:, :local].reshape(local)
    bias_v[...] = both[:, 2 * local : 3 * local].reshape(local)


class Chain:
    def __init__(self, along, size, halvings, pieces):
        bits = [1 << i for i in range(size.bit_length() - 1)]
        halvings = min(halvings, len(bits))
        self.along = along
        self.plan = [("half", b) for b in bits[:halvings]] + [("full", b) for b in bits[halvings:]]
        self.plan += [("back", b) for b in reversed(bits[:halvings])]
        self.at = -1
        self.pieces = pieces

    def left(self):
        return len(self.plan) - 1 - self.at

    def last(self):
        return tuple(self.pieces[0])

    def due(self):
        kind, bit = self.plan[self.at + 1]
        if kind == "half":
            return "halves", self.pieces, bit
        if self.at >= 0 and self.plan[self.at][0] == "back":
            return ("merge",) + tuple(self.pieces[0]) + (self.plan[self.at][1],)
        return "sum", self.pieces

    def taken(self, *results):
        self.at += 1
        send, keep = results if len(results) == 2 else results * 2
        self.pieces = [(keep, self.along(send, self.plan[self.at][1]))]


def swap(value, axis, size, bit):
    return lax.ppermute(value, axis, [(i, i ^ bit) for i in range(size)])


def on_device(dp, frames, query_weight, query_bias, key_weight, value_weight, value_bias, out_weight, out_bias, first_gain, first_shift,
              expand_weight, expand_bias, reduce_weight, reduce_bias, second_gain, second_shift, span_start, span_end, empty_flag, cotangent):
    half = frames.shape[0]
    rows = -(-half // CHUNK) * CHUNK
    keys = 2 * rows
    local = query_weight.shape[1]
    heads = local // HEAD
    blocks = rows // CHUNK
    line = Line()

    def across(v, bit):
        return swap(v, "tensor", TENSOR, bit)

    def along(v, bit):
        return swap(v, "dp", dp, bit)

    xs = across(frames, 1)
    pa0, small = line.run(
        pack_kernel, (shaped(D + EXTRA, 4 * local), shaped(8, D, dtype=F32)), "f" * 12,
        (query_weight, key_weight, value_weight, out_weight, query_bias, value_bias,
         first_gain, first_shift, out_bias, second_gain, second_shift, reduce_bias), us=2,
    )
    pa2 = across(pa0, 2)
    pa1 = across(pa0, 1)

    forward_outs = (
        (shaped(heads, blocks, keys, CHUNK), "V"), shaped(local, rows), shaped(local, keys), shaped(local, keys),
        shaped(local, rows, dtype=F32), shaped(heads, rows, dtype=F32),
    )
    forward_scratch = (
        pltpu.VMEM((2, keys, CHUNK), F32),
    )
    spans = (span_start, span_end, empty_flag)
    ff_weights = (expand_weight, reduce_weight, expand_bias)
    ff0_shape = shaped(2 * D + 3 * EXTRA, CHUNK)
    ff1_shape = shaped(2 * D + 4 * EXTRA, CHUNK)
    normed, ff0, x, *s0 = line.run(
        functools.partial(start_kernel, half), (shaped(D, keys), ff0_shape, shaped(rows, D)) + forward_outs, "sssfvvvfff",
        spans + (frames, xs, small, pa0) + ff_weights, forward_scratch + (pltpu.VMEM((rows, D), BF),), us=8,
    )
    ff0_far = across(ff0, 2)
    ff0_near = across(ff0, 1)
    cot, *s1 = line.run(
        functools.partial(near_kernel, half), (shaped(rows, D),) + forward_outs, "sssvvf",
        spans + (normed, pa1, cotangent), forward_scratch, us=7,
    )
    pa2 = line.touch(pa2)
    pa3 = across(pa2, 1)
    ff1, *s2 = line.run(
        functools.partial(far_kernel, half), (ff1_shape,) + forward_outs, "sssvvfff",
        spans + (normed, pa2) + ff_weights, forward_scratch, us=7,
    )
    ff1_far = across(ff1, 2)
    s3 = line.run(
        functools.partial(attention_forward, half), forward_outs, "sssvv",
        spans + (normed, pa3), forward_scratch, us=7,
    )
    slots = (s0, s1, s2, s3)
    mixed = tuple(s[4] for s in slots)
    packs = (pa0, pa1, pa2, pa3)
    cuts = [(i * CHUNK, CHUNK) for i in range(3)] + [(3 * CHUNK, ff0_shape.shape[0] - 3 * CHUNK)]
    ff0_cross = [across(v, 1) for v in line.tick(*(("sum", [((ff0_far,) + cut,)]) for cut in cuts))]
    whole = shaped(rows, D, dtype=F32)
    hidden, n2, n2T = line.run(
        out_kernel, (whole, shaped(rows, D), shaped(D, rows)), "v" * 10,
        (x,) + mixed + packs + (small,), us=8,
    )
    ff1_near = across(ff1, 1)
    ff_scratch = (pltpu.VMEM((rows, TENSOR * CHUNK), BF), pltpu.VMEM((rows, TENSOR * CHUNK), BF))
    bias_shape = shaped(TENSOR, CHUNK, dtype=F32)
    ff_grads = (shaped(2 * D, CHUNK),) * TENSOR
    ff_acts = (shaped(rows, CHUNK),) * TENSOR
    two = (whole,) + ff_grads[:2] + ff_acts[:2] + (shaped(2, CHUNK, dtype=F32),)
    half_scratch = (pltpu.VMEM((rows, 2 * CHUNK), BF), pltpu.VMEM((rows, 2 * CHUNK), BF))
    back, a2, *a3, act2, act3, bias_far = line.run(
        ff_first_kernel, two[:2] + (shaped(CHUNK, CHUNK),) * 4 + two[3:], "v" * 8, (n2, n2T, cot, ff0_far, *ff0_cross), half_scratch,
        us=4, vmem=10,
    )
    got_a3 = [across(v, 1) for v in a3]
    back, a0, a1, act0, act1, bias_near = line.run(
        ff_kernel, two, "v" * 6, (n2, n2T, cot, ff0, ff0_near, back), half_scratch, us=4, vmem=10,
    )
    acts_a, bias_a = (act0, act1, act2, act3), (bias_near, bias_far)
    got_a1 = across(a1, 1)
    spare = jnp.zeros((EXTRA, CHUNK), BF)
    (far_a,) = line.tick(("sum", [((a2, i * CHUNK, CHUNK), v) for i, v in enumerate(got_a3)] + [(spare,)]))
    y_a = across(far_a, 2)
    ff1_far = line.touch(ff1_far)
    ff1_cross = across(ff1_far, 1)
    size_b = 2 * D + 2 * local
    grad_hidden, *rest = line.run(
        turn_kernel,
        ((whole, "f"),) + (shaped(local, rows),) * TENSOR + ff_grads
        + (shaped(2 * local, CHUNK), shaped(2 * local, CHUNK), shaped(4 * local, CHUNK)) + ff_acts + (bias_shape, shaped(4, D, dtype=F32)),
        "v" * 18,
        (n2, n2T, cot, ff1, ff1_near, ff1_far, ff1_cross, back, hidden) + mixed + packs + (small,),
        ff_scratch + (pltpu.VMEM((rows, D), F32),), us=12, vmem=14,
    )
    dT, (f0, f1, f2, f3, o0, o2, o_send) = rest[:TENSOR], rest[TENSOR : TENSOR + 7]
    acts_b, (bias_b, small_two) = rest[TENSOR + 7 : 2 * TENSOR + 7], rest[2 * TENSOR + 7 :]
    got_f1 = across(f1, 1)
    got_f3 = across(f3, 1)
    got_o = across(o_send, 1)

    backward_outs = (
        shaped(local, rows), shaped(local, keys), shaped(local, keys), shaped(D, 3 * local), shaped(1, 3 * local, dtype=F32),
    )

    def backward(slot):
        e, q, k, v, m, inv = slots[slot]
        return line.run(
            attention_backward, backward_outs, "V" + "v" * 7,
            (e, dT[slot], inv, m, v, q, k, normed), (pltpu.VMEM((2, keys, CHUNK), BF),), us=8, vmem=8,
        )

    def chain(halvings, pieces):
        return Chain(along, dp, halvings, pieces)

    *d3, g3, b3 = backward(3)
    chain_a = chain(2, [(a0, got_a1, (y_a, 0, 2 * D))])
    pair = 2 * local
    far_b, send_3, *halves = line.tick(
        ("sum", [(f2, got_f3), (o2, (got_o, pair, pair))]), ("sum", [(g3,)]), chain_a.due()
    )
    y_b = across(far_b, 2)
    got_3 = across(send_3, 1)
    chain_a.taken(*halves)
    *d2, g2, b2 = backward(2)
    spare = jnp.zeros((EXTRA, 3 * local), BF)
    far_q, *halves = line.tick(("sum", [(g2, got_3), (spare,)]), chain_a.due())
    y_q = across(far_q, 2)
    chain_a.taken(*halves)
    *d1, g1, b1 = backward(1)
    chain_b = chain(2, [(f0, got_f1, (y_b, 0, 2 * D)), (o0, (got_o, 0, pair), (y_b, 2 * D, pair))])
    send_1, whole_a, *halves = line.tick(("sum", [(g1,)]), chain_a.due(), chain_b.due())
    got_1 = across(send_1, 1)
    chain_a.taken(whole_a)
    chain_b.taken(*halves)
    *d0, g0, b0 = backward(0)
    chain_q = chain(1, [(g0, got_1, (y_q, 0, D))])
    send_q, keep_q, send_b, keep_b, whole_a = line.tick(chain_q.due(), chain_b.due(), chain_a.due())
    chain_q.taken(send_q, keep_q)
    chain_b.taken(send_b, keep_b)
    chain_a.taken(whole_a)
    own, sib, sums = line.run(
        functools.partial(first_kernel, half), (whole, shaped(rows, D), shaped(16, D, dtype=F32)), "v" * 26,
        (x, xs) + packs + (*d0, *d1, *d2, *d3, small_two, b0, b1, b2, b3) + bias_a + (bias_b,), us=6,
    )
    (sums,) = line.tick(("sum", [(sums,)]))
    pending = across(sums, 1)
    part_q, part_b, part_a, sums, sib = line.tick(
        chain_q.due(), chain_b.due(), chain_a.due(), ("sum", [(sums, pending)]), ("sum", [(sib,)])
    )
    chain_q.taken(part_q)
    chain_b.taken(part_b)
    chain_a.taken(part_a)
    pending = across(sums, 2)
    got = across(sib, 1)
    (grad_frames,) = line.run(
        last_kernel, ((shaped(half, D, dtype=F32), "f"),), "vvvfv", (x, own, got, grad_hidden, small), us=4
    )
    bits = [1 << i for i in range(dp.bit_length() - 1)]

    def step(*chains, more=()):
        nonlocal sums, pending
        chains = [c for c in chains if c.left()]
        with_sums = bool(bits)
        jobs = [c.due() for c in chains] + [("sum", [(sums, pending)])] * with_sums + list(more)
        if not jobs:
            return ()
        made = list(line.tick(*jobs))
        for c in chains:
            c.taken(made.pop(0))
        if with_sums:
            sums = made.pop(0)
            pending = along(sums, bits.pop(0))
        return made

    step(chain_q, chain_b, chain_a)
    (output,) = line.run(
        branch_kernel, ((shaped(half, D), "f"),), "v" * 21,
        (hidden, small) + tuple(acts_a) + tuple(acts_b) + (ff0, ff0_near, ff0_far, *ff0_cross, ff1, ff1_near, ff1_far, ff1_cross), us=3,
    )
    while chain_a.left() or chain_b.left() > 1:
        step(chain_q, chain_b, chain_a)
    (whole_a,) = step(chain_b, more=(("merge",) + chain_a.last() + (1,),))
    while bits or chain_q.left():
        step(chain_q)
    grad_expand, grad_reduce, grad_out = line.run(
        finish_ff_kernel, tuple((shaped(*o, dtype=F32), "f") for o in ((D, 2 * CHUNK), (2 * CHUNK, D), (local, D))),
        "vvv", (whole_a,) + chain_b.last(), (pltpu.VMEM((size_b, CHUNK), F32),), us=2,
    )
    vector = (shaped(D, dtype=F32), "f")
    short = (shaped(local, dtype=F32), "f")
    grad_q, grad_k, grad_v, bias_q, bias_v, bias_ff, *globals_ = line.run(
        finish_qkv_kernel, ((shaped(D, local, dtype=F32), "f"),) * 3 + (short, short, vector) + (vector,) * 6, "vvvv",
        chain_q.last() + (sums, pending), (pltpu.VMEM((D, 3 * local), F32), pltpu.VMEM(sums.shape, F32)), us=1,
    )
    return (
        output, grad_frames, grad_q, bias_q, grad_k, grad_v, bias_v, grad_out, globals_[0], globals_[4], globals_[5],
        grad_expand, bias_ff, grad_reduce, globals_[3], globals_[1], globals_[2],
    )


def solution(mesh):
    dp = mesh.shape["dp"]
    assert mesh.shape["tensor"] == TENSOR and dp & (dp - 1) == 0
    split = P(("dp", "tensor"), None)
    column = P(None, "tensor")
    return jax.shard_map(
        functools.partial(on_device, dp),
        mesh=mesh,
        in_specs=(
            split, column, P("tensor"), column, column, P("tensor"), P("tensor", None), P(), P(), P(),
            column, P("tensor"), P("tensor", None), P(), P(), P(), P("dp"), P("dp"), P("dp"), split,
        ),
        out_specs=(
            split, split, column, P("tensor"), column, column, P("tensor"), P("tensor", None), P(), P(), P(),
            column, P("tensor"), P("tensor", None), P(), P(), P(),
        ),
        check_vma=False,
    )
```

```python
import functools

import jax
import jax.numpy as jnp
from jax import lax
from jax.experimental import pallas as pl
from jax.experimental.pallas import tpu as pltpu
from jax.sharding import PartitionSpec as P

BF = jnp.bfloat16
F32 = jnp.float32
D = 512
HEADS = 8
HEAD = D // HEADS
EPS = 1e-05
TENSOR = 4
CHUNK = 256
EXTRA = 16
LANES = 128
NN = (((1,), (0,)), ((), ()))
NT = (((1,), (1,)), ((), ()))
TN = (((0,), (0,)), ((), ()))
TT = (((0,), (1,)), ((), ()))
VMEM = pl.BlockSpec(memory_space=pltpu.VMEM)
SMEM = pl.BlockSpec(memory_space=pltpu.SMEM)
ANY = pl.BlockSpec(memory_space=pl.ANY)


def dot(left, right, dims):
    return lax.dot_general(left, right, dims, preferred_element_type=F32)


class Fetched:
    def __init__(self, source, buffer, sem):
        self.buffer, self.shape, self.waited = buffer, buffer.shape, False
        self.copy = pltpu.make_async_copy(source, buffer, sem)
        self.copy.start()

    def __getitem__(self, index):
        if not self.waited:
            self.copy.wait()
            self.waited = True
        return self.buffer[index]


class Stored:
    def __init__(self, target, buffer, sem):
        self.buffer, self.shape, self.dtype, self.sent = buffer, buffer.shape, buffer.dtype, False
        self.copy = pltpu.make_async_copy(buffer, target, sem)

    def __getitem__(self, index):
        return self.buffer[index]

    def __setitem__(self, index, value):
        self.buffer[index] = value

    def flush(self):
        if not self.sent:
            self.copy.start()
            self.sent = True


HBM = pl.BlockSpec(memory_space=pltpu.HBM)
SPEC = {"f": HBM, "h": HBM, "s": HBM, "v": VMEM, "V": VMEM}
PINNED = {"f": pltpu.HBM, "h": pltpu.HBM, "s": pltpu.HBM, "V": pltpu.VMEM}


class Rows:
    def __init__(self, *refs):
        self.refs, self.at = refs, [0]
        for ref in refs:
            self.at.append(self.at[-1] + ref.shape[0])

    def spans(self, rows):
        first, last, _ = rows.indices(self.at[-1])
        for ref, low, high in zip(self.refs, self.at, self.at[1:]):
            if max(first, low) < min(last, high):
                yield ref, slice(max(first, low) - low, min(last, high) - low), slice(max(first, low) - first, min(last, high) - first)

    def __getitem__(self, index):
        parts = [ref[here, index[1]] for ref, here, _ in self.spans(index[0])]
        return parts[0] if len(parts) == 1 else jnp.concatenate(parts, axis=0)

    def __setitem__(self, index, value):
        for ref, here, there in self.spans(index[0]):
            ref[here, index[1]] = value[there]


class Line:
    def __init__(self):
        self.waits = ()

    def run(self, kernel, outs, ins, args, scratch=(), us=8, vmem=12):
        waits = self.waits
        outs = [o if isinstance(o, tuple) else (o, "v") for o in outs]
        kinds = list(ins)
        skip, last = len(kinds), len(outs)
        moved = [i for i, k in enumerate(kinds) if k in "fs"]
        built = [i for i, (_, k) in enumerate(outs) if k == "f"]
        space = {"f": pltpu.VMEM, "s": pltpu.SMEM}
        buffers = [space[kinds[i]](args[i].shape, args[i].dtype) for i in moved] + [pltpu.VMEM(outs[i][0].shape, outs[i][0].dtype) for i in built]

        def body(*refs):
            inputs = list(refs[:skip])
            rest = refs[skip + len(waits) :]
            results, zeros, rest = list(rest[:last]), rest[last], rest[last + 1 :]
            held, sems, rest = rest[: len(buffers)], rest[len(buffers)], rest[len(buffers) + 1 :]
            for n, i in enumerate(moved):
                inputs[i] = Fetched(inputs[i], held[n], sems.at[n])
            for n, i in enumerate(built, len(moved)):
                results[i] = Stored(results[i], held[n], sems.at[n])
            zeros[...] = jnp.zeros((8, 128), F32)
            kernel(*inputs, *results, *rest)
            for i in built:
                results[i].flush()
            for i in moved:
                if not inputs[i].waited:
                    inputs[i].copy.wait()
            for i in built:
                results[i].copy.wait()

        *got, zeros = pl.pallas_call(
            body,
            out_shape=tuple(PINNED[k](o.shape, o.dtype) if k in PINNED else o for o, k in outs) + (jax.ShapeDtypeStruct((8, 128), F32),),
            in_specs=[SPEC[k] for k in kinds] + [ANY] * len(waits),
            out_specs=[SPEC[k] for _, k in outs] + [VMEM],
            scratch_shapes=buffers + [pltpu.SemaphoreType.DMA((len(buffers) + 1,))] + list(scratch),
            compiler_params=pltpu.CompilerParams(vmem_limit_bytes=vmem * 2**20),
            cost_estimate=pl.CostEstimate(flops=10**6, bytes_accessed=2**10, transcendentals=0),
        )(*(pltpu.with_memory_space_constraint(a, PINNED[k]) if k in PINNED else a for a, k in zip(args, kinds)), *waits)
        self.waits = (zeros,)
        return got

    def touch(self, value):
        waits = self.waits
        got = (
            pl.pallas_call(
                lambda given, *rest: None,
                out_shape=jax.ShapeDtypeStruct(value.shape, value.dtype),
                in_specs=[ANY] * (1 + len(waits)),
                out_specs=ANY,
                input_output_aliases={0: 0},
                compiler_params=pltpu.CompilerParams(vmem_limit_bytes=2**20),
                cost_estimate=pl.CostEstimate(flops=10**6, bytes_accessed=1024, transcendentals=0),
            )(value, *waits)
        )
        self.waits = self.waits + (got,)
        return got

    def tick(self, *jobs):
        args, outs, scratch, plans = [], [], [], []

        def place(part):
            array, first, rows = part if isinstance(part, tuple) else (part, 0, part.shape[0])
            args.append(array)
            return len(args) - 1, first, rows

        for kind, *rest in jobs:
            pieces = [[place(part) for part in piece] for piece in ([[p] for p in rest[:2]] if kind == "merge" else rest[0])]
            rows = sum(piece[0][2] for piece in pieces)
            like = args[pieces[0][0][0]]
            columns = like.shape[1:]
            plans.append((kind, pieces, len(outs), len(scratch), rest[-1]))
            if kind == "halves":
                outs += [shaped(rows // 2, *columns)] * 2
            else:
                outs.append(jax.ShapeDtypeStruct((rows, *columns), like.dtype))
            if kind != "sum":
                scratch.append(pltpu.VMEM((rows, *columns), F32))

        def body(*refs):
            ins, results, buffers = refs[: len(args)], refs[len(args) : len(args) + len(outs)], refs[len(args) + len(outs) :]
            for kind, pieces, out, held, bit in plans:
                if kind == "merge":
                    kept, got = (ins[piece[0][0]] for piece in pieces)
                    merge(kept, got, buffers[held], bit)
                    results[out][...] = buffers[held][...].astype(results[out].dtype)
                    continue
                target = buffers[held] if kind == "halves" else results[out]
                at = 0
                for piece in pieces:
                    count = piece[0][2]
                    total = sum(ins[i][first : first + count].astype(F32) for i, first, _ in piece)
                    target[at : at + count] = total.astype(target.dtype)
                    at += count
                if kind == "halves":
                    half = at // 2
                    upper = place_of(bit)
                    results[out][...] = target[pl.ds(pl.multiple_of((1 - upper) * half, half), half), :].astype(BF)
                    results[out + 1][...] = target[pl.ds(pl.multiple_of(upper * half, half), half), :].astype(BF)

        return self.run(body, outs, "v" * len(args), args, scratch, us=1, vmem=6)


def shaped(*shape, dtype=BF):
    return jax.ShapeDtypeStruct(shape, dtype)


def norm_terms(rows_in):
    center = jnp.mean(rows_in, axis=-1, keepdims=True)
    centered = rows_in - center
    spread = jnp.mean(centered * centered, axis=-1, keepdims=True)
    scale = lax.rsqrt(spread + EPS)
    return centered * scale, scale


def norm_back(grad, gain, xhat, scale):
    e = grad * gain
    mean_e = jnp.mean(e, axis=-1, keepdims=True)
    mean_ex = jnp.mean(e * xhat, axis=-1, keepdims=True)
    return scale * (e - mean_e - xhat * mean_ex)


def valid_row(start_ref, end_ref, empty_ref, rows, half):
    lane = lax.broadcasted_iota(jnp.int32, (1, 2 * rows), 1)
    second = lane >= rows
    local = jnp.where(second, lane - rows, lane)
    device = lax.axis_index("tensor")
    clip = device // 2
    core = device % 2
    position = local + half * jnp.where(second, 1 - core, core)
    inside = (position >= start_ref[clip]) & (position < end_ref[clip])
    return (local < half) & jnp.logical_not(inside) & (empty_ref[clip] == 0)


def attention_forward(half, start_ref, end_ref, empty_ref, nT_ref, pack, e_ref, qT_ref, kT_ref, vT_ref, mixed_ref, inv_ref, s_buf,
                      prepare=None):
    rows = qT_ref.shape[1]
    keys = kT_ref.shape[1]
    local = qT_ref.shape[0]
    heads = local // HEAD
    first_row = lax.broadcasted_iota(jnp.int32, (EXTRA, keys), 0) == 0
    ones16 = first_row.astype(F32).astype(BF)

    def project(first, last, columns):
        product = dot(pack[:D, first * local : last * local], nT_ref[:D, columns], TN)
        bias = dot(pack[D:, first * local : last * local], ones16[:, :LANES], TN)
        return (product + jnp.concatenate([bias] * (rows // LANES), axis=1)).astype(BF)

    for part in (1, 0):
        columns = slice(part * rows, (part + 1) * rows)
        if prepare is not None:
            prepare(part)
        both = project(1, 3, columns)
        kT_ref[:, columns] = both[:local]
        vT_ref[:, columns] = both[local:]
    qT_ref[...] = (project(0, 1, slice(0, rows)).astype(F32) * HEAD**-0.5).astype(BF)

    valid = valid_row(start_ref, end_ref, empty_ref, rows, half)
    some = jnp.max(valid.astype(F32), axis=1, keepdims=True)
    mask = jnp.where(first_row, jnp.where(valid, 0.0, -1e30), 0.0).astype(BF)

    blocks = [(h, c) for h in range(heads) for c in range(rows // CHUNK)]
    tops = {}

    def score(i):
        h, c = blocks[i]
        q = jnp.concatenate([qT_ref[h * HEAD : (h + 1) * HEAD, c * CHUNK : (c + 1) * CHUNK], ones16[:, :CHUNK]], axis=0)
        top = None
        for k in range(keys // CHUNK):
            span = slice(k * CHUNK, (k + 1) * CHUNK)
            s = dot(jnp.concatenate([kT_ref[h * HEAD : (h + 1) * HEAD, span], mask[:, span]], axis=0), q, TN)
            s_buf[i % 2, span, :] = s
            part = jnp.max(s.reshape(CHUNK // 8, 8, CHUNK), axis=0)
            top = part if top is None else jnp.maximum(top, part)
        tops[i] = jnp.max(top, axis=0, keepdims=True)

    score(0)
    for i, (h, c) in enumerate(blocks):
        if i + 1 < len(blocks):
            score(i + 1)
        columns = slice(c * CHUNK, (c + 1) * CHUNK)
        for k in range(keys // CHUNK):
            span = slice(k * CHUNK, (k + 1) * CHUNK)
            e_ref[h, c, span, :] = jnp.exp(s_buf[i % 2, span, :] - tops[i]).astype(BF)
        value = jnp.concatenate([vT_ref[h * HEAD : (h + 1) * HEAD, :], jnp.ones((EXTRA, keys), BF)], axis=0)
        o = dot(value, e_ref[h, c], NN)
        inv = some / o[HEAD : HEAD + 1, :]
        mixed_ref[h * HEAD : (h + 1) * HEAD, columns] = o[:HEAD] * inv
        inv_ref[h : h + 1, columns] = inv


def ff_pack(first, w1_ref, w2_ref, b1_ref, out_ref):
    out_ref[:D, :] = w1_ref[:, first : first + CHUNK]
    for part in range(2):
        out_ref[D + part * CHUNK : D + (part + 1) * CHUNK, :] = w2_ref[first : first + CHUNK, part * CHUNK : (part + 1) * CHUNK]
    out_ref[2 * D :, :] = jnp.broadcast_to(b1_ref[...].reshape(1, -1)[:, first : first + CHUNK], (out_ref.shape[0] - 2 * D, CHUNK))


def pack_kernel(wq, wk, wv, wo, bq, bv, g1, s1, ob, g2, s2, rb, pack_ref, small_ref):
    local = wq.shape[1]
    for index, ref in enumerate((wq, wk, wv)):
        pack_ref[:D, index * local : (index + 1) * local] = ref[...]
    pack_ref[:D, 3 * local :] = wo[...].T
    pack_ref[D:, :] = jnp.zeros((EXTRA, 4 * local), BF)
    pack_ref[D : D + 1, :local] = bq[...].reshape(1, local)
    pack_ref[D : D + 1, 2 * local : 3 * local] = bv[...].reshape(1, local)
    for index, ref in enumerate((g1, s1, ob, g2, s2, rb)):
        small_ref[index : index + 1, :] = ref[...].astype(F32).reshape(1, D)


def start_kernel(half, start_ref, end_ref, empty_ref, x_ref, xs_ref, small_ref, pack, w1_ref, w2_ref, b1_ref, nT_ref, ff_ref, pad_ref, *rest):
    *rest, n_buf = rest
    rows = n_buf.shape[1]
    gain = small_ref[0:1, :]
    shift = small_ref[1:2, :]
    nT_ref[D:, :] = (lax.broadcasted_iota(jnp.int32, (EXTRA, 2 * rows), 0) == 0).astype(F32).astype(BF)

    def prepare(part):
        xhat, _ = norm_terms((x_ref, xs_ref)[part][...].astype(F32))
        n_buf[part, :half, :] = (xhat * gain + shift).astype(BF)
        n_buf[part, half:, :] = jnp.zeros((rows - half, D), BF)
        nT_ref[:D, part * rows : (part + 1) * rows] = n_buf[part].T

    attention_forward(half, start_ref, end_ref, empty_ref, nT_ref, pack, *rest, prepare=prepare)
    ff_pack(0, w1_ref, w2_ref, b1_ref, ff_ref)
    pad_ref[half:, :] = jnp.zeros((rows - half, D), BF)
    pad_ref[:half, :] = x_ref[...]


def near_kernel(half, start_ref, end_ref, empty_ref, nT_ref, pack, cot_ref, w1_ref, w2_ref, b1_ref, pad_ref, ff_ref, *rest):
    attention_forward(half, start_ref, end_ref, empty_ref, nT_ref, pack, *rest)
    pad_ref[half:, :] = jnp.zeros((pad_ref.shape[0] - half, D), BF)
    pad_ref[:half, :] = cot_ref[...]
    ff_pack(CHUNK, w1_ref, w2_ref, b1_ref, ff_ref)


def out_kernel(x_ref, m0, m1, m2, m3, pa0, pa1, pa2, pa3, small_ref, hidden_ref, n2_ref, n2T_ref):
    local = m0.shape[0]
    mixed = jnp.concatenate([m[...].astype(BF) for m in (m0, m1, m2, m3)], axis=0)
    weight = jnp.concatenate([p[:D, 3 * local :] for p in (pa0, pa1, pa2, pa3)], axis=1)
    hidden = dot(mixed, weight, TT) + small_ref[2:3, :] + x_ref[...].astype(F32)
    hidden_ref[...] = hidden
    xhat, _ = norm_terms(hidden)
    n2 = (xhat * small_ref[3:4, :] + small_ref[4:5, :]).astype(BF)
    n2_ref[...] = n2
    n2T_ref[:D, :] = n2.T
    n2T_ref[D:, :] = (lax.broadcasted_iota(jnp.int32, (EXTRA, n2.shape[0]), 0) == 0).astype(F32).astype(BF)


def phi_terms(inner):
    bell = jnp.exp(inner * inner * -0.5)
    x = jnp.abs(inner) * 0.7071067811865476
    t = 1.0 / (1.0 + 0.3275911 * x)
    poly = t * (0.254829592 + t * (-0.284496736 + t * (1.421413741 + t * (-1.453152027 + t * 1.061405429))))
    tail = 0.5 * poly * bell
    return jnp.where(inner >= 0, 1.0 - tail, tail), bell * 0.3989422804014327


def ff_slots(n2, n2T, cot, packs, back_ref, grad_refs, act_refs, bias_ref, act_buf, gi_buf):
    parts = 3
    piece = n2.shape[0] // parts
    units = [(s, r) for s in range(len(packs)) for r in range(parts)]

    def enter(s, r):
        p = packs[s]
        at = slice(r * piece, (r + 1) * piece)
        w2 = jnp.concatenate([p[D : D + CHUNK, :], p[D + CHUNK : 2 * D, :]], axis=1)
        return dot(n2[at], p[:D, :], NN) + p[2 * D : 2 * D + 1, :].astype(F32), dot(cot[at], w2, NT)

    ahead = enter(*units[0])
    for i, (s, r) in enumerate(units):
        inner, grad = ahead
        if i + 1 < len(units):
            ahead = enter(*units[i + 1])
        at = slice(r * piece, (r + 1) * piece)
        lanes = slice(s * CHUNK, (s + 1) * CHUNK)
        cdf, density = phi_terms(inner)
        act = (inner * cdf).astype(BF)
        act_buf[at, lanes] = act
        act_refs[s][at, :] = act
        gi_buf[at, lanes] = (grad * (cdf + inner * density)).astype(BF)
    w1 = jnp.concatenate([p[:D, :] for p in packs], axis=1)
    back_ref[...] = dot(gi_buf[...], w1, NT)

    def weight_grads():
        first = dot(n2T, gi_buf[...], NN)
        second = dot(act_buf[...], cot, TN).astype(BF)
        for s, ref in enumerate(grad_refs):
            at = slice(s * CHUNK, (s + 1) * CHUNK)
            ref[:D, :] = first[:D, at].astype(BF)
            ref[D : D + CHUNK, :] = second[at, :CHUNK]
            ref[D + CHUNK : 2 * D, :] = second[at, CHUNK:]
            bias_ref[s : s + 1, :] = first[D : D + 1, at]

    return weight_grads


def ff_kernel(n2_ref, n2T_ref, cot_ref, p0, p1, back_in, back_ref, g0, g1, act0, act1, bias_ref, act_buf, gi_buf):
    ff_slots(n2_ref[...], n2T_ref[...], cot_ref[...], (p0, p1), back_ref, (g0, g1), (act0, act1), bias_ref, act_buf, gi_buf)()
    back_ref[...] += back_in[...]


def ff_first_kernel(n2_ref, n2T_ref, cot_ref, p0, c0, c1, back_ref, g0, d0, d1, act0, act1, bias_ref, act_buf, gi_buf):
    ff_slots(n2_ref[...], n2T_ref[...], cot_ref[...], (p0, Rows(c0, c1)), back_ref, (g0, Rows(d0, d1)), (act0, act1),
             bias_ref, act_buf, gi_buf)()


def turn_kernel(n2_ref, n2T_ref, cot_ref, p0, p1, p2, p3, back_in, hidden_ref, m0, m1, m2, m3, pa0, pa1, pa2, pa3, small_in,
                gh_ref, dT0, dT1, dT2, dT3, g0, g1, g2, g3, o0, o2, o_send, act0, act1, act2, act3, bias_ref, small_ref,
                act_buf, gi_buf, back_buf):
    local = m0.shape[0]
    weight_grads = ff_slots(n2_ref[...], n2T_ref[...], cot_ref[...], (p0, p1, p2, p3), back_buf, (g0, g1, g2, g3), (act0, act1, act2, act3), bias_ref,
             act_buf, gi_buf)
    cot_f = cot_ref[...].astype(F32)
    back = back_buf[...] + back_in[...]
    xhat, scale = norm_terms(hidden_ref[...])
    grad_hidden = cot_f + norm_back(back, small_in[3:4, :], xhat, scale)
    gh_ref[...] = grad_hidden
    small_ref[0:1, :] = jnp.sum(grad_hidden, axis=0, keepdims=True)
    small_ref[1:2, :] = jnp.sum(back * xhat, axis=0, keepdims=True)
    small_ref[2:3, :] = jnp.sum(back, axis=0, keepdims=True)
    small_ref[3:4, :] = jnp.sum(cot_f, axis=0, keepdims=True)
    low = grad_hidden.astype(BF)
    weight_grads()
    weight = jnp.concatenate([p[:D, 3 * local :] for p in (pa0, pa1, pa2, pa3)], axis=1)
    grads_T = dot(weight, low, TT).astype(BF)
    for s, ref in enumerate((dT0, dT1, dT2, dT3)):
        ref[...] = grads_T[s * local : (s + 1) * local]
    mixed = jnp.concatenate([m[...].astype(BF) for m in (m0, m1, m2, m3)], axis=0)
    grad = dot(mixed, low, NN).astype(BF)
    for s, (ref, first) in enumerate(((o0, 0), (o_send, 0), (o2, 0), (o_send, 2 * local))):
        for part in range(2):
            at = first + part * local
            ref[at : at + local, :] = grad[s * local : (s + 1) * local, part * CHUNK : (part + 1) * CHUNK]


def attention_backward(e_ref, dT_ref, inv_ref, mixed_ref, vT_ref, qT_ref, kT_ref, nT_ref, dq_ref, dkv_ref, grad_ref, bias_ref,
                       ds_buf):
    rows = qT_ref.shape[1]
    keys = kT_ref.shape[1]
    local = qT_ref.shape[0]
    heads = local // HEAD
    blocks = [(h, c) for h in range(heads) for c in range(rows // CHUNK)]
    which = lax.broadcasted_iota(jnp.int32, (EXTRA, CHUNK), 0)
    ones2 = (lax.broadcasted_iota(jnp.int32, (EXTRA, CHUNK), 0) < 2).astype(F32).astype(BF)
    lows = {}

    def enter(i):
        h, c = blocks[i]
        here = slice(h * HEAD, (h + 1) * HEAD)
        columns = slice(c * CHUNK, (c + 1) * CHUNK)
        low = (dT_ref[here, columns].astype(F32) * inv_ref[h : h + 1, columns]).astype(BF)
        delta = jnp.sum(low.astype(F32) * mixed_ref[here, columns], axis=0, keepdims=True)
        high = (-delta).astype(BF).astype(F32)
        extra = jnp.where(which == 0, high, jnp.where(which == 1, -delta - high, 0.0)).astype(BF)
        more = jnp.concatenate([low, extra], axis=0)
        lows[i] = low
        for k in range(keys // CHUNK):
            span = slice(k * CHUNK, (k + 1) * CHUNK)
            v = jnp.concatenate([vT_ref[here, span], ones2], axis=0)
            ds_buf[i % 2, span, :] = (e_ref[h, c, span, :].astype(F32) * dot(v, more, TN)).astype(BF)

    dv = None
    dk = None
    enter(0)
    for i, (h, c) in enumerate(blocks):
        if i + 1 < len(blocks):
            enter(i + 1)
        here = slice(h * HEAD, (h + 1) * HEAD)
        columns = slice(c * CHUNK, (c + 1) * CHUNK)
        part = dot(lows[i], e_ref[h, c], NT)
        dv = part if c == 0 else dv + part
        dq_ref[here, columns] = (dot(kT_ref[here, :], ds_buf[i % 2], NN) * HEAD**-0.5).astype(BF)
        part = dot(qT_ref[here, columns], ds_buf[i % 2], NT)
        dk = part if c == 0 else dk + part
        if c == rows // CHUNK - 1:
            dkv_ref[here, :] = dk.astype(BF)
            dkv_ref[local + h * HEAD : local + (h + 1) * HEAD, :] = dv.astype(BF)
    for ref, count, columns in ((dq_ref, rows, slice(0, local)), (dkv_ref, keys, slice(local, 3 * local))):
        grad = dot(nT_ref[:, :count], ref[...], NT)
        grad_ref[:, columns] = grad[:D].astype(BF)
        bias_ref[:, columns] = grad[D : D + 1]


def first_kernel(half, x_ref, xs_ref, pa0, pa1, pa2, pa3, *rest):
    sources = rest[:8]
    small_two, b0, b1, b2, b3, f00, f01, f1, own_ref, sib_ref, small_ref = rest[8:]
    local = pa0.shape[1] // TENSOR
    rows = own_ref.shape[0]
    device = lax.axis_index("tensor")
    small_ref[...] = jnp.zeros(small_ref.shape, F32)
    gain_sum = 0.0
    shift_sum = 0.0
    for part, ref in enumerate((x_ref, xs_ref)):
        columns = slice(part * rows, (part + 1) * rows)
        total = None
        for slot, p in enumerate((pa0, pa1, pa2, pa3)):
            for index, lanes in ((0, slice(0, local)), (1, slice(local, 3 * local)))[part:]:
                term = dot(sources[slot * 2 + index][:, columns], p[:D, lanes], TT)
                total = term if total is None else total + term
        if part == 0:
            own_ref[...] = total
        else:
            sib_ref[...] = total.astype(BF)
        xhat, _ = norm_terms(ref[:half, :].astype(F32))
        gain_sum = gain_sum + jnp.sum(total[:half] * xhat, axis=0, keepdims=True)
        shift_sum = shift_sum + jnp.sum(total, axis=0, keepdims=True)
    small_ref[0:4, :] = small_two[...]
    small_ref[4:5, :] = gain_sum
    small_ref[5:6, :] = shift_sum
    for slot, b in enumerate((b0, b1, b2, b3)):
        owner = jnp.bitwise_xor(device, slot)
        small_ref[pl.ds(8 + owner, 1), :] = jnp.concatenate(
            [(f00, f01)[slot // 2][slot % 2 : slot % 2 + 1, :], f1[slot : slot + 1, :]], axis=1
        )
        small_ref[pl.ds(12 + owner, 1), : 3 * local] = b[...]


def branch_kernel(hidden_ref, small_ref, *rest):
    *refs, out_ref = rest
    acts, packs = refs[: 2 * TENSOR], refs[2 * TENSOR :]
    packs = packs[:3] + [Rows(*packs[3:5])] + packs[5:]
    act = jnp.concatenate([a[...] for a in acts], axis=1)
    weight = jnp.concatenate(
        [jnp.concatenate([p[D : D + CHUNK, :], p[D + CHUNK : 2 * D, :]], axis=1) for p in packs], axis=0
    )
    total = hidden_ref[...] + dot(act, weight, NN) + small_ref[5:6, :]
    out_ref[...] = total[: out_ref.shape[0]].astype(BF)


def last_kernel(x_ref, own_ref, got_ref, gh_ref, small_ref, out_ref):
    half = out_ref.shape[0]
    grad = own_ref[:half, :] + got_ref[:half, :].astype(F32)
    xhat, scale = norm_terms(x_ref[:half, :].astype(F32))
    out_ref[...] = gh_ref[:half, :] + norm_back(grad, small_ref[0:1, :], xhat, scale)


def place_of(bit):
    return lax.rem(lax.div(lax.axis_index("dp"), bit), 2)


def merge(kept, got, buf, bit=1):
    rows = kept.shape[0]
    upper = place_of(bit)
    buf[pl.ds(pl.multiple_of(upper * rows, rows), rows), :] = kept[...].astype(F32)
    buf[pl.ds(pl.multiple_of((1 - upper) * rows, rows), rows), :] = got[...].astype(F32)


def finish_ff_kernel(first, kept, got, expand_ref, reduce_ref, out_ref, second):
    local = out_ref.shape[0]
    merge(kept, got, second)
    for index, ref in enumerate((first, second)):
        lanes = slice(index * CHUNK, (index + 1) * CHUNK)
        expand_ref[:, lanes] = ref[:D, :].astype(F32)
        for part in range(2):
            rows = slice(D + part * CHUNK, D + (part + 1) * CHUNK)
            reduce_ref[lanes, part * CHUNK : (part + 1) * CHUNK] = ref[rows, :].astype(F32)
    for part in range(2):
        rows = slice(2 * D + part * local, 2 * D + (part + 1) * local)
        out_ref[:, part * CHUNK : (part + 1) * CHUNK] = second[rows, :]


def finish_qkv_kernel(kept, got, sums_ref, more_ref, q_ref, k_ref, v_ref, bias_q, bias_v, bias_ff, s0, s1, s2, s3, s4, s5, buf, sums):
    merge(kept, got, buf)
    local = q_ref.shape[1]
    for index, ref in enumerate((q_ref, k_ref, v_ref)):
        ref[...] = buf[:, index * local : (index + 1) * local]
        ref.flush()
    sums[...] = sums_ref[...] + more_ref[...]
    device = lax.axis_index("tensor")
    for index, ref in enumerate((s0, s1, s2, s3, s4, s5)):
        ref[...] = sums[index : index + 1, :].reshape(D)
    bias_ff[...] = sums[pl.ds(8 + device, 1), :].reshape(D)
    both = sums[pl.ds(12 + device, 1), :]
    bias_q[...] = both[:, :local].reshape(local)
    bias_v[...] = both[:, 2 * local : 3 * local].reshape(local)


class Chain:
    def __init__(self, along, size, halvings, pieces):
        bits = [1 << i for i in range(size.bit_length() - 1)]
        halvings = min(halvings, len(bits))
        self.along = along
        self.plan = [("half", b) for b in bits[:halvings]] + [("full", b) for b in bits[halvings:]]
        self.plan += [("back", b) for b in reversed(bits[:halvings])]
        self.at = -1
        self.pieces = pieces

    def left(self):
        return len(self.plan) - 1 - self.at

    def last(self):
        return tuple(self.pieces[0])

    def due(self):
        kind, bit = self.plan[self.at + 1]
        if kind == "half":
            return "halves", self.pieces, bit
        if self.at >= 0 and self.plan[self.at][0] == "back":
            return ("merge",) + tuple(self.pieces[0]) + (self.plan[self.at][1],)
        return "sum", self.pieces

    def taken(self, *results):
        self.at += 1
        send, keep = results if len(results) == 2 else results * 2
        self.pieces = [(keep, self.along(send, self.plan[self.at][1]))]


def swap(value, axis, size, bit):
    return lax.ppermute(value, axis, [(i, i ^ bit) for i in range(size)])


def on_device(dp, frames, query_weight, query_bias, key_weight, value_weight, value_bias, out_weight, out_bias, first_gain, first_shift,
              expand_weight, expand_bias, reduce_weight, reduce_bias, second_gain, second_shift, span_start, span_end, empty_flag, cotangent):
    half = frames.shape[0]
    rows = -(-half // CHUNK) * CHUNK
    keys = 2 * rows
    local = query_weight.shape[1]
    heads = local // HEAD
    blocks = rows // CHUNK
    line = Line()

    def across(v, bit):
        return swap(v, "tensor", TENSOR, bit)

    def along(v, bit):
        return swap(v, "dp", dp, bit)

    xs = across(frames, 1)
    pa0, small = line.run(
        pack_kernel, (shaped(D + EXTRA, 4 * local), shaped(8, D, dtype=F32)), "f" * 12,
        (query_weight, key_weight, value_weight, out_weight, query_bias, value_bias,
         first_gain, first_shift, out_bias, second_gain, second_shift, reduce_bias), us=2,
    )
    pa2 = across(pa0, 2)
    pa1 = across(pa0, 1)

    forward_outs = (
        (shaped(heads, blocks, keys, CHUNK), "V"), shaped(local, rows), shaped(local, keys), shaped(local, keys),
        shaped(local, rows, dtype=F32), shaped(heads, rows, dtype=F32),
    )
    forward_scratch = (
        pltpu.VMEM((2, keys, CHUNK), F32),
    )
    spans = (span_start, span_end, empty_flag)
    ff_weights = (expand_weight, reduce_weight, expand_bias)
    ff0_shape = shaped(2 * D + 3 * EXTRA, CHUNK)
    ff1_shape = shaped(2 * D + 4 * EXTRA, CHUNK)
    normed, ff0, x, *s0 = line.run(
        functools.partial(start_kernel, half), (shaped(D + EXTRA, keys), ff0_shape, shaped(rows, D)) + forward_outs, "sssfvvvfff",
        spans + (frames, xs, small, pa0) + ff_weights, forward_scratch + (pltpu.VMEM((2, rows, D), BF),), us=8,
    )
    ff0_far = across(ff0, 2)
    ff0_near = across(ff0, 1)
    cot, ff1, *s1 = line.run(
        functools.partial(near_kernel, half), (shaped(rows, D), ff1_shape) + forward_outs, "sssvvffff",
        spans + (normed, pa1, cotangent) + ff_weights, forward_scratch, us=7,
    )
    pa2 = line.touch(pa2)
    pa3 = across(pa2, 1)
    s2 = line.run(
        functools.partial(attention_forward, half), forward_outs, "sssvv", spans + (normed, pa2), forward_scratch, us=7,
    )
    ff1 = line.touch(ff1)
    ff1_far = across(ff1, 2)
    s3 = line.run(
        functools.partial(attention_forward, half), forward_outs, "sssvv",
        spans + (normed, pa3), forward_scratch, us=7,
    )
    slots = (s0, s1, s2, s3)
    mixed = tuple(s[4] for s in slots)
    packs = (pa0, pa1, pa2, pa3)
    cuts = [(0, D), (D, ff0_shape.shape[0] - D)]
    ff0_cross = [across(v, 1) for v in line.tick(*(("sum", [((ff0_far,) + cut,)]) for cut in cuts))]
    whole = shaped(rows, D, dtype=F32)
    hidden, n2, n2T = line.run(
        out_kernel, (whole, shaped(rows, D), shaped(D + EXTRA, rows)), "v" * 10,
        (x,) + mixed + packs + (small,), us=8,
    )
    ff1_near = across(ff1, 1)
    ff_scratch = (pltpu.VMEM((rows, TENSOR * CHUNK), BF), pltpu.VMEM((rows, TENSOR * CHUNK), BF))
    bias_shape = shaped(TENSOR, CHUNK, dtype=F32)
    ff_grads = (shaped(2 * D, CHUNK),) * TENSOR
    ff_acts = (shaped(rows, CHUNK),) * TENSOR
    two = (whole,) + ff_grads[:2] + ff_acts[:2] + (shaped(2, CHUNK, dtype=F32),)
    half_scratch = (pltpu.VMEM((rows, 2 * CHUNK), BF), pltpu.VMEM((rows, 2 * CHUNK), BF))
    back, a2, *a3, act2, act3, bias_far = line.run(
        ff_first_kernel, two[:2] + (shaped(D, CHUNK),) * 2 + two[3:], "v" * 6, (n2, n2T, cot, ff0_far, *ff0_cross), half_scratch,
        us=4, vmem=10,
    )
    got_a3 = [across(v, 1) for v in a3]
    back, a0, a1, act0, act1, bias_near = line.run(
        ff_kernel, two, "v" * 6, (n2, n2T, cot, ff0, ff0_near, back), half_scratch, us=4, vmem=10,
    )
    acts_a, bias_a = (act0, act1, act2, act3), (bias_near, bias_far)
    got_a1 = across(a1, 1)
    spare = jnp.zeros((EXTRA, CHUNK), BF)
    (far_a,) = line.tick(("sum", [((a2, i * D, D), v) for i, v in enumerate(got_a3)] + [(spare,)]))
    y_a = across(far_a, 2)
    ff1_far = line.touch(ff1_far)
    ff1_cross = across(ff1_far, 1)
    size_b = 2 * D + 2 * local
    grad_hidden, *rest = line.run(
        turn_kernel,
        ((whole, "f"),) + (shaped(local, rows),) * TENSOR + ff_grads
        + (shaped(2 * local, CHUNK), shaped(2 * local, CHUNK), shaped(4 * local, CHUNK)) + ff_acts + (bias_shape, shaped(4, D, dtype=F32)),
        "v" * 18,
        (n2, n2T, cot, ff1, ff1_near, ff1_far, ff1_cross, back, hidden) + mixed + packs + (small,),
        ff_scratch + (pltpu.VMEM((rows, D), F32),), us=12, vmem=14,
    )
    dT, (f0, f1, f2, f3, o0, o2, o_send) = rest[:TENSOR], rest[TENSOR : TENSOR + 7]
    acts_b, (bias_b, small_two) = rest[TENSOR + 7 : 2 * TENSOR + 7], rest[2 * TENSOR + 7 :]
    got_f1 = across(f1, 1)
    got_f3 = across(f3, 1)
    got_o = across(o_send, 1)

    backward_outs = (
        shaped(local, rows), shaped(2 * local, keys), shaped(D, 3 * local), shaped(1, 3 * local, dtype=F32),
    )

    def backward(slot):
        e, q, k, v, m, inv = slots[slot]
        return line.run(
            attention_backward, backward_outs, "V" + "v" * 7,
            (e, dT[slot], inv, m, v, q, k, normed), (pltpu.VMEM((2, keys, CHUNK), BF),), us=8, vmem=8,
        )

    def chain(halvings, pieces):
        return Chain(along, dp, halvings, pieces)

    *d3, g3, b3 = backward(3)
    chain_a = chain(1, [(a0, got_a1, (y_a, 0, 2 * D))])
    pair = 2 * local
    far_b, send_3, *halves = line.tick(
        ("sum", [(f2, got_f3), (o2, (got_o, pair, pair))]), ("sum", [(g3,)]), chain_a.due()
    )
    y_b = across(far_b, 2)
    got_3 = across(send_3, 1)
    chain_a.taken(*halves)
    *d2, g2, b2 = backward(2)
    spare = jnp.zeros((EXTRA, 3 * local), BF)
    far_q, whole_a = line.tick(("sum", [(g2, got_3), (spare,)]), chain_a.due())
    y_q = across(far_q, 2)
    chain_a.taken(whole_a)
    *d1, g1, b1 = backward(1)
    chain_b = chain(2, [(f0, got_f1, (y_b, 0, 2 * D)), (o0, (got_o, 0, pair), (y_b, 2 * D, pair))])
    send_1, whole_a, *halves = line.tick(("sum", [(g1,)]), chain_a.due(), chain_b.due())
    got_1 = across(send_1, 1)
    chain_a.taken(whole_a)
    chain_b.taken(*halves)
    *d0, g0, b0 = backward(0)
    chain_q = chain(2, [(g0, got_1, (y_q, 0, D))])
    send_q, keep_q, send_b, keep_b = line.tick(chain_q.due(), chain_b.due())
    chain_q.taken(send_q, keep_q)
    chain_b.taken(send_b, keep_b)
    own, sib, sums = line.run(
        functools.partial(first_kernel, half), (whole, shaped(rows, D), shaped(16, D, dtype=F32)), "v" * 22,
        (x, xs) + packs + (*d0, *d1, *d2, *d3, small_two, b0, b1, b2, b3) + bias_a + (bias_b,), us=6,
    )
    (sums,) = line.tick(("sum", [(sums,)]))
    pending = across(sums, 1)
    chain_q.taken(*line.tick(chain_q.due()))
    part_b, part_a, sums, sib = line.tick(chain_b.due(), chain_a.due(), ("sum", [(sums, pending)]), ("sum", [(sib,)]))
    chain_b.taken(part_b)
    chain_a.taken(part_a)
    pending = across(sums, 2)
    got = across(sib, 1)
    (grad_frames,) = line.run(
        last_kernel, ((shaped(half, D, dtype=F32), "f"),), "vvvfv", (x, own, got, grad_hidden, small), us=4
    )
    bits = [1 << i for i in range(dp.bit_length() - 1)]

    def step(*chains, more=()):
        nonlocal sums, pending
        chains = [c for c in chains if c.left()]
        with_sums = bool(bits)
        jobs = [c.due() for c in chains] + [("sum", [(sums, pending)])] * with_sums + list(more)
        if not jobs:
            return ()
        made = list(line.tick(*jobs))
        for c in chains:
            c.taken(made.pop(0))
        if with_sums:
            sums = made.pop(0)
            pending = along(sums, bits.pop(0))
        return made

    step(chain_q, chain_b, chain_a)
    (output,) = line.run(
        branch_kernel, ((shaped(half, D), "f"),), "v" * 19,
        (hidden, small) + tuple(acts_a) + tuple(acts_b) + (ff0, ff0_near, ff0_far, *ff0_cross, ff1, ff1_near, ff1_far, ff1_cross), us=3,
    )
    while chain_a.left() or chain_b.left() > 1:
        step(chain_q, chain_b, chain_a)
    (whole_a,) = step(chain_q, chain_b, more=(("merge",) + chain_a.last() + (1,),))
    while bits or chain_q.left():
        step(chain_q)
    grad_expand, grad_reduce, grad_out = line.run(
        finish_ff_kernel, tuple((shaped(*o, dtype=F32), "f") for o in ((D, 2 * CHUNK), (2 * CHUNK, D), (local, D))),
        "vvv", (whole_a,) + chain_b.last(), (pltpu.VMEM((size_b, CHUNK), F32),), us=2,
    )
    vector = (shaped(D, dtype=F32), "f")
    short = (shaped(local, dtype=F32), "f")
    grad_q, grad_k, grad_v, bias_q, bias_v, bias_ff, *globals_ = line.run(
        finish_qkv_kernel, ((shaped(D, local, dtype=F32), "f"),) * 3 + (short, short, vector) + (vector,) * 6, "vvvv",
        chain_q.last() + (sums, pending), (pltpu.VMEM((D, 3 * local), F32), pltpu.VMEM(sums.shape, F32)), us=1,
    )
    return (
        output, grad_frames, grad_q, bias_q, grad_k, grad_v, bias_v, grad_out, globals_[0], globals_[4], globals_[5],
        grad_expand, bias_ff, grad_reduce, globals_[3], globals_[1], globals_[2],
    )


def solution(mesh):
    dp = mesh.shape["dp"]
    assert mesh.shape["tensor"] == TENSOR and dp & (dp - 1) == 0
    split = P(("dp", "tensor"), None)
    column = P(None, "tensor")
    return jax.shard_map(
        functools.partial(on_device, dp),
        mesh=mesh,
        in_specs=(
            split, column, P("tensor"), column, column, P("tensor"), P("tensor", None), P(), P(), P(),
            column, P("tensor"), P("tensor", None), P(), P(), P(), P("dp"), P("dp"), P("dp"), split,
        ),
        out_specs=(
            split, split, column, P("tensor"), column, column, P("tensor"), P("tensor", None), P(), P(), P(),
            column, P("tensor"), P("tensor", None), P(), P(), P(),
        ),
        check_vma=False,
    )
```

```python
import functools

import jax
import jax.numpy as jnp
from jax import lax
from jax.experimental import pallas as pl
from jax.experimental.pallas import tpu as pltpu
from jax.sharding import PartitionSpec as P

BF = jnp.bfloat16
F32 = jnp.float32
D = 512
HEADS = 8
HEAD = D // HEADS
EPS = 1e-05
TENSOR = 4
CHUNK = 256
EXTRA = 16
LANES = 128
NN = (((1,), (0,)), ((), ()))
NT = (((1,), (1,)), ((), ()))
TN = (((0,), (0,)), ((), ()))
TT = (((0,), (1,)), ((), ()))
VMEM = pl.BlockSpec(memory_space=pltpu.VMEM)
SMEM = pl.BlockSpec(memory_space=pltpu.SMEM)
ANY = pl.BlockSpec(memory_space=pl.ANY)


def dot(left, right, dims):
    return lax.dot_general(left, right, dims, preferred_element_type=F32)


class Fetched:
    def __init__(self, source, buffer, sem):
        self.buffer, self.shape, self.waited = buffer, buffer.shape, False
        self.copy = pltpu.make_async_copy(source, buffer, sem)
        self.copy.start()

    def __getitem__(self, index):
        if not self.waited:
            self.copy.wait()
            self.waited = True
        return self.buffer[index]


class Stored:
    def __init__(self, target, buffer, sem):
        self.buffer, self.shape, self.dtype, self.sent = buffer, buffer.shape, buffer.dtype, False
        self.copy = pltpu.make_async_copy(buffer, target, sem)

    def __getitem__(self, index):
        return self.buffer[index]

    def __setitem__(self, index, value):
        self.buffer[index] = value

    def flush(self):
        if not self.sent:
            self.copy.start()
            self.sent = True


HBM = pl.BlockSpec(memory_space=pltpu.HBM)
SPEC = {"f": HBM, "h": HBM, "s": HBM, "v": VMEM, "V": VMEM}
PINNED = {"f": pltpu.HBM, "h": pltpu.HBM, "s": pltpu.HBM, "V": pltpu.VMEM}


class Rows:
    def __init__(self, *refs):
        self.refs, self.at = refs, [0]
        for ref in refs:
            self.at.append(self.at[-1] + ref.shape[0])

    def spans(self, rows):
        first, last, _ = rows.indices(self.at[-1])
        for ref, low, high in zip(self.refs, self.at, self.at[1:]):
            if max(first, low) < min(last, high):
                yield ref, slice(max(first, low) - low, min(last, high) - low), slice(max(first, low) - first, min(last, high) - first)

    def __getitem__(self, index):
        parts = [ref[here, index[1]] for ref, here, _ in self.spans(index[0])]
        return parts[0] if len(parts) == 1 else jnp.concatenate(parts, axis=0)

    def __setitem__(self, index, value):
        for ref, here, there in self.spans(index[0]):
            ref[here, index[1]] = value[there]


class Line:
    def __init__(self):
        self.waits = ()

    def run(self, kernel, outs, ins, args, scratch=(), us=8, vmem=12):
        waits = self.waits
        outs = [o if isinstance(o, tuple) else (o, "v") for o in outs]
        kinds = list(ins)
        skip, last = len(kinds), len(outs)
        moved = [i for i, k in enumerate(kinds) if k in "fs"]
        built = [i for i, (_, k) in enumerate(outs) if k == "f"]
        space = {"f": pltpu.VMEM, "s": pltpu.SMEM}
        buffers = [space[kinds[i]](args[i].shape, args[i].dtype) for i in moved] + [pltpu.VMEM(outs[i][0].shape, outs[i][0].dtype) for i in built]

        def body(*refs):
            inputs = list(refs[:skip])
            rest = refs[skip + len(waits) :]
            results, zeros, rest = list(rest[:last]), rest[last], rest[last + 1 :]
            held, sems, rest = rest[: len(buffers)], rest[len(buffers)], rest[len(buffers) + 1 :]
            for n, i in enumerate(moved):
                inputs[i] = Fetched(inputs[i], held[n], sems.at[n])
            for n, i in enumerate(built, len(moved)):
                results[i] = Stored(results[i], held[n], sems.at[n])
            zeros[...] = jnp.zeros((8, 128), F32)
            kernel(*inputs, *results, *rest)
            for i in built:
                results[i].flush()
            for i in moved:
                if not inputs[i].waited:
                    inputs[i].copy.wait()
            for i in built:
                results[i].copy.wait()

        *got, zeros = pl.pallas_call(
            body,
            out_shape=tuple(PINNED[k](o.shape, o.dtype) if k in PINNED else o for o, k in outs) + (jax.ShapeDtypeStruct((8, 128), F32),),
            in_specs=[SPEC[k] for k in kinds] + [ANY] * len(waits),
            out_specs=[SPEC[k] for _, k in outs] + [VMEM],
            scratch_shapes=buffers + [pltpu.SemaphoreType.DMA((len(buffers) + 1,))] + list(scratch),
            compiler_params=pltpu.CompilerParams(vmem_limit_bytes=vmem * 2**20),
            cost_estimate=pl.CostEstimate(flops=10**6, bytes_accessed=2**10, transcendentals=0),
        )(*(pltpu.with_memory_space_constraint(a, PINNED[k]) if k in PINNED else a for a, k in zip(args, kinds)), *waits)
        self.waits = (zeros,)
        return got

    def touch(self, value):
        waits = self.waits
        got = (
            pl.pallas_call(
                lambda given, *rest: None,
                out_shape=jax.ShapeDtypeStruct(value.shape, value.dtype),
                in_specs=[ANY] * (1 + len(waits)),
                out_specs=ANY,
                input_output_aliases={0: 0},
                compiler_params=pltpu.CompilerParams(vmem_limit_bytes=2**20),
                cost_estimate=pl.CostEstimate(flops=10**6, bytes_accessed=1024, transcendentals=0),
            )(value, *waits)
        )
        self.waits = self.waits + (got,)
        return got

    def tick(self, *jobs):
        args, outs, scratch, plans = [], [], [], []

        def place(part):
            array, first, rows = part if isinstance(part, tuple) else (part, 0, part.shape[0])
            args.append(array)
            return len(args) - 1, first, rows

        for kind, *rest in jobs:
            pieces = [[place(part) for part in piece] for piece in ([[p] for p in rest[:2]] if kind == "merge" else rest[0])]
            rows = sum(piece[0][2] for piece in pieces)
            like = args[pieces[0][0][0]]
            columns = like.shape[1:]
            plans.append((kind, pieces, len(outs), len(scratch), rest[-1]))
            if kind == "halves":
                outs += [shaped(rows // 2, *columns)] * 2
            else:
                outs.append(jax.ShapeDtypeStruct((rows, *columns), like.dtype))
            if kind != "sum":
                scratch.append(pltpu.VMEM((rows, *columns), F32))

        def body(*refs):
            ins, results, buffers = refs[: len(args)], refs[len(args) : len(args) + len(outs)], refs[len(args) + len(outs) :]
            for kind, pieces, out, held, bit in plans:
                if kind == "merge":
                    kept, got = (ins[piece[0][0]] for piece in pieces)
                    merge(kept, got, buffers[held], bit)
                    results[out][...] = buffers[held][...].astype(results[out].dtype)
                    continue
                target = buffers[held] if kind == "halves" else results[out]
                at = 0
                for piece in pieces:
                    count = piece[0][2]
                    total = sum(ins[i][first : first + count].astype(F32) for i, first, _ in piece)
                    target[at : at + count] = total.astype(target.dtype)
                    at += count
                if kind == "halves":
                    half = at // 2
                    upper = place_of(bit)
                    results[out][...] = target[pl.ds(pl.multiple_of((1 - upper) * half, half), half), :].astype(BF)
                    results[out + 1][...] = target[pl.ds(pl.multiple_of(upper * half, half), half), :].astype(BF)

        return self.run(body, outs, "v" * len(args), args, scratch, us=1, vmem=6)


def shaped(*shape, dtype=BF):
    return jax.ShapeDtypeStruct(shape, dtype)


def norm_terms(rows_in):
    center = jnp.mean(rows_in, axis=-1, keepdims=True)
    centered = rows_in - center
    spread = jnp.mean(centered * centered, axis=-1, keepdims=True)
    scale = lax.rsqrt(spread + EPS)
    return centered * scale, scale


def norm_back(grad, gain, xhat, scale):
    e = grad * gain
    mean_e = jnp.mean(e, axis=-1, keepdims=True)
    mean_ex = jnp.mean(e * xhat, axis=-1, keepdims=True)
    return scale * (e - mean_e - xhat * mean_ex)


def valid_row(start_ref, end_ref, empty_ref, rows, half):
    lane = lax.broadcasted_iota(jnp.int32, (1, 2 * rows), 1)
    second = lane >= rows
    local = jnp.where(second, lane - rows, lane)
    device = lax.axis_index("tensor")
    clip = device // 2
    core = device % 2
    position = local + half * jnp.where(second, 1 - core, core)
    inside = (position >= start_ref[clip]) & (position < end_ref[clip])
    return (local < half) & jnp.logical_not(inside) & (empty_ref[clip] == 0)


def attention_forward(half, start_ref, end_ref, empty_ref, nT_ref, pack, e_ref, qT_ref, kT_ref, vT_ref, mixed_ref, inv_ref, s_buf,
                      prepare=None):
    rows = qT_ref.shape[1]
    keys = kT_ref.shape[1]
    local = qT_ref.shape[0]
    heads = local // HEAD
    first_row = lax.broadcasted_iota(jnp.int32, (EXTRA, keys), 0) == 0
    ones16 = first_row.astype(F32).astype(BF)

    def project(first, last, columns):
        product = dot(pack[:D, first * local : last * local], nT_ref[:D, columns], TN)
        bias = dot(pack[D:, first * local : last * local], ones16[:, :LANES], TN)
        return (product + jnp.concatenate([bias] * (rows // LANES), axis=1)).astype(BF)

    for part in (1, 0):
        columns = slice(part * rows, (part + 1) * rows)
        if prepare is not None:
            prepare(part)
        both = project(1, 3, columns)
        kT_ref[:, columns] = both[:local]
        vT_ref[:, columns] = both[local:]
    qT_ref[...] = (project(0, 1, slice(0, rows)).astype(F32) * HEAD**-0.5).astype(BF)

    valid = valid_row(start_ref, end_ref, empty_ref, rows, half)
    some = jnp.max(valid.astype(F32), axis=1, keepdims=True)
    mask = jnp.where(first_row, jnp.where(valid, 0.0, -1e30), 0.0).astype(BF)

    blocks = [(h, c) for h in range(heads) for c in range(rows // CHUNK)]
    tops = {}

    def score(i):
        h, c = blocks[i]
        q = jnp.concatenate([qT_ref[h * HEAD : (h + 1) * HEAD, c * CHUNK : (c + 1) * CHUNK], ones16[:, :CHUNK]], axis=0)
        top = None
        for k in range(keys // CHUNK):
            span = slice(k * CHUNK, (k + 1) * CHUNK)
            s = dot(jnp.concatenate([kT_ref[h * HEAD : (h + 1) * HEAD, span], mask[:, span]], axis=0), q, TN)
            s_buf[i % 2, span, :] = s
            part = jnp.max(s.reshape(CHUNK // 8, 8, CHUNK), axis=0)
            top = part if top is None else jnp.maximum(top, part)
        tops[i] = jnp.max(top, axis=0, keepdims=True)

    score(0)
    for i, (h, c) in enumerate(blocks):
        if i + 1 < len(blocks):
            score(i + 1)
        columns = slice(c * CHUNK, (c + 1) * CHUNK)
        for k in range(keys // CHUNK):
            span = slice(k * CHUNK, (k + 1) * CHUNK)
            e_ref[h, c, span, :] = jnp.exp(s_buf[i % 2, span, :] - tops[i]).astype(BF)
        value = jnp.concatenate([vT_ref[h * HEAD : (h + 1) * HEAD, :], jnp.ones((EXTRA, keys), BF)], axis=0)
        o = dot(value, e_ref[h, c], NN)
        inv = some / o[HEAD : HEAD + 1, :]
        mixed_ref[h * HEAD : (h + 1) * HEAD, columns] = o[:HEAD] * inv
        inv_ref[h : h + 1, columns] = inv


def ff_pack(first, w1_ref, w2_ref, out_ref):
    out_ref[:D, :] = w1_ref[:, first : first + CHUNK]
    for part in range(2):
        out_ref[D + part * CHUNK : D + (part + 1) * CHUNK, :] = w2_ref[first : first + CHUNK, part * CHUNK : (part + 1) * CHUNK]


def pack_kernel(wq, wk, wv, wo, bq, bv, b1, g1, s1, ob, g2, s2, rb, pack_ref, small_ref):
    local = wq.shape[1]
    for index, ref in enumerate((wq, wk, wv)):
        pack_ref[:D, index * local : (index + 1) * local] = ref[...]
    pack_ref[:D, 3 * local :] = wo[...].T
    pack_ref[D:, :] = jnp.zeros((EXTRA, 4 * local), BF)
    pack_ref[D : D + 1, :local] = bq[...].reshape(1, local)
    pack_ref[D : D + 1, 2 * local : 3 * local] = bv[...].reshape(1, local)
    pack_ref[D + 1 : D + 2, :] = b1[...].reshape(1, 4 * local)
    for index, ref in enumerate((g1, s1, ob, g2, s2, rb)):
        small_ref[index : index + 1, :] = ref[...].astype(F32).reshape(1, D)


def start_kernel(half, start_ref, end_ref, empty_ref, x_ref, xs_ref, small_ref, pack, w1_ref, w2_ref, nT_ref, ff_ref, pad_ref, *rest):
    *rest, n_buf = rest
    rows = n_buf.shape[1]
    gain = small_ref[0:1, :]
    shift = small_ref[1:2, :]
    nT_ref[D:, :] = (lax.broadcasted_iota(jnp.int32, (EXTRA, 2 * rows), 0) == 0).astype(F32).astype(BF)

    def prepare(part):
        xhat, _ = norm_terms((x_ref, xs_ref)[part][...].astype(F32))
        n_buf[part, :half, :] = (xhat * gain + shift).astype(BF)
        n_buf[part, half:, :] = jnp.zeros((rows - half, D), BF)
        nT_ref[:D, part * rows : (part + 1) * rows] = n_buf[part].T

    attention_forward(half, start_ref, end_ref, empty_ref, nT_ref, pack, *rest, prepare=prepare)
    ff_pack(0, w1_ref, w2_ref, ff_ref)
    pad_ref[half:, :] = jnp.zeros((rows - half, D), BF)
    pad_ref[:half, :] = x_ref[...]


def near_kernel(half, start_ref, end_ref, empty_ref, nT_ref, pack, cot_ref, w1_ref, w2_ref, pad_ref, ff_ref, *rest):
    attention_forward(half, start_ref, end_ref, empty_ref, nT_ref, pack, *rest)
    pad_ref[half:, :] = jnp.zeros((pad_ref.shape[0] - half, D), BF)
    pad_ref[:half, :] = cot_ref[...]
    ff_pack(CHUNK, w1_ref, w2_ref, ff_ref)


def cross_kernel(half, start_ref, end_ref, empty_ref, nT_ref, first, second, pack_ref, *rest):
    pack_ref[: first.shape[0], :] = first[...]
    pack_ref[first.shape[0] :, :] = second[...]
    attention_forward(half, start_ref, end_ref, empty_ref, nT_ref, pack_ref, *rest)


def out_kernel(x_ref, m0, m1, m2, m3, pa0, pa1, pa2, pa3, small_ref, hidden_ref, n2_ref, n2T_ref):
    local = m0.shape[0]
    mixed = jnp.concatenate([m[...].astype(BF) for m in (m0, m1, m2, m3)], axis=0)
    weight = jnp.concatenate([p[:D, 3 * local :] for p in (pa0, pa1, pa2, pa3)], axis=1)
    hidden = dot(mixed, weight, TT) + small_ref[2:3, :] + x_ref[...].astype(F32)
    hidden_ref[...] = hidden
    xhat, _ = norm_terms(hidden)
    n2 = (xhat * small_ref[3:4, :] + small_ref[4:5, :]).astype(BF)
    n2_ref[...] = n2
    n2T_ref[:D, :] = n2.T
    n2T_ref[D:, :] = (lax.broadcasted_iota(jnp.int32, (EXTRA, n2.shape[0]), 0) == 0).astype(F32).astype(BF)


def phi_terms(inner):
    bell = jnp.exp(inner * inner * -0.5)
    x = jnp.abs(inner) * 0.7071067811865476
    t = 1.0 / (1.0 + 0.3275911 * x)
    poly = t * (0.254829592 + t * (-0.284496736 + t * (1.421413741 + t * (-1.453152027 + t * 1.061405429))))
    tail = 0.5 * poly * bell
    return jnp.where(inner >= 0, 1.0 - tail, tail), bell * 0.3989422804014327


def ff_slots(n2, n2T, cot, packs, biases, back_ref, grad_refs, act_refs, bias_ref, act_buf, gi_buf):
    parts = 3
    piece = n2.shape[0] // parts
    units = [(s, r) for s in range(len(packs)) for r in range(parts)]

    def enter(s, r):
        p = packs[s]
        at = slice(r * piece, (r + 1) * piece)
        w2 = jnp.concatenate([p[D : D + CHUNK, :], p[D + CHUNK : 2 * D, :]], axis=1)
        return dot(n2[at], p[:D, :], NN) + biases[s].astype(F32), dot(cot[at], w2, NT)

    ahead = enter(*units[0])
    for i, (s, r) in enumerate(units):
        inner, grad = ahead
        if i + 1 < len(units):
            ahead = enter(*units[i + 1])
        at = slice(r * piece, (r + 1) * piece)
        lanes = slice(s * CHUNK, (s + 1) * CHUNK)
        cdf, density = phi_terms(inner)
        act = (inner * cdf).astype(BF)
        act_buf[at, lanes] = act
        act_refs[s][at, :] = act
        gi_buf[at, lanes] = (grad * (cdf + inner * density)).astype(BF)
    w1 = jnp.concatenate([p[:D, :] for p in packs], axis=1)
    back_ref[...] = dot(gi_buf[...], w1, NT)

    def weight_grads():
        first = dot(n2T, gi_buf[...], NN)
        second = dot(act_buf[...], cot, TN).astype(BF)
        for s, ref in enumerate(grad_refs):
            at = slice(s * CHUNK, (s + 1) * CHUNK)
            ref[:D, :] = first[:D, at].astype(BF)
            ref[D : D + CHUNK, :] = second[at, :CHUNK]
            ref[D + CHUNK : 2 * D, :] = second[at, CHUNK:]
            bias_ref[s : s + 1, :] = first[D : D + 1, at]

    return weight_grads


def expand_biases(first, *packs):
    return [p[D + 1 : D + 2, first : first + CHUNK] for p in packs]


def ff_kernel(n2_ref, n2T_ref, cot_ref, p0, p1, pa0, pa1, back_in, back_ref, g0, g1, act0, act1, bias_ref, act_buf, gi_buf):
    ff_slots(n2_ref[...], n2T_ref[...], cot_ref[...], (p0, p1), expand_biases(0, pa0, pa1), back_ref, (g0, g1), (act0, act1), bias_ref,
             act_buf, gi_buf)()
    back_ref[...] += back_in[...]


def ff_first_kernel(n2_ref, n2T_ref, cot_ref, p0, c0, c1, c2, pa0, pa1, back_ref, g0, d0, d1, act0, act1, bias_ref, act_buf, gi_buf):
    ff_slots(n2_ref[...], n2T_ref[...], cot_ref[...], (p0, Rows(c0, c1, c2)), expand_biases(0, pa0, pa1), back_ref, (g0, Rows(d0, d1)),
             (act0, act1), bias_ref, act_buf, gi_buf)()


def turn_kernel(n2_ref, n2T_ref, cot_ref, p0, p1, p2, p3, back_in, hidden_ref, m0, m1, m2, m3, pa0, pa1, pa2, pa3, small_in,
                gh_ref, dT0, dT1, dT2, dT3, g0, g1, g2, g3, o0, o2, o_send, act0, act1, act2, act3, bias_ref, small_ref,
                act_buf, gi_buf, back_buf):
    local = m0.shape[0]
    weight_grads = ff_slots(n2_ref[...], n2T_ref[...], cot_ref[...], (p0, p1, p2, p3),
                            expand_biases(CHUNK, pa0, pa1, pa2, pa3), back_buf, (g0, g1, g2, g3), (act0, act1, act2, act3), bias_ref,
             act_buf, gi_buf)
    cot_f = cot_ref[...].astype(F32)
    back = back_buf[...] + back_in[...]
    xhat, scale = norm_terms(hidden_ref[...])
    grad_hidden = cot_f + norm_back(back, small_in[3:4, :], xhat, scale)
    gh_ref[...] = grad_hidden
    small_ref[0:1, :] = jnp.sum(grad_hidden, axis=0, keepdims=True)
    small_ref[1:2, :] = jnp.sum(back * xhat, axis=0, keepdims=True)
    small_ref[2:3, :] = jnp.sum(back, axis=0, keepdims=True)
    small_ref[3:4, :] = jnp.sum(cot_f, axis=0, keepdims=True)
    low = grad_hidden.astype(BF)
    weight_grads()
    weight = jnp.concatenate([p[:D, 3 * local :] for p in (pa0, pa1, pa2, pa3)], axis=1)
    grads_T = dot(weight, low, TT).astype(BF)
    for s, ref in enumerate((dT0, dT1, dT2, dT3)):
        ref[...] = grads_T[s * local : (s + 1) * local]
    mixed = jnp.concatenate([m[...].astype(BF) for m in (m0, m1, m2, m3)], axis=0)
    grad = dot(mixed, low, NN).astype(BF)
    for s, (ref, first) in enumerate(((o0, 0), (o_send, 0), (o2, 0), (o_send, 2 * local))):
        for part in range(2):
            at = first + part * local
            ref[at : at + local, :] = grad[s * local : (s + 1) * local, part * CHUNK : (part + 1) * CHUNK]


def attention_backward(e_ref, dT_ref, inv_ref, mixed_ref, vT_ref, qT_ref, kT_ref, nT_ref, dq_ref, dkv_ref, grad_ref, bias_ref,
                       ds_buf):
    rows = qT_ref.shape[1]
    keys = kT_ref.shape[1]
    local = qT_ref.shape[0]
    heads = local // HEAD
    blocks = [(h, c) for h in range(heads) for c in range(rows // CHUNK)]
    which = lax.broadcasted_iota(jnp.int32, (EXTRA, CHUNK), 0)
    ones2 = (lax.broadcasted_iota(jnp.int32, (EXTRA, CHUNK), 0) < 2).astype(F32).astype(BF)
    lows = {}

    def enter(i):
        h, c = blocks[i]
        here = slice(h * HEAD, (h + 1) * HEAD)
        columns = slice(c * CHUNK, (c + 1) * CHUNK)
        low = (dT_ref[here, columns].astype(F32) * inv_ref[h : h + 1, columns]).astype(BF)
        delta = jnp.sum(low.astype(F32) * mixed_ref[here, columns], axis=0, keepdims=True)
        high = (-delta).astype(BF).astype(F32)
        extra = jnp.where(which == 0, high, jnp.where(which == 1, -delta - high, 0.0)).astype(BF)
        more = jnp.concatenate([low, extra], axis=0)
        lows[i] = low
        for k in range(keys // CHUNK):
            span = slice(k * CHUNK, (k + 1) * CHUNK)
            v = jnp.concatenate([vT_ref[here, span], ones2], axis=0)
            ds_buf[i % 2, span, :] = (e_ref[h, c, span, :].astype(F32) * dot(v, more, TN)).astype(BF)

    dv = None
    dk = None
    enter(0)
    for i, (h, c) in enumerate(blocks):
        if i + 1 < len(blocks):
            enter(i + 1)
        here = slice(h * HEAD, (h + 1) * HEAD)
        columns = slice(c * CHUNK, (c + 1) * CHUNK)
        part = dot(lows[i], e_ref[h, c], NT)
        dv = part if c == 0 else dv + part
        dq_ref[here, columns] = (dot(kT_ref[here, :], ds_buf[i % 2], NN) * HEAD**-0.5).astype(BF)
        part = dot(qT_ref[here, columns], ds_buf[i % 2], NT)
        dk = part if c == 0 else dk + part
        if c == rows // CHUNK - 1:
            dkv_ref[here, :] = dk.astype(BF)
            dkv_ref[local + h * HEAD : local + (h + 1) * HEAD, :] = dv.astype(BF)
    for ref, count, columns in ((dq_ref, rows, slice(0, local)), (dkv_ref, keys, slice(local, 3 * local))):
        grad = dot(nT_ref[:, :count], ref[...], NT)
        grad_ref[:, columns] = grad[:D].astype(BF)
        bias_ref[:, columns] = grad[D : D + 1]


def first_kernel(half, x_ref, xs_ref, pa0, pa1, pa2, pa3, *rest):
    sources = rest[:8]
    small_two, b0, b1, b2, b3, f00, f01, f1, own_ref, sib_ref, small_ref = rest[8:]
    local = pa0.shape[1] // TENSOR
    rows = own_ref.shape[0]
    device = lax.axis_index("tensor")
    small_ref[...] = jnp.zeros(small_ref.shape, F32)
    gain_sum = 0.0
    shift_sum = 0.0
    for part, ref in enumerate((x_ref, xs_ref)):
        columns = slice(part * rows, (part + 1) * rows)
        total = None
        for slot, p in enumerate((pa0, pa1, pa2, pa3)):
            for index, lanes in ((0, slice(0, local)), (1, slice(local, 3 * local)))[part:]:
                term = dot(sources[slot * 2 + index][:, columns], p[:D, lanes], TT)
                total = term if total is None else total + term
        if part == 0:
            own_ref[...] = total
        else:
            sib_ref[...] = total.astype(BF)
        xhat, _ = norm_terms(ref[:half, :].astype(F32))
        gain_sum = gain_sum + jnp.sum(total[:half] * xhat, axis=0, keepdims=True)
        shift_sum = shift_sum + jnp.sum(total, axis=0, keepdims=True)
    small_ref[0:4, :] = small_two[...]
    small_ref[4:5, :] = gain_sum
    small_ref[5:6, :] = shift_sum
    for slot, b in enumerate((b0, b1, b2, b3)):
        owner = jnp.bitwise_xor(device, slot)
        small_ref[pl.ds(8 + owner, 1), :] = jnp.concatenate(
            [(f00, f01)[slot // 2][slot % 2 : slot % 2 + 1, :], f1[slot : slot + 1, :]], axis=1
        )
        small_ref[pl.ds(12 + owner, 1), : 3 * local] = b[...]


def branch_kernel(hidden_ref, small_ref, *rest):
    *refs, out_ref = rest
    acts, packs = refs[: 2 * TENSOR], refs[2 * TENSOR :]
    packs = packs[:3] + [Rows(*packs[3:6])] + packs[6:]
    act = jnp.concatenate([a[...] for a in acts], axis=1)
    weight = jnp.concatenate(
        [jnp.concatenate([p[D : D + CHUNK, :], p[D + CHUNK : 2 * D, :]], axis=1) for p in packs], axis=0
    )
    total = hidden_ref[...] + dot(act, weight, NN) + small_ref[5:6, :]
    out_ref[...] = total[: out_ref.shape[0]].astype(BF)


def last_kernel(x_ref, own_ref, got_ref, gh_ref, small_ref, out_ref):
    half = out_ref.shape[0]
    grad = own_ref[:half, :] + got_ref[:half, :].astype(F32)
    xhat, scale = norm_terms(x_ref[:half, :].astype(F32))
    out_ref[...] = gh_ref[:half, :] + norm_back(grad, small_ref[0:1, :], xhat, scale)


def place_of(bit):
    return lax.rem(lax.div(lax.axis_index("dp"), bit), 2)


def merge(kept, got, buf, bit=1):
    rows = kept.shape[0]
    upper = place_of(bit)
    buf[pl.ds(pl.multiple_of(upper * rows, rows), rows), :] = kept[...].astype(F32)
    buf[pl.ds(pl.multiple_of((1 - upper) * rows, rows), rows), :] = got[...].astype(F32)


def finish_ff_kernel(first, kept, got, expand_ref, reduce_ref, out_ref, second):
    local = out_ref.shape[0]
    merge(kept, got, second)
    for index, ref in enumerate((first, second)):
        lanes = slice(index * CHUNK, (index + 1) * CHUNK)
        expand_ref[:, lanes] = ref[:D, :].astype(F32)
        for part in range(2):
            rows = slice(D + part * CHUNK, D + (part + 1) * CHUNK)
            reduce_ref[lanes, part * CHUNK : (part + 1) * CHUNK] = ref[rows, :].astype(F32)
    for part in range(2):
        rows = slice(2 * D + part * local, 2 * D + (part + 1) * local)
        out_ref[:, part * CHUNK : (part + 1) * CHUNK] = second[rows, :]


def finish_qkv_kernel(kept, got, sums_ref, more_ref, q_ref, k_ref, v_ref, bias_q, bias_v, bias_ff, s0, s1, s2, s3, s4, s5, buf, sums):
    merge(kept, got, buf)
    local = q_ref.shape[1]
    for index, ref in enumerate((q_ref, k_ref, v_ref)):
        ref[...] = buf[:, index * local : (index + 1) * local]
        ref.flush()
    sums[...] = sums_ref[...] + more_ref[...]
    device = lax.axis_index("tensor")
    for index, ref in enumerate((s0, s1, s2, s3, s4, s5)):
        ref[...] = sums[index : index + 1, :].reshape(D)
    bias_ff[...] = sums[pl.ds(8 + device, 1), :].reshape(D)
    both = sums[pl.ds(12 + device, 1), :]
    bias_q[...] = both[:, :local].reshape(local)
    bias_v[...] = both[:, 2 * local : 3 * local].reshape(local)


class Chain:
    def __init__(self, along, size, halvings, pieces):
        bits = [1 << i for i in range(size.bit_length() - 1)]
        halvings = min(halvings, len(bits))
        self.along = along
        self.plan = [("half", b) for b in bits[:halvings]] + [("full", b) for b in bits[halvings:]]
        self.plan += [("back", b) for b in reversed(bits[:halvings])]
        self.at = -1
        self.pieces = pieces

    def left(self):
        return len(self.plan) - 1 - self.at

    def last(self):
        return tuple(self.pieces[0])

    def due(self):
        kind, bit = self.plan[self.at + 1]
        if kind == "half":
            return "halves", self.pieces, bit
        if self.at >= 0 and self.plan[self.at][0] == "back":
            return ("merge",) + tuple(self.pieces[0]) + (self.plan[self.at][1],)
        return "sum", self.pieces

    def taken(self, *results):
        self.at += 1
        send, keep = results if len(results) == 2 else results * 2
        self.pieces = [(keep, self.along(send, self.plan[self.at][1]))]


def swap(value, axis, size, bit):
    return lax.ppermute(value, axis, [(i, i ^ bit) for i in range(size)])


def on_device(dp, frames, query_weight, query_bias, key_weight, value_weight, value_bias, out_weight, out_bias, first_gain, first_shift,
              expand_weight, expand_bias, reduce_weight, reduce_bias, second_gain, second_shift, span_start, span_end, empty_flag, cotangent):
    half = frames.shape[0]
    rows = -(-half // CHUNK) * CHUNK
    keys = 2 * rows
    local = query_weight.shape[1]
    heads = local // HEAD
    blocks = rows // CHUNK
    line = Line()

    def across(v, bit):
        return swap(v, "tensor", TENSOR, bit)

    def along(v, bit):
        return swap(v, "dp", dp, bit)

    xs = across(frames, 1)
    pa0, small = line.run(
        pack_kernel, (shaped(D + EXTRA, 4 * local), shaped(8, D, dtype=F32)), "f" * 13,
        (query_weight, key_weight, value_weight, out_weight, query_bias, value_bias, expand_bias,
         first_gain, first_shift, out_bias, second_gain, second_shift, reduce_bias), us=2,
    )
    pa2 = across(pa0, 2)
    pa1 = across(pa0, 1)

    forward_outs = (
        (shaped(heads, blocks, keys, CHUNK), "V"), shaped(local, rows), shaped(local, keys), shaped(local, keys),
        shaped(local, rows, dtype=F32), shaped(heads, rows, dtype=F32),
    )
    forward_scratch = (
        pltpu.VMEM((2, keys, CHUNK), F32),
    )
    spans = (span_start, span_end, empty_flag)
    ff_weights = (expand_weight, reduce_weight)
    ff_shape = shaped(2 * D, CHUNK)
    normed, ff0, x, *s0 = line.run(
        functools.partial(start_kernel, half), (shaped(D + EXTRA, keys), ff_shape, shaped(rows, D)) + forward_outs, "sssfvvvff",
        spans + (frames, xs, small, pa0) + ff_weights, forward_scratch + (pltpu.VMEM((2, rows, D), BF),), us=8,
    )
    ff0_far = across(ff0, 2)
    ff0_near = across(ff0, 1)
    cot, ff1, *s1 = line.run(
        functools.partial(near_kernel, half), (shaped(rows, D), ff_shape) + forward_outs, "sssvvfff",
        spans + (normed, pa1, cotangent) + ff_weights, forward_scratch, us=7,
    )
    pa3 = [across(v, 1) for v in line.tick(("sum", [((pa2, 0, CHUNK),)]), ("sum", [((pa2, CHUNK, D + EXTRA - CHUNK),)]))]
    s2 = line.run(
        functools.partial(attention_forward, half), forward_outs, "sssvv", spans + (normed, pa2), forward_scratch, us=7,
    )
    ff1 = line.touch(ff1)
    ff1_far = across(ff1, 2)
    pa3, *s3 = line.run(
        functools.partial(cross_kernel, half), (shaped(D + EXTRA, 4 * local),) + forward_outs, "sssvvv",
        spans + (normed, *pa3), forward_scratch, us=7,
    )
    slots = (s0, s1, s2, s3)
    mixed = tuple(s[4] for s in slots)
    packs = (pa0, pa1, pa2, pa3)
    cuts = [(0, 384), (384, 320), (704, 320)]
    ff0_cross = [across(v, 1) for v in line.tick(*(("sum", [((ff0_far,) + cut,)]) for cut in cuts))]
    whole = shaped(rows, D, dtype=F32)
    hidden, n2, n2T = line.run(
        out_kernel, (whole, shaped(rows, D), shaped(D + EXTRA, rows)), "v" * 10,
        (x,) + mixed + packs + (small,), us=8,
    )
    ff1_near = across(ff1, 1)
    ff_scratch = (pltpu.VMEM((rows, TENSOR * CHUNK), BF), pltpu.VMEM((rows, TENSOR * CHUNK), BF))
    bias_shape = shaped(TENSOR, CHUNK, dtype=F32)
    ff_grads = (shaped(2 * D, CHUNK),) * TENSOR
    ff_acts = (shaped(rows, CHUNK),) * TENSOR
    two = (whole,) + ff_grads[:2] + ff_acts[:2] + (shaped(2, CHUNK, dtype=F32),)
    half_scratch = (pltpu.VMEM((rows, 2 * CHUNK), BF), pltpu.VMEM((rows, 2 * CHUNK), BF))
    back, a2, *a3, act2, act3, bias_far = line.run(
        ff_first_kernel, two[:2] + (shaped(D, CHUNK),) * 2 + two[3:], "v" * 9, (n2, n2T, cot, ff0_far, *ff0_cross, pa2, pa3), half_scratch,
        us=4, vmem=10,
    )
    got_a3 = [across(v, 1) for v in a3]
    back, a0, a1, act0, act1, bias_near = line.run(
        ff_kernel, two, "v" * 8, (n2, n2T, cot, ff0, ff0_near, pa0, pa1, back), half_scratch, us=4, vmem=10,
    )
    acts_a, bias_a = (act0, act1, act2, act3), (bias_near, bias_far)
    got_a1 = across(a1, 1)
    spare = jnp.zeros((EXTRA, CHUNK), BF)
    (far_a,) = line.tick(("sum", [((a2, i * D, D), v) for i, v in enumerate(got_a3)] + [(spare,)]))
    y_a = across(far_a, 2)
    ff1_far = line.touch(ff1_far)
    ff1_cross = across(ff1_far, 1)
    size_b = 2 * D + 2 * local
    grad_hidden, *rest = line.run(
        turn_kernel,
        ((whole, "f"),) + (shaped(local, rows),) * TENSOR + ff_grads
        + (shaped(2 * local, CHUNK), shaped(2 * local, CHUNK), shaped(4 * local, CHUNK)) + ff_acts + (bias_shape, shaped(4, D, dtype=F32)),
        "v" * 18,
        (n2, n2T, cot, ff1, ff1_near, ff1_far, ff1_cross, back, hidden) + mixed + packs + (small,),
        ff_scratch + (pltpu.VMEM((rows, D), F32),), us=12, vmem=14,
    )
    dT, (f0, f1, f2, f3, o0, o2, o_send) = rest[:TENSOR], rest[TENSOR : TENSOR + 7]
    acts_b, (bias_b, small_two) = rest[TENSOR + 7 : 2 * TENSOR + 7], rest[2 * TENSOR + 7 :]
    got_f1 = across(f1, 1)
    got_f3 = across(f3, 1)
    got_o = across(o_send, 1)

    backward_outs = (
        shaped(local, rows), shaped(2 * local, keys), shaped(D, 3 * local), shaped(1, 3 * local, dtype=F32),
    )

    def backward(slot):
        e, q, k, v, m, inv = slots[slot]
        return line.run(
            attention_backward, backward_outs, "V" + "v" * 7,
            (e, dT[slot], inv, m, v, q, k, normed), (pltpu.VMEM((2, keys, CHUNK), BF),), us=8, vmem=8,
        )

    def chain(halvings, pieces):
        return Chain(along, dp, halvings, pieces)

    *d3, g3, b3 = backward(3)
    chain_a = chain(1, [(a0, got_a1, (y_a, 0, 2 * D))])
    pair = 2 * local
    far_b, send_3, *halves = line.tick(
        ("sum", [(f2, got_f3), (o2, (got_o, pair, pair))]), ("sum", [(g3,)]), chain_a.due()
    )
    y_b = across(far_b, 2)
    got_3 = across(send_3, 1)
    chain_a.taken(*halves)
    *d2, g2, b2 = backward(2)
    spare = jnp.zeros((EXTRA, 3 * local), BF)
    far_q, whole_a = line.tick(("sum", [(g2, got_3), (spare,)]), chain_a.due())
    y_q = across(far_q, 2)
    chain_a.taken(whole_a)
    *d1, g1, b1 = backward(1)
    chain_b = chain(2, [(f0, got_f1, (y_b, 0, 2 * D)), (o0, (got_o, 0, pair), (y_b, 2 * D, pair))])
    send_1, whole_a, *halves = line.tick(("sum", [(g1,)]), chain_a.due(), chain_b.due())
    got_1 = across(send_1, 1)
    chain_a.taken(whole_a)
    chain_b.taken(*halves)
    *d0, g0, b0 = backward(0)
    chain_q = chain(2, [(g0, got_1, (y_q, 0, D))])
    send_q, keep_q, send_b, keep_b = line.tick(chain_q.due(), chain_b.due())
    chain_q.taken(send_q, keep_q)
    chain_b.taken(send_b, keep_b)
    own, sib, sums = line.run(
        functools.partial(first_kernel, half), (whole, shaped(rows, D), shaped(16, D, dtype=F32)), "v" * 22,
        (x, xs) + packs + (*d0, *d1, *d2, *d3, small_two, b0, b1, b2, b3) + bias_a + (bias_b,), us=6,
    )
    (sums,) = line.tick(("sum", [(sums,)]))
    pending = across(sums, 1)
    chain_q.taken(*line.tick(chain_q.due()))
    part_b, part_a, sums, sib = line.tick(chain_b.due(), chain_a.due(), ("sum", [(sums, pending)]), ("sum", [(sib,)]))
    chain_b.taken(part_b)
    chain_a.taken(part_a)
    pending = across(sums, 2)
    got = across(sib, 1)
    (grad_frames,) = line.run(
        last_kernel, ((shaped(half, D, dtype=F32), "f"),), "vvvfv", (x, own, got, grad_hidden, small), us=4
    )
    bits = [1 << i for i in range(dp.bit_length() - 1)]

    def step(*chains, more=()):
        nonlocal sums, pending
        chains = [c for c in chains if c.left()]
        with_sums = bool(bits)
        jobs = [c.due() for c in chains] + [("sum", [(sums, pending)])] * with_sums + list(more)
        if not jobs:
            return ()
        made = list(line.tick(*jobs))
        for c in chains:
            c.taken(made.pop(0))
        if with_sums:
            sums = made.pop(0)
            pending = along(sums, bits.pop(0))
        return made

    step(chain_q, chain_b, chain_a)
    (output,) = line.run(
        branch_kernel, ((shaped(half, D), "f"),), "v" * 20,
        (hidden, small) + tuple(acts_a) + tuple(acts_b) + (ff0, ff0_near, ff0_far, *ff0_cross, ff1, ff1_near, ff1_far, ff1_cross), us=3,
    )
    while chain_a.left() or chain_b.left() > 1:
        step(chain_q, chain_b, chain_a)
    (whole_a,) = step(chain_q, chain_b, more=(("merge",) + chain_a.last() + (1,),))
    while bits or chain_q.left():
        step(chain_q)
    grad_expand, grad_reduce, grad_out = line.run(
        finish_ff_kernel, tuple((shaped(*o, dtype=F32), "f") for o in ((D, 2 * CHUNK), (2 * CHUNK, D), (local, D))),
        "vvv", (whole_a,) + chain_b.last(), (pltpu.VMEM((size_b, CHUNK), F32),), us=2,
    )
    vector = (shaped(D, dtype=F32), "f")
    short = (shaped(local, dtype=F32), "f")
    grad_q, grad_k, grad_v, bias_q, bias_v, bias_ff, *globals_ = line.run(
        finish_qkv_kernel, ((shaped(D, local, dtype=F32), "f"),) * 3 + (short, short, vector) + (vector,) * 6, "vvvv",
        chain_q.last() + (sums, pending), (pltpu.VMEM((D, 3 * local), F32), pltpu.VMEM(sums.shape, F32)), us=1,
    )
    return (
        output, grad_frames, grad_q, bias_q, grad_k, grad_v, bias_v, grad_out, globals_[0], globals_[4], globals_[5],
        grad_expand, bias_ff, grad_reduce, globals_[3], globals_[1], globals_[2],
    )


def solution(mesh):
    dp = mesh.shape["dp"]
    assert mesh.shape["tensor"] == TENSOR and dp & (dp - 1) == 0
    split = P(("dp", "tensor"), None)
    column = P(None, "tensor")
    return jax.shard_map(
        functools.partial(on_device, dp),
        mesh=mesh,
        in_specs=(
            split, column, P("tensor"), column, column, P("tensor"), P("tensor", None), P(), P(), P(),
            column, P("tensor"), P("tensor", None), P(), P(), P(), P("dp"), P("dp"), P("dp"), split,
        ),
        out_specs=(
            split, split, column, P("tensor"), column, column, P("tensor"), P("tensor", None), P(), P(), P(),
            column, P("tensor"), P("tensor", None), P(), P(), P(),
        ),
        check_vma=False,
    )
```

```python
import functools

import jax
import jax.numpy as jnp
from jax import lax
from jax.experimental import pallas as pl
from jax.experimental.pallas import tpu as pltpu
from jax.sharding import PartitionSpec as P

BF = jnp.bfloat16
F32 = jnp.float32
D = 512
HEADS = 8
HEAD = D // HEADS
EPS = 1e-05
TENSOR = 4
CHUNK = 256
EXTRA = 16
LANES = 128
NN = (((1,), (0,)), ((), ()))
NT = (((1,), (1,)), ((), ()))
TN = (((0,), (0,)), ((), ()))
TT = (((0,), (1,)), ((), ()))
VMEM = pl.BlockSpec(memory_space=pltpu.VMEM)
SMEM = pl.BlockSpec(memory_space=pltpu.SMEM)
ANY = pl.BlockSpec(memory_space=pl.ANY)


def dot(left, right, dims):
    return lax.dot_general(left, right, dims, preferred_element_type=F32)


class Fetched:
    def __init__(self, source, buffer, sem):
        self.buffer, self.shape, self.waited = buffer, buffer.shape, False
        self.copy = pltpu.make_async_copy(source, buffer, sem)
        self.copy.start()

    def __getitem__(self, index):
        if not self.waited:
            self.copy.wait()
            self.waited = True
        return self.buffer[index]


class Stored:
    def __init__(self, target, buffer, sem):
        self.buffer, self.shape, self.dtype, self.sent = buffer, buffer.shape, buffer.dtype, False
        self.copy = pltpu.make_async_copy(buffer, target, sem)

    def __getitem__(self, index):
        return self.buffer[index]

    def __setitem__(self, index, value):
        self.buffer[index] = value

    def flush(self):
        if not self.sent:
            self.copy.start()
            self.sent = True


HBM = pl.BlockSpec(memory_space=pltpu.HBM)
SPEC = {"f": HBM, "h": HBM, "s": HBM, "v": VMEM, "V": VMEM}
PINNED = {"f": pltpu.HBM, "h": pltpu.HBM, "s": pltpu.HBM, "V": pltpu.VMEM}


class Rows:
    def __init__(self, *refs):
        self.refs, self.at = refs, [0]
        for ref in refs:
            self.at.append(self.at[-1] + ref.shape[0])

    def spans(self, rows):
        first, last, _ = rows.indices(self.at[-1])
        for ref, low, high in zip(self.refs, self.at, self.at[1:]):
            if max(first, low) < min(last, high):
                yield ref, slice(max(first, low) - low, min(last, high) - low), slice(max(first, low) - first, min(last, high) - first)

    def __getitem__(self, index):
        parts = [ref[here, index[1]] for ref, here, _ in self.spans(index[0])]
        return parts[0] if len(parts) == 1 else jnp.concatenate(parts, axis=0)

    def __setitem__(self, index, value):
        for ref, here, there in self.spans(index[0]):
            ref[here, index[1]] = value[there]


class Line:
    def __init__(self):
        self.waits = ()

    def run(self, kernel, outs, ins, args, scratch=(), us=8, vmem=12):
        waits = self.waits
        outs = [o if isinstance(o, tuple) else (o, "v") for o in outs]
        kinds = list(ins)
        skip, last = len(kinds), len(outs)
        moved = [i for i, k in enumerate(kinds) if k in "fs"]
        built = [i for i, (_, k) in enumerate(outs) if k == "f"]
        space = {"f": pltpu.VMEM, "s": pltpu.SMEM}
        buffers = [space[kinds[i]](args[i].shape, args[i].dtype) for i in moved] + [pltpu.VMEM(outs[i][0].shape, outs[i][0].dtype) for i in built]

        def body(*refs):
            inputs = list(refs[:skip])
            rest = refs[skip + len(waits) :]
            results, zeros, rest = list(rest[:last]), rest[last], rest[last + 1 :]
            held, sems, rest = rest[: len(buffers)], rest[len(buffers)], rest[len(buffers) + 1 :]
            for n, i in enumerate(moved):
                inputs[i] = Fetched(inputs[i], held[n], sems.at[n])
            for n, i in enumerate(built, len(moved)):
                results[i] = Stored(results[i], held[n], sems.at[n])
            zeros[...] = jnp.zeros((8, 128), F32)
            kernel(*inputs, *results, *rest)
            for i in built:
                results[i].flush()
            for i in moved:
                if not inputs[i].waited:
                    inputs[i].copy.wait()
            for i in built:
                results[i].copy.wait()

        *got, zeros = pl.pallas_call(
            body,
            out_shape=tuple(PINNED[k](o.shape, o.dtype) if k in PINNED else o for o, k in outs) + (jax.ShapeDtypeStruct((8, 128), F32),),
            in_specs=[SPEC[k] for k in kinds] + [ANY] * len(waits),
            out_specs=[SPEC[k] for _, k in outs] + [VMEM],
            scratch_shapes=buffers + [pltpu.SemaphoreType.DMA((len(buffers) + 1,))] + list(scratch),
            compiler_params=pltpu.CompilerParams(vmem_limit_bytes=vmem * 2**20),
            cost_estimate=pl.CostEstimate(flops=10**6, bytes_accessed=2**10, transcendentals=0),
        )(*(pltpu.with_memory_space_constraint(a, PINNED[k]) if k in PINNED else a for a, k in zip(args, kinds)), *waits)
        self.waits = (zeros,)
        return got

    def touch(self, value):
        waits = self.waits
        got = (
            pl.pallas_call(
                lambda given, *rest: None,
                out_shape=jax.ShapeDtypeStruct(value.shape, value.dtype),
                in_specs=[ANY] * (1 + len(waits)),
                out_specs=ANY,
                input_output_aliases={0: 0},
                compiler_params=pltpu.CompilerParams(vmem_limit_bytes=2**20),
                cost_estimate=pl.CostEstimate(flops=10**6, bytes_accessed=1024, transcendentals=0),
            )(value, *waits)
        )
        self.waits = self.waits + (got,)
        return got

    def tick(self, *jobs):
        args, outs, scratch, plans = [], [], [], []

        def place(part):
            array, first, rows = part if isinstance(part, tuple) else (part, 0, part.shape[0])
            args.append(array)
            return len(args) - 1, first, rows

        for kind, *rest in jobs:
            pieces = [[place(part) for part in piece] for piece in ([[p] for p in rest[:2]] if kind == "merge" else rest[0])]
            rows = sum(piece[0][2] for piece in pieces)
            like = args[pieces[0][0][0]]
            columns = like.shape[1:]
            plans.append((kind, pieces, len(outs), len(scratch), rest[-1]))
            if kind == "halves":
                outs += [shaped(rows // 2, *columns)] * 2
            else:
                outs.append(jax.ShapeDtypeStruct((rows, *columns), like.dtype))
            if kind != "sum":
                scratch.append(pltpu.VMEM((rows, *columns), F32))

        def body(*refs):
            ins, results, buffers = refs[: len(args)], refs[len(args) : len(args) + len(outs)], refs[len(args) + len(outs) :]
            for kind, pieces, out, held, bit in plans:
                if kind == "merge":
                    kept, got = (ins[piece[0][0]] for piece in pieces)
                    merge(kept, got, buffers[held], bit)
                    results[out][...] = buffers[held][...].astype(results[out].dtype)
                    continue
                target = buffers[held] if kind == "halves" else results[out]
                at = 0
                for piece in pieces:
                    count = piece[0][2]
                    total = sum(ins[i][first : first + count].astype(F32) for i, first, _ in piece)
                    target[at : at + count] = total.astype(target.dtype)
                    at += count
                if kind == "halves":
                    half = at // 2
                    upper = place_of(bit)
                    results[out][...] = target[pl.ds(pl.multiple_of((1 - upper) * half, half), half), :].astype(BF)
                    results[out + 1][...] = target[pl.ds(pl.multiple_of(upper * half, half), half), :].astype(BF)

        return self.run(body, outs, "v" * len(args), args, scratch, us=1, vmem=6)


def shaped(*shape, dtype=BF):
    return jax.ShapeDtypeStruct(shape, dtype)


def norm_terms(rows_in):
    center = jnp.mean(rows_in, axis=-1, keepdims=True)
    centered = rows_in - center
    spread = jnp.mean(centered * centered, axis=-1, keepdims=True)
    scale = lax.rsqrt(spread + EPS)
    return centered * scale, scale


def norm_back(grad, gain, xhat, scale):
    e = grad * gain
    mean_e = jnp.mean(e, axis=-1, keepdims=True)
    mean_ex = jnp.mean(e * xhat, axis=-1, keepdims=True)
    return scale * (e - mean_e - xhat * mean_ex)


def valid_row(start_ref, end_ref, empty_ref, rows, half):
    lane = lax.broadcasted_iota(jnp.int32, (1, 2 * rows), 1)
    second = lane >= rows
    local = jnp.where(second, lane - rows, lane)
    device = lax.axis_index("tensor")
    clip = device // 2
    core = device % 2
    position = local + half * jnp.where(second, 1 - core, core)
    inside = (position >= start_ref[clip]) & (position < end_ref[clip])
    return (local < half) & jnp.logical_not(inside) & (empty_ref[clip] == 0)


def attention_forward(half, start_ref, end_ref, empty_ref, nT_ref, pack, e_ref, qT_ref, kT_ref, vT_ref, mixed_ref, inv_ref, s_buf,
                      prepare=None):
    rows = qT_ref.shape[1]
    keys = kT_ref.shape[1]
    local = qT_ref.shape[0]
    heads = local // HEAD
    first_row = lax.broadcasted_iota(jnp.int32, (EXTRA, keys), 0) == 0
    ones16 = first_row.astype(F32).astype(BF)

    def project(first, last, columns):
        product = dot(pack[:D, first * local : last * local], nT_ref[:D, columns], TN)
        bias = dot(pack[D:, first * local : last * local], ones16[:, :LANES], TN)
        return (product + jnp.concatenate([bias] * (rows // LANES), axis=1)).astype(BF)

    for part in (1, 0):
        columns = slice(part * rows, (part + 1) * rows)
        if prepare is not None:
            prepare(part)
        both = project(1, 3, columns)
        kT_ref[:, columns] = both[:local]
        vT_ref[:, columns] = both[local:]
    qT_ref[...] = (project(0, 1, slice(0, rows)).astype(F32) * HEAD**-0.5).astype(BF)

    valid = valid_row(start_ref, end_ref, empty_ref, rows, half)
    some = jnp.max(valid.astype(F32), axis=1, keepdims=True)
    mask = jnp.where(first_row, jnp.where(valid, 0.0, -1e30), 0.0).astype(BF)

    blocks = [(h, c) for h in range(heads) for c in range(rows // CHUNK)]
    tops = {}

    def score(i):
        h, c = blocks[i]
        q = jnp.concatenate([qT_ref[h * HEAD : (h + 1) * HEAD, c * CHUNK : (c + 1) * CHUNK], ones16[:, :CHUNK]], axis=0)
        top = None
        for k in range(keys // CHUNK):
            span = slice(k * CHUNK, (k + 1) * CHUNK)
            s = dot(jnp.concatenate([kT_ref[h * HEAD : (h + 1) * HEAD, span], mask[:, span]], axis=0), q, TN)
            s_buf[i % 2, span, :] = s
            part = jnp.max(s.reshape(CHUNK // 8, 8, CHUNK), axis=0)
            top = part if top is None else jnp.maximum(top, part)
        tops[i] = jnp.max(top, axis=0, keepdims=True)

    score(0)
    for i, (h, c) in enumerate(blocks):
        if i + 1 < len(blocks):
            score(i + 1)
        columns = slice(c * CHUNK, (c + 1) * CHUNK)
        for k in range(keys // CHUNK):
            span = slice(k * CHUNK, (k + 1) * CHUNK)
            e_ref[h, c, span, :] = jnp.exp(s_buf[i % 2, span, :] - tops[i]).astype(BF)
        value = jnp.concatenate([vT_ref[h * HEAD : (h + 1) * HEAD, :], jnp.ones((EXTRA, keys), BF)], axis=0)
        o = dot(value, e_ref[h, c], NN)
        inv = some / o[HEAD : HEAD + 1, :]
        mixed_ref[h * HEAD : (h + 1) * HEAD, columns] = o[:HEAD] * inv
        inv_ref[h : h + 1, columns] = inv


def ff_pack(first, w1_ref, w2_ref, out_ref):
    out_ref[:D, :] = w1_ref[:, first : first + CHUNK]
    for part in range(2):
        out_ref[D + part * CHUNK : D + (part + 1) * CHUNK, :] = w2_ref[first : first + CHUNK, part * CHUNK : (part + 1) * CHUNK]


def pack_kernel(wq, wk, wv, wo, bq, bv, b1, g1, s1, ob, g2, s2, rb, pack_ref, small_ref):
    local = wq.shape[1]
    for index, ref in enumerate((wq, wk, wv)):
        pack_ref[:D, index * local : (index + 1) * local] = ref[...]
    pack_ref[:D, 3 * local :] = wo[...].T
    pack_ref[D:, :] = jnp.zeros((EXTRA, 4 * local), BF)
    pack_ref[D : D + 1, :local] = bq[...].reshape(1, local)
    pack_ref[D : D + 1, 2 * local : 3 * local] = bv[...].reshape(1, local)
    pack_ref[D + 1 : D + 2, :] = b1[...].reshape(1, 4 * local)
    for index, ref in enumerate((g1, s1, ob, g2, s2, rb)):
        small_ref[index : index + 1, :] = ref[...].astype(F32).reshape(1, D)


def start_kernel(half, start_ref, end_ref, empty_ref, x_ref, xs_ref, small_ref, pack, w1_ref, w2_ref, nT_ref, ff_ref, pad_ref, *rest):
    *rest, n_buf = rest
    rows = n_buf.shape[1]
    gain = small_ref[0:1, :]
    shift = small_ref[1:2, :]
    nT_ref[D:, :] = (lax.broadcasted_iota(jnp.int32, (EXTRA, 2 * rows), 0) == 0).astype(F32).astype(BF)

    def prepare(part):
        xhat, _ = norm_terms((x_ref, xs_ref)[part][...].astype(F32))
        n_buf[part, :half, :] = (xhat * gain + shift).astype(BF)
        n_buf[part, half:, :] = jnp.zeros((rows - half, D), BF)
        nT_ref[:D, part * rows : (part + 1) * rows] = n_buf[part].T

    attention_forward(half, start_ref, end_ref, empty_ref, nT_ref, pack, *rest, prepare=prepare)
    ff_pack(0, w1_ref, w2_ref, ff_ref)
    pad_ref[half:, :] = jnp.zeros((rows - half, D), BF)
    pad_ref[:half, :] = x_ref[...]


def near_kernel(half, start_ref, end_ref, empty_ref, nT_ref, pack, cot_ref, w1_ref, w2_ref, pad_ref, ff_ref, *rest):
    attention_forward(half, start_ref, end_ref, empty_ref, nT_ref, pack, *rest)
    pad_ref[half:, :] = jnp.zeros((pad_ref.shape[0] - half, D), BF)
    pad_ref[:half, :] = cot_ref[...]
    ff_pack(CHUNK, w1_ref, w2_ref, ff_ref)


def cross_kernel(half, start_ref, end_ref, empty_ref, nT_ref, first, second, pack_ref, *rest):
    pack_ref[: first.shape[0], :] = first[...]
    pack_ref[first.shape[0] :, :] = second[...]
    attention_forward(half, start_ref, end_ref, empty_ref, nT_ref, pack_ref, *rest)


def out_kernel(x_ref, m0, m1, m2, m3, pa0, pa1, pa2, pa3, small_ref, hidden_ref, n2_ref, n2T_ref):
    local = m0.shape[0]
    mixed = jnp.concatenate([m[...].astype(BF) for m in (m0, m1, m2, m3)], axis=0)
    weight = jnp.concatenate([p[:D, 3 * local :] for p in (pa0, pa1, pa2, pa3)], axis=1)
    hidden = dot(mixed, weight, TT) + small_ref[2:3, :] + x_ref[...].astype(F32)
    hidden_ref[...] = hidden
    xhat, _ = norm_terms(hidden)
    n2 = (xhat * small_ref[3:4, :] + small_ref[4:5, :]).astype(BF)
    n2_ref[...] = n2
    n2T_ref[:D, :] = n2.T
    n2T_ref[D:, :] = (lax.broadcasted_iota(jnp.int32, (EXTRA, n2.shape[0]), 0) == 0).astype(F32).astype(BF)


def phi_terms(inner):
    bell = jnp.exp(inner * inner * -0.5)
    x = jnp.abs(inner) * 0.7071067811865476
    t = 1.0 / (1.0 + 0.3275911 * x)
    poly = t * (0.254829592 + t * (-0.284496736 + t * (1.421413741 + t * (-1.453152027 + t * 1.061405429))))
    tail = 0.5 * poly * bell
    return jnp.where(inner >= 0, 1.0 - tail, tail), bell * 0.3989422804014327


def ff_slots(n2, n2T, cot, packs, biases, grad_refs, act_refs, bias_ref, act_buf, gi_buf):
    parts = 2
    piece = n2.shape[0] // parts
    units = [(s, r) for s in range(len(packs)) for r in range(parts)]

    def enter(s, r):
        p = packs[s]
        at = slice(r * piece, (r + 1) * piece)
        w2 = jnp.concatenate([p[D : D + CHUNK, :], p[D + CHUNK : 2 * D, :]], axis=1)
        return dot(n2[at], p[:D, :], NN) + biases[s].astype(F32), dot(cot[at], w2, NT)

    ahead = enter(*units[0])
    for i, (s, r) in enumerate(units):
        inner, grad = ahead
        if i + 1 < len(units):
            ahead = enter(*units[i + 1])
        at = slice(r * piece, (r + 1) * piece)
        lanes = slice(s * CHUNK, (s + 1) * CHUNK)
        cdf, density = phi_terms(inner)
        act = (inner * cdf).astype(BF)
        act_buf[at, lanes] = act
        act_refs[s][at, :] = act
        gi_buf[at, lanes] = (grad * (cdf + inner * density)).astype(BF)
    w1 = jnp.concatenate([p[:D, :] for p in packs], axis=1)

    def rows_back(at):
        return dot(gi_buf[at], w1, NT)

    def first_grad():
        first = dot(n2T, gi_buf[...], NN)
        for s, ref in enumerate(grad_refs):
            at = slice(s * CHUNK, (s + 1) * CHUNK)
            ref[:D, :] = first[:D, at].astype(BF)
            bias_ref[s : s + 1, :] = first[D : D + 1, at]

    def second_grad():
        second = dot(act_buf[...], cot, TN).astype(BF)
        for s, ref in enumerate(grad_refs):
            at = slice(s * CHUNK, (s + 1) * CHUNK)
            ref[D : D + CHUNK, :] = second[at, :CHUNK]
            ref[D + CHUNK : 2 * D, :] = second[at, CHUNK:]

    return rows_back, first_grad, second_grad


def finish_slots(back_ref, back_in, steps):
    rows_back, first_grad, second_grad = steps
    everything = slice(0, back_ref.shape[0])
    back = rows_back(everything)
    back_ref[...] = back if back_in is None else back + back_in[...]
    first_grad()
    second_grad()


def expand_biases(first, *packs):
    return [p[D + 1 : D + 2, first : first + CHUNK] for p in packs]


def ff_kernel(n2_ref, n2T_ref, cot_ref, p0, p1, pa0, pa1, back_in, back_ref, g0, g1, act0, act1, bias_ref, act_buf, gi_buf):
    steps = ff_slots(n2_ref[...], n2T_ref[...], cot_ref[...], (p0, p1), expand_biases(0, pa0, pa1), (g0, g1), (act0, act1), bias_ref,
                     act_buf, gi_buf)
    finish_slots(back_ref, back_in, steps)


def ff_first_kernel(n2_ref, n2T_ref, cot_ref, p0, c0, c1, c2, pa0, pa1, back_ref, g0, d0, d1, act0, act1, bias_ref, act_buf, gi_buf):
    steps = ff_slots(n2_ref[...], n2T_ref[...], cot_ref[...], (p0, Rows(c0, c1, c2)), expand_biases(0, pa0, pa1), (g0, Rows(d0, d1)),
                     (act0, act1), bias_ref, act_buf, gi_buf)
    finish_slots(back_ref, None, steps)


def turn_kernel(n2_ref, n2T_ref, cot_ref, p0, p1, p2, p3, back_in, hidden_ref, m0, m1, m2, m3, pa0, pa1, pa2, pa3, small_in,
                gh_ref, dT0, dT1, dT2, dT3, g0, g1, g2, g3, o0, o2, o_send, act0, act1, act2, act3, bias_ref, small_ref,
                act_buf, gi_buf, low_buf):
    local = m0.shape[0]
    rows_back, first_grad, second_grad = ff_slots(
        n2_ref[...], n2T_ref[...], cot_ref[...], (p0, p1, p2, p3), expand_biases(CHUNK, pa0, pa1, pa2, pa3), (g0, g1, g2, g3),
        (act0, act1, act2, act3), bias_ref, act_buf, gi_buf)
    total = [0.0] * 4
    between = {0: first_grad, 1: second_grad}
    for r in range(hidden_ref.shape[0] // CHUNK):
        at = slice(r * CHUNK, (r + 1) * CHUNK)
        back = rows_back(at) + back_in[at, :]
        if r in between:
            between[r]()
        cot_f = cot_ref[at, :].astype(F32)
        xhat, scale = norm_terms(hidden_ref[at, :])
        grad_hidden = cot_f + norm_back(back, small_in[3:4, :], xhat, scale)
        gh_ref[at, :] = grad_hidden
        low_buf[at, :] = grad_hidden.astype(BF)
        for k, value in enumerate((grad_hidden, back * xhat, back, cot_f)):
            total[k] = total[k] + jnp.sum(value, axis=0, keepdims=True)
    for k in range(4):
        small_ref[k : k + 1, :] = total[k]
    low = low_buf[...]
    weight = jnp.concatenate([p[:D, 3 * local :] for p in (pa0, pa1, pa2, pa3)], axis=1)
    grads_T = dot(weight, low, TT).astype(BF)
    for s, ref in enumerate((dT0, dT1, dT2, dT3)):
        ref[...] = grads_T[s * local : (s + 1) * local]
    mixed = jnp.concatenate([m[...].astype(BF) for m in (m0, m1, m2, m3)], axis=0)
    grad = dot(mixed, low, NN).astype(BF)
    for s, (ref, first) in enumerate(((o0, 0), (o_send, 0), (o2, 0), (o_send, 2 * local))):
        for part in range(2):
            at = first + part * local
            ref[at : at + local, :] = grad[s * local : (s + 1) * local, part * CHUNK : (part + 1) * CHUNK]


def attention_backward(e_ref, dT_ref, inv_ref, mixed_ref, vT_ref, qT_ref, kT_ref, nT_ref, dq_ref, dkv_ref, grad_ref, bias_ref,
                       ds_buf):
    rows = qT_ref.shape[1]
    keys = kT_ref.shape[1]
    local = qT_ref.shape[0]
    heads = local // HEAD
    blocks = [(h, c) for h in range(heads) for c in range(rows // CHUNK)]
    which = lax.broadcasted_iota(jnp.int32, (EXTRA, CHUNK), 0)
    ones2 = (lax.broadcasted_iota(jnp.int32, (EXTRA, 2 * CHUNK), 0) < 2).astype(F32).astype(BF)
    lows = {}

    def enter(i):
        h, c = blocks[i]
        here = slice(h * HEAD, (h + 1) * HEAD)
        columns = slice(c * CHUNK, (c + 1) * CHUNK)
        low = (dT_ref[here, columns].astype(F32) * inv_ref[h : h + 1, columns]).astype(BF)
        delta = jnp.sum(low.astype(F32) * mixed_ref[here, columns], axis=0, keepdims=True)
        high = (-delta).astype(BF).astype(F32)
        extra = jnp.where(which == 0, high, jnp.where(which == 1, -delta - high, 0.0)).astype(BF)
        more = jnp.concatenate([low, extra], axis=0)
        lows[i] = low
        for k in range(keys // (2 * CHUNK)):
            span = slice(k * 2 * CHUNK, (k + 1) * 2 * CHUNK)
            v = jnp.concatenate([vT_ref[here, span], ones2], axis=0)
            ds_buf[i % 2, span, :] = (e_ref[h, c, span, :].astype(F32) * dot(v, more, TN)).astype(BF)

    dv = None
    dk = None
    enter(0)
    for i, (h, c) in enumerate(blocks):
        if i + 1 < len(blocks):
            enter(i + 1)
        here = slice(h * HEAD, (h + 1) * HEAD)
        columns = slice(c * CHUNK, (c + 1) * CHUNK)
        part = dot(lows[i], e_ref[h, c], NT)
        dv = part if c == 0 else dv + part
        dq_ref[here, columns] = (dot(kT_ref[here, :], ds_buf[i % 2], NN) * HEAD**-0.5).astype(BF)
        part = dot(qT_ref[here, columns], ds_buf[i % 2], NT)
        dk = part if c == 0 else dk + part
        if c == rows // CHUNK - 1:
            dkv_ref[here, :] = dk.astype(BF)
            dkv_ref[local + h * HEAD : local + (h + 1) * HEAD, :] = dv.astype(BF)
    for ref, count, columns in ((dq_ref, rows, slice(0, local)), (dkv_ref, keys, slice(local, 3 * local))):
        grad = dot(nT_ref[:, :count], ref[...], NT)
        grad_ref[:, columns] = grad[:D].astype(BF)
        bias_ref[:, columns] = grad[D : D + 1]


def first_kernel(half, x_ref, xs_ref, pa0, pa1, pa2, pa3, *rest):
    sources = rest[:8]
    small_two, b0, b1, b2, b3, f00, f01, f1, own_ref, sib_ref, small_ref = rest[8:]
    local = pa0.shape[1] // TENSOR
    rows = own_ref.shape[0]
    device = lax.axis_index("tensor")
    small_ref[...] = jnp.zeros(small_ref.shape, F32)
    gain_sum = 0.0
    shift_sum = 0.0
    for part, ref in enumerate((x_ref, xs_ref)):
        columns = slice(part * rows, (part + 1) * rows)
        total = None
        for slot, p in enumerate((pa0, pa1, pa2, pa3)):
            for index, lanes in ((0, slice(0, local)), (1, slice(local, 3 * local)))[part:]:
                term = dot(sources[slot * 2 + index][:, columns], p[:D, lanes], TT)
                total = term if total is None else total + term
        if part == 0:
            own_ref[...] = total
        else:
            sib_ref[...] = total.astype(BF)
        xhat, _ = norm_terms(ref[:half, :].astype(F32))
        gain_sum = gain_sum + jnp.sum(total[:half] * xhat, axis=0, keepdims=True)
        shift_sum = shift_sum + jnp.sum(total, axis=0, keepdims=True)
    small_ref[0:4, :] = small_two[...]
    small_ref[4:5, :] = gain_sum
    small_ref[5:6, :] = shift_sum
    for slot, b in enumerate((b0, b1, b2, b3)):
        owner = jnp.bitwise_xor(device, slot)
        small_ref[pl.ds(8 + owner, 1), :] = jnp.concatenate(
            [(f00, f01)[slot // 2][slot % 2 : slot % 2 + 1, :], f1[slot : slot + 1, :]], axis=1
        )
        small_ref[pl.ds(12 + owner, 1), : 3 * local] = b[...]


def branch_kernel(hidden_ref, small_ref, *rest):
    *refs, out_ref = rest
    acts, packs = refs[: 2 * TENSOR], refs[2 * TENSOR :]
    packs = packs[:3] + [Rows(*packs[3:6])] + packs[6:]
    act = jnp.concatenate([a[...] for a in acts], axis=1)
    weight = jnp.concatenate(
        [jnp.concatenate([p[D : D + CHUNK, :], p[D + CHUNK : 2 * D, :]], axis=1) for p in packs], axis=0
    )
    total = hidden_ref[...] + dot(act, weight, NN) + small_ref[5:6, :]
    out_ref[...] = total[: out_ref.shape[0]].astype(BF)


def last_kernel(x_ref, own_ref, got_ref, gh_ref, small_ref, out_ref):
    half = out_ref.shape[0]
    grad = own_ref[:half, :] + got_ref[:half, :].astype(F32)
    xhat, scale = norm_terms(x_ref[:half, :].astype(F32))
    out_ref[...] = gh_ref[:half, :] + norm_back(grad, small_ref[0:1, :], xhat, scale)


def place_of(bit):
    return lax.rem(lax.div(lax.axis_index("dp"), bit), 2)


def merge(kept, got, buf, bit=1):
    rows = kept.shape[0]
    upper = place_of(bit)
    buf[pl.ds(pl.multiple_of(upper * rows, rows), rows), :] = kept[...].astype(F32)
    buf[pl.ds(pl.multiple_of((1 - upper) * rows, rows), rows), :] = got[...].astype(F32)


def finish_ff_kernel(first, kept, got, expand_ref, reduce_ref, out_ref, second):
    local = out_ref.shape[0]
    merge(kept, got, second)
    for index, ref in enumerate((first, second)):
        lanes = slice(index * CHUNK, (index + 1) * CHUNK)
        expand_ref[:, lanes] = ref[:D, :].astype(F32)
        for part in range(2):
            rows = slice(D + part * CHUNK, D + (part + 1) * CHUNK)
            reduce_ref[lanes, part * CHUNK : (part + 1) * CHUNK] = ref[rows, :].astype(F32)
    for part in range(2):
        rows = slice(2 * D + part * local, 2 * D + (part + 1) * local)
        out_ref[:, part * CHUNK : (part + 1) * CHUNK] = second[rows, :]


def finish_qkv_kernel(kept, got, sums_ref, more_ref, q_ref, k_ref, v_ref, bias_q, bias_v, bias_ff, s0, s1, s2, s3, s4, s5, sums):
    half, local = kept.shape[0], q_ref.shape[1]
    upper = place_of(1)
    for index, ref in enumerate((q_ref, k_ref, v_ref)):
        lanes = slice(index * local, (index + 1) * local)
        ref[pl.ds(pl.multiple_of(upper * half, half), half), :] = kept[:, lanes].astype(F32)
        ref[pl.ds(pl.multiple_of((1 - upper) * half, half), half), :] = got[:, lanes].astype(F32)
        ref.flush()
    sums[...] = sums_ref[...] + more_ref[...]
    device = lax.axis_index("tensor")
    for index, ref in enumerate((s0, s1, s2, s3, s4, s5)):
        ref[...] = sums[index : index + 1, :].reshape(D)
    bias_ff[...] = sums[pl.ds(8 + device, 1), :].reshape(D)
    both = sums[pl.ds(12 + device, 1), :]
    bias_q[...] = both[:, :local].reshape(local)
    bias_v[...] = both[:, 2 * local : 3 * local].reshape(local)


class Chain:
    def __init__(self, along, size, halvings, pieces):
        bits = [1 << i for i in range(size.bit_length() - 1)]
        halvings = min(halvings, len(bits))
        self.along = along
        self.plan = [("half", b) for b in bits[:halvings]] + [("full", b) for b in bits[halvings:]]
        self.plan += [("back", b) for b in reversed(bits[:halvings])]
        self.at = -1
        self.pieces = pieces

    def left(self):
        return len(self.plan) - 1 - self.at

    def last(self):
        return tuple(self.pieces[0])

    def due(self):
        kind, bit = self.plan[self.at + 1]
        if kind == "half":
            return "halves", self.pieces, bit
        if self.at >= 0 and self.plan[self.at][0] == "back":
            return ("merge",) + tuple(self.pieces[0]) + (self.plan[self.at][1],)
        return "sum", self.pieces

    def taken(self, *results):
        self.at += 1
        send, keep = results if len(results) == 2 else results * 2
        self.pieces = [(keep, self.along(send, self.plan[self.at][1]))]


def swap(value, axis, size, bit):
    return lax.ppermute(value, axis, [(i, i ^ bit) for i in range(size)])


def on_device(dp, frames, query_weight, query_bias, key_weight, value_weight, value_bias, out_weight, out_bias, first_gain, first_shift,
              expand_weight, expand_bias, reduce_weight, reduce_bias, second_gain, second_shift, span_start, span_end, empty_flag, cotangent):
    half = frames.shape[0]
    rows = -(-half // CHUNK) * CHUNK
    keys = 2 * rows
    local = query_weight.shape[1]
    heads = local // HEAD
    blocks = rows // CHUNK
    line = Line()

    def across(v, bit):
        return swap(v, "tensor", TENSOR, bit)

    def along(v, bit):
        return swap(v, "dp", dp, bit)

    xs = across(frames, 1)
    pa0, small = line.run(
        pack_kernel, (shaped(D + EXTRA, 4 * local), shaped(8, D, dtype=F32)), "f" * 13,
        (query_weight, key_weight, value_weight, out_weight, query_bias, value_bias, expand_bias,
         first_gain, first_shift, out_bias, second_gain, second_shift, reduce_bias), us=2,
    )
    pa2 = across(pa0, 2)
    pa1 = across(pa0, 1)

    forward_outs = (
        (shaped(heads, blocks, keys, CHUNK), "V"), shaped(local, rows), shaped(local, keys), shaped(local, keys),
        shaped(local, rows, dtype=F32), shaped(heads, rows, dtype=F32),
    )
    forward_scratch = (
        pltpu.VMEM((2, keys, CHUNK), F32),
    )
    spans = (span_start, span_end, empty_flag)
    ff_weights = (expand_weight, reduce_weight)
    ff_shape = shaped(2 * D, CHUNK)
    normed, ff0, x, *s0 = line.run(
        functools.partial(start_kernel, half), (shaped(D + EXTRA, keys), ff_shape, shaped(rows, D)) + forward_outs, "sssfvvvff",
        spans + (frames, xs, small, pa0) + ff_weights, forward_scratch + (pltpu.VMEM((2, rows, D), BF),), us=8,
    )
    ff0_far = across(ff0, 2)
    ff0_near = across(ff0, 1)
    cot, ff1, *s1 = line.run(
        functools.partial(near_kernel, half), (shaped(rows, D), ff_shape) + forward_outs, "sssvvfff",
        spans + (normed, pa1, cotangent) + ff_weights, forward_scratch, us=7,
    )
    pa3 = [across(v, 1) for v in line.tick(("sum", [((pa2, 0, CHUNK),)]), ("sum", [((pa2, CHUNK, D + EXTRA - CHUNK),)]))]
    s2 = line.run(
        functools.partial(attention_forward, half), forward_outs, "sssvv", spans + (normed, pa2), forward_scratch, us=7,
    )
    ff1 = line.touch(ff1)
    ff1_far = across(ff1, 2)
    pa3, *s3 = line.run(
        functools.partial(cross_kernel, half), (shaped(D + EXTRA, 4 * local),) + forward_outs, "sssvvv",
        spans + (normed, *pa3), forward_scratch, us=7,
    )
    slots = (s0, s1, s2, s3)
    mixed = tuple(s[4] for s in slots)
    packs = (pa0, pa1, pa2, pa3)
    cuts = [(0, 384), (384, 320), (704, 320)]
    ff0_cross = [across(v, 1) for v in line.tick(*(("sum", [((ff0_far,) + cut,)]) for cut in cuts))]
    whole = shaped(rows, D, dtype=F32)
    hidden, n2, n2T = line.run(
        out_kernel, (whole, shaped(rows, D), shaped(D + EXTRA, rows)), "v" * 10,
        (x,) + mixed + packs + (small,), us=8,
    )
    ff1_near = across(ff1, 1)
    ff_scratch = (pltpu.VMEM((rows, TENSOR * CHUNK), BF), pltpu.VMEM((rows, TENSOR * CHUNK), BF))
    bias_shape = shaped(TENSOR, CHUNK, dtype=F32)
    ff_grads = (shaped(2 * D, CHUNK),) * TENSOR
    ff_acts = (shaped(rows, CHUNK),) * TENSOR
    two = (whole,) + ff_grads[:2] + ff_acts[:2] + (shaped(2, CHUNK, dtype=F32),)
    half_scratch = (pltpu.VMEM((rows, 2 * CHUNK), BF), pltpu.VMEM((rows, 2 * CHUNK), BF))
    back, a2, *a3, act2, act3, bias_far = line.run(
        ff_first_kernel, two[:2] + (shaped(D, CHUNK),) * 2 + two[3:], "v" * 9, (n2, n2T, cot, ff0_far, *ff0_cross, pa2, pa3), half_scratch,
        us=4, vmem=10,
    )
    got_a3 = [across(v, 1) for v in a3]
    back, a0, a1, act0, act1, bias_near = line.run(
        ff_kernel, two, "v" * 8, (n2, n2T, cot, ff0, ff0_near, pa0, pa1, back), half_scratch, us=4, vmem=10,
    )
    acts_a, bias_a = (act0, act1, act2, act3), (bias_near, bias_far)
    got_a1 = across(a1, 1)
    spare = jnp.zeros((EXTRA, CHUNK), BF)
    (far_a,) = line.tick(("sum", [((a2, i * D, D), v) for i, v in enumerate(got_a3)] + [(spare,)]))
    y_a = across(far_a, 2)
    ff1_far = line.touch(ff1_far)
    ff1_cross = across(ff1_far, 1)
    size_b = 2 * D + 2 * local
    grad_hidden, *rest = line.run(
        turn_kernel,
        ((whole, "V"),) + (shaped(local, rows),) * TENSOR + ff_grads
        + (shaped(2 * local, CHUNK), shaped(2 * local, CHUNK), shaped(4 * local, CHUNK)) + ff_acts + (bias_shape, shaped(4, D, dtype=F32)),
        "v" * 18,
        (n2, n2T, cot, ff1, ff1_near, ff1_far, ff1_cross, back, hidden) + mixed + packs + (small,),
        ff_scratch + (pltpu.VMEM((rows, D), BF),), us=12, vmem=11,
    )
    dT, (f0, f1, f2, f3, o0, o2, o_send) = rest[:TENSOR], rest[TENSOR : TENSOR + 7]
    acts_b, (bias_b, small_two) = rest[TENSOR + 7 : 2 * TENSOR + 7], rest[2 * TENSOR + 7 :]
    got_f1 = across(f1, 1)
    got_f3 = across(f3, 1)
    got_o = across(o_send, 1)

    backward_outs = (
        shaped(local, rows), shaped(2 * local, keys), shaped(D, 3 * local), shaped(1, 3 * local, dtype=F32),
    )

    def backward(slot):
        e, q, k, v, m, inv = slots[slot]
        return line.run(
            attention_backward, backward_outs, "V" + "v" * 7,
            (e, dT[slot], inv, m, v, q, k, normed), (pltpu.VMEM((2, keys, CHUNK), BF),), us=8, vmem=5,
        )

    def chain(halvings, pieces):
        return Chain(along, dp, halvings, pieces)

    *d3, g3, b3 = backward(3)
    chain_a = chain(1, [(a0, got_a1, (y_a, 0, 2 * D))])
    pair = 2 * local
    far_b, send_3, *halves = line.tick(
        ("sum", [(f2, got_f3), (o2, (got_o, pair, pair))]), ("sum", [(g3,)]), chain_a.due()
    )
    y_b = across(far_b, 2)
    got_3 = across(send_3, 1)
    chain_a.taken(*halves)
    *d2, g2, b2 = backward(2)
    spare = jnp.zeros((EXTRA, 3 * local), BF)
    far_q, whole_a = line.tick(("sum", [(g2, got_3), (spare,)]), chain_a.due())
    y_q = across(far_q, 2)
    chain_a.taken(whole_a)
    *d1, g1, b1 = backward(1)
    chain_b = chain(2, [(f0, got_f1, (y_b, 0, 2 * D)), (o0, (got_o, 0, pair), (y_b, 2 * D, pair))])
    send_1, whole_a, *halves = line.tick(("sum", [(g1,)]), chain_a.due(), chain_b.due())
    got_1 = across(send_1, 1)
    chain_a.taken(whole_a)
    chain_b.taken(*halves)
    *d0, g0, b0 = backward(0)
    chain_q = chain(2, [(g0, got_1, (y_q, 0, D))])
    send_q, keep_q, send_b, keep_b = line.tick(chain_q.due(), chain_b.due())
    chain_q.taken(send_q, keep_q)
    chain_b.taken(send_b, keep_b)
    own, sib, sums = line.run(
        functools.partial(first_kernel, half), (whole, shaped(rows, D), shaped(16, D, dtype=F32)), "v" * 22,
        (x, xs) + packs + (*d0, *d1, *d2, *d3, small_two, b0, b1, b2, b3) + bias_a + (bias_b,), us=6,
    )
    (sums,) = line.tick(("sum", [(sums,)]))
    pending = across(sums, 1)
    chain_q.taken(*line.tick(chain_q.due()))
    part_b, part_a, sums, sib = line.tick(chain_b.due(), chain_a.due(), ("sum", [(sums, pending)]), ("sum", [(sib,)]))
    chain_b.taken(part_b)
    chain_a.taken(part_a)
    pending = across(sums, 2)
    got = across(sib, 1)
    (grad_frames,) = line.run(
        last_kernel, ((shaped(half, D, dtype=F32), "f"),), "vvvVv", (x, own, got, grad_hidden, small), us=4
    )
    bits = [1 << i for i in range(dp.bit_length() - 1)]

    def step(*chains, more=()):
        nonlocal sums, pending
        chains = [c for c in chains if c.left()]
        with_sums = bool(bits)
        jobs = [c.due() for c in chains] + [("sum", [(sums, pending)])] * with_sums + list(more)
        if not jobs:
            return ()
        made = list(line.tick(*jobs))
        for c in chains:
            c.taken(made.pop(0))
        if with_sums:
            sums = made.pop(0)
            pending = along(sums, bits.pop(0))
        return made

    step(chain_q, chain_b, chain_a)
    (output,) = line.run(
        branch_kernel, ((shaped(half, D), "f"),), "v" * 20,
        (hidden, small) + tuple(acts_a) + tuple(acts_b) + (ff0, ff0_near, ff0_far, *ff0_cross, ff1, ff1_near, ff1_far, ff1_cross), us=3,
    )
    while chain_a.left() or chain_b.left() > 1:
        step(chain_q, chain_b, chain_a)
    (whole_a,) = step(chain_q, chain_b, more=(("merge",) + chain_a.last() + (1,),))
    while bits or chain_q.left():
        step(chain_q)
    grad_expand, grad_reduce, grad_out = line.run(
        finish_ff_kernel, tuple((shaped(*o, dtype=F32), "f") for o in ((D, 2 * CHUNK), (2 * CHUNK, D), (local, D))),
        "vvv", (whole_a,) + chain_b.last(), (pltpu.VMEM((size_b, CHUNK), F32),), us=2,
    )
    vector = (shaped(D, dtype=F32), "f")
    short = (shaped(local, dtype=F32), "f")
    grad_q, grad_k, grad_v, bias_q, bias_v, bias_ff, *globals_ = line.run(
        finish_qkv_kernel, ((shaped(D, local, dtype=F32), "f"),) * 3 + (short, short, vector) + (vector,) * 6, "vvvv",
        chain_q.last() + (sums, pending), (pltpu.VMEM(sums.shape, F32),), us=1,
    )
    return (
        output, grad_frames, grad_q, bias_q, grad_k, grad_v, bias_v, grad_out, globals_[0], globals_[4], globals_[5],
        grad_expand, bias_ff, grad_reduce, globals_[3], globals_[1], globals_[2],
    )


def solution(mesh):
    dp = mesh.shape["dp"]
    assert mesh.shape["tensor"] == TENSOR and dp & (dp - 1) == 0
    split = P(("dp", "tensor"), None)
    column = P(None, "tensor")
    return jax.shard_map(
        functools.partial(on_device, dp),
        mesh=mesh,
        in_specs=(
            split, column, P("tensor"), column, column, P("tensor"), P("tensor", None), P(), P(), P(),
            column, P("tensor"), P("tensor", None), P(), P(), P(), P("dp"), P("dp"), P("dp"), split,
        ),
        out_specs=(
            split, split, column, P("tensor"), column, column, P("tensor"), P("tensor", None), P(), P(), P(),
            column, P("tensor"), P("tensor", None), P(), P(), P(),
        ),
        check_vma=False,
    )
```

```python
import functools

import jax
import jax.numpy as jnp
from jax import lax
from jax.experimental import pallas as pl
from jax.experimental.pallas import tpu as pltpu
from jax.sharding import PartitionSpec as P

BF = jnp.bfloat16
F32 = jnp.float32
D = 512
HEADS = 8
HEAD = D // HEADS
EPS = 1e-05
TENSOR = 4
CHUNK = 256
EXTRA = 16
LANES = 128
NN = (((1,), (0,)), ((), ()))
NT = (((1,), (1,)), ((), ()))
TN = (((0,), (0,)), ((), ()))
TT = (((0,), (1,)), ((), ()))
VMEM = pl.BlockSpec(memory_space=pltpu.VMEM)
SMEM = pl.BlockSpec(memory_space=pltpu.SMEM)
ANY = pl.BlockSpec(memory_space=pl.ANY)


def dot(left, right, dims):
    return lax.dot_general(left, right, dims, preferred_element_type=F32)


class Fetched:
    def __init__(self, source, buffer, sem):
        self.buffer, self.shape, self.waited = buffer, buffer.shape, False
        self.copy = pltpu.make_async_copy(source, buffer, sem)
        self.copy.start()

    def __getitem__(self, index):
        if not self.waited:
            self.copy.wait()
            self.waited = True
        return self.buffer[index]


class Stored:
    def __init__(self, target, buffer, sem):
        self.buffer, self.shape, self.dtype, self.sent = buffer, buffer.shape, buffer.dtype, False
        self.copy = pltpu.make_async_copy(buffer, target, sem)

    def __getitem__(self, index):
        return self.buffer[index]

    def __setitem__(self, index, value):
        self.buffer[index] = value

    def flush(self):
        if not self.sent:
            self.copy.start()
            self.sent = True


HBM = pl.BlockSpec(memory_space=pltpu.HBM)
SPEC = {"f": HBM, "h": HBM, "s": HBM, "v": VMEM, "V": VMEM}
PINNED = {"f": pltpu.HBM, "h": pltpu.HBM, "s": pltpu.HBM, "V": pltpu.VMEM}


class Rows:
    def __init__(self, *refs):
        self.refs, self.at = refs, [0]
        for ref in refs:
            self.at.append(self.at[-1] + ref.shape[0])

    def spans(self, rows):
        first, last, _ = rows.indices(self.at[-1])
        for ref, low, high in zip(self.refs, self.at, self.at[1:]):
            if max(first, low) < min(last, high):
                yield ref, slice(max(first, low) - low, min(last, high) - low), slice(max(first, low) - first, min(last, high) - first)

    def __getitem__(self, index):
        parts = [ref[here, index[1]] for ref, here, _ in self.spans(index[0])]
        return parts[0] if len(parts) == 1 else jnp.concatenate(parts, axis=0)

    def __setitem__(self, index, value):
        for ref, here, there in self.spans(index[0]):
            ref[here, index[1]] = value[there]


class Line:
    def __init__(self):
        self.waits = ()

    def run(self, kernel, outs, ins, args, scratch=(), us=8, vmem=12):
        waits = self.waits
        outs = [o if isinstance(o, tuple) else (o, "v") for o in outs]
        kinds = list(ins)
        skip, last = len(kinds), len(outs)
        moved = [i for i, k in enumerate(kinds) if k in "fs"]
        built = [i for i, (_, k) in enumerate(outs) if k == "f"]
        space = {"f": pltpu.VMEM, "s": pltpu.SMEM}
        buffers = [space[kinds[i]](args[i].shape, args[i].dtype) for i in moved] + [pltpu.VMEM(outs[i][0].shape, outs[i][0].dtype) for i in built]

        def body(*refs):
            inputs = list(refs[:skip])
            rest = refs[skip + len(waits) :]
            results, zeros, rest = list(rest[:last]), rest[last], rest[last + 1 :]
            held, sems, rest = rest[: len(buffers)], rest[len(buffers)], rest[len(buffers) + 1 :]
            for n, i in enumerate(moved):
                inputs[i] = Fetched(inputs[i], held[n], sems.at[n])
            for n, i in enumerate(built, len(moved)):
                results[i] = Stored(results[i], held[n], sems.at[n])
            zeros[...] = jnp.zeros((8, 128), F32)
            kernel(*inputs, *results, *rest)
            for i in built:
                results[i].flush()
            for i in moved:
                if not inputs[i].waited:
                    inputs[i].copy.wait()
            for i in built:
                results[i].copy.wait()

        *got, zeros = pl.pallas_call(
            body,
            out_shape=tuple(PINNED[k](o.shape, o.dtype) if k in PINNED else o for o, k in outs) + (jax.ShapeDtypeStruct((8, 128), F32),),
            in_specs=[SPEC[k] for k in kinds] + [ANY] * len(waits),
            out_specs=[SPEC[k] for _, k in outs] + [VMEM],
            scratch_shapes=buffers + [pltpu.SemaphoreType.DMA((len(buffers) + 1,))] + list(scratch),
            compiler_params=pltpu.CompilerParams(vmem_limit_bytes=vmem * 2**20),
            cost_estimate=pl.CostEstimate(flops=10**6, bytes_accessed=2**10, transcendentals=0),
        )(*(pltpu.with_memory_space_constraint(a, PINNED[k]) if k in PINNED else a for a, k in zip(args, kinds)), *waits)
        self.waits = (zeros,)
        return got

    def touch(self, value):
        waits = self.waits
        got = (
            pl.pallas_call(
                lambda given, *rest: None,
                out_shape=jax.ShapeDtypeStruct(value.shape, value.dtype),
                in_specs=[ANY] * (1 + len(waits)),
                out_specs=ANY,
                input_output_aliases={0: 0},
                compiler_params=pltpu.CompilerParams(vmem_limit_bytes=2**20),
                cost_estimate=pl.CostEstimate(flops=10**6, bytes_accessed=1024, transcendentals=0),
            )(value, *waits)
        )
        self.waits = self.waits + (got,)
        return got

    def tick(self, *jobs):
        args, outs, scratch, plans = [], [], [], []

        def place(part):
            array, first, rows = part if isinstance(part, tuple) else (part, 0, part.shape[0])
            args.append(array)
            return len(args) - 1, first, rows

        for kind, *rest in jobs:
            pieces = [[place(part) for part in piece] for piece in ([[p] for p in rest[:2]] if kind == "merge" else rest[0])]
            rows = sum(piece[0][2] for piece in pieces)
            like = args[pieces[0][0][0]]
            columns = like.shape[1:]
            plans.append((kind, pieces, len(outs), len(scratch), rest[-1]))
            if kind == "halves":
                outs += [shaped(rows // 2, *columns)] * 2
            else:
                outs.append(jax.ShapeDtypeStruct((rows, *columns), like.dtype))
            if kind != "sum":
                scratch.append(pltpu.VMEM((rows, *columns), F32))

        def body(*refs):
            ins, results, buffers = refs[: len(args)], refs[len(args) : len(args) + len(outs)], refs[len(args) + len(outs) :]
            for kind, pieces, out, held, bit in plans:
                if kind == "merge":
                    kept, got = (ins[piece[0][0]] for piece in pieces)
                    merge(kept, got, buffers[held], bit)
                    results[out][...] = buffers[held][...].astype(results[out].dtype)
                    continue
                target = buffers[held] if kind == "halves" else results[out]
                at = 0
                for piece in pieces:
                    count = piece[0][2]
                    total = sum(ins[i][first : first + count].astype(F32) for i, first, _ in piece)
                    target[at : at + count] = total.astype(target.dtype)
                    at += count
                if kind == "halves":
                    half = at // 2
                    upper = place_of(bit)
                    results[out][...] = target[pl.ds(pl.multiple_of((1 - upper) * half, half), half), :].astype(BF)
                    results[out + 1][...] = target[pl.ds(pl.multiple_of(upper * half, half), half), :].astype(BF)

        return self.run(body, outs, "v" * len(args), args, scratch, us=1, vmem=6)


def shaped(*shape, dtype=BF):
    return jax.ShapeDtypeStruct(shape, dtype)


def norm_terms(rows_in):
    center = jnp.mean(rows_in, axis=-1, keepdims=True)
    centered = rows_in - center
    spread = jnp.mean(centered * centered, axis=-1, keepdims=True)
    scale = lax.rsqrt(spread + EPS)
    return centered * scale, scale


def norm_back(grad, gain, xhat, scale):
    e = grad * gain
    mean_e = jnp.mean(e, axis=-1, keepdims=True)
    mean_ex = jnp.mean(e * xhat, axis=-1, keepdims=True)
    return scale * (e - mean_e - xhat * mean_ex)


def valid_row(start_ref, end_ref, empty_ref, rows, half):
    lane = lax.broadcasted_iota(jnp.int32, (1, 2 * rows), 1)
    second = lane >= rows
    local = jnp.where(second, lane - rows, lane)
    device = lax.axis_index("tensor")
    clip = device // 2
    core = device % 2
    position = local + half * jnp.where(second, 1 - core, core)
    inside = (position >= start_ref[clip]) & (position < end_ref[clip])
    return (local < half) & jnp.logical_not(inside) & (empty_ref[clip] == 0)


def attention_forward(half, start_ref, end_ref, empty_ref, nT_ref, pack, e_ref, qT_ref, kT_ref, vT_ref, mixed_ref, inv_ref, s_buf,
                      prepare=None):
    rows = qT_ref.shape[1]
    keys = kT_ref.shape[1]
    local = qT_ref.shape[0]
    heads = local // HEAD
    first_row = lax.broadcasted_iota(jnp.int32, (EXTRA, keys), 0) == 0
    ones16 = first_row.astype(F32).astype(BF)

    def project(first, last, columns):
        product = dot(pack[:D, first * local : last * local], nT_ref[:D, columns], TN)
        bias = dot(pack[D:, first * local : last * local], ones16[:, :LANES], TN)
        return (product + jnp.concatenate([bias] * (rows // LANES), axis=1)).astype(BF)

    for part in (1, 0):
        columns = slice(part * rows, (part + 1) * rows)
        if prepare is not None:
            prepare(part)
        both = project(1, 3, columns)
        kT_ref[:, columns] = both[:local]
        vT_ref[:, columns] = both[local:]
    qT_ref[...] = (project(0, 1, slice(0, rows)).astype(F32) * HEAD**-0.5).astype(BF)

    valid = valid_row(start_ref, end_ref, empty_ref, rows, half)
    some = jnp.max(valid.astype(F32), axis=1, keepdims=True)
    mask = jnp.where(first_row, jnp.where(valid, 0.0, -1e30), 0.0).astype(BF)

    blocks = [(h, c) for h in range(heads) for c in range(rows // CHUNK)]
    tops = {}

    def score(i):
        h, c = blocks[i]
        q = jnp.concatenate([qT_ref[h * HEAD : (h + 1) * HEAD, c * CHUNK : (c + 1) * CHUNK], ones16[:, :CHUNK]], axis=0)
        top = None
        for k in range(keys // CHUNK):
            span = slice(k * CHUNK, (k + 1) * CHUNK)
            s = dot(jnp.concatenate([kT_ref[h * HEAD : (h + 1) * HEAD, span], mask[:, span]], axis=0), q, TN)
            s_buf[i % 2, span, :] = s
            part = jnp.max(s.reshape(CHUNK // 8, 8, CHUNK), axis=0)
            top = part if top is None else jnp.maximum(top, part)
        tops[i] = jnp.max(top, axis=0, keepdims=True)

    score(0)
    for i, (h, c) in enumerate(blocks):
        if i + 1 < len(blocks):
            score(i + 1)
        columns = slice(c * CHUNK, (c + 1) * CHUNK)
        for k in range(keys // CHUNK):
            span = slice(k * CHUNK, (k + 1) * CHUNK)
            e_ref[h, c, span, :] = jnp.exp(s_buf[i % 2, span, :] - tops[i]).astype(BF)
        value = jnp.concatenate([vT_ref[h * HEAD : (h + 1) * HEAD, :], jnp.ones((EXTRA, keys), BF)], axis=0)
        o = dot(value, e_ref[h, c], NN)
        inv = some / o[HEAD : HEAD + 1, :]
        mixed_ref[h * HEAD : (h + 1) * HEAD, columns] = o[:HEAD] * inv
        inv_ref[h : h + 1, columns] = inv


def ff_pack(first, w1_ref, w2_ref, out_ref):
    out_ref[:D, :] = w1_ref[:, first : first + CHUNK]
    for part in range(2):
        out_ref[D + part * CHUNK : D + (part + 1) * CHUNK, :] = w2_ref[first : first + CHUNK, part * CHUNK : (part + 1) * CHUNK]


def pack_kernel(wq, wk, wv, wo, bq, bv, b1, g1, s1, ob, g2, s2, rb, pack_ref, small_ref):
    local = wq.shape[1]
    for index, ref in enumerate((wq, wk, wv)):
        pack_ref[:D, index * local : (index + 1) * local] = ref[...]
    pack_ref[:D, 3 * local :] = wo[...].T
    pack_ref[D:, :] = jnp.zeros((EXTRA, 4 * local), BF)
    pack_ref[D : D + 1, :local] = bq[...].reshape(1, local)
    pack_ref[D : D + 1, 2 * local : 3 * local] = bv[...].reshape(1, local)
    pack_ref[D + 1 : D + 2, :] = b1[...].reshape(1, 4 * local)
    for index, ref in enumerate((g1, s1, ob, g2, s2, rb)):
        small_ref[index : index + 1, :] = ref[...].astype(F32).reshape(1, D)


def start_kernel(half, start_ref, end_ref, empty_ref, x_ref, xs_ref, small_ref, pack, w1_ref, w2_ref, nT_ref, ff_ref, pad_ref, *rest):
    *rest, n_buf = rest
    rows = n_buf.shape[1]
    gain = small_ref[0:1, :]
    shift = small_ref[1:2, :]
    nT_ref[D:, :] = (lax.broadcasted_iota(jnp.int32, (EXTRA, 2 * rows), 0) == 0).astype(F32).astype(BF)

    def prepare(part):
        xhat, _ = norm_terms((x_ref, xs_ref)[part][...].astype(F32))
        n_buf[part, :half, :] = (xhat * gain + shift).astype(BF)
        n_buf[part, half:, :] = jnp.zeros((rows - half, D), BF)
        nT_ref[:D, part * rows : (part + 1) * rows] = n_buf[part].T

    attention_forward(half, start_ref, end_ref, empty_ref, nT_ref, pack, *rest, prepare=prepare)
    ff_pack(0, w1_ref, w2_ref, ff_ref)
    pad_ref[half:, :] = jnp.zeros((rows - half, D), BF)
    pad_ref[:half, :] = x_ref[...]


def near_kernel(half, start_ref, end_ref, empty_ref, nT_ref, pack, cot_ref, w1_ref, w2_ref, pad_ref, ff_ref, *rest):
    attention_forward(half, start_ref, end_ref, empty_ref, nT_ref, pack, *rest)
    pad_ref[half:, :] = jnp.zeros((pad_ref.shape[0] - half, D), BF)
    pad_ref[:half, :] = cot_ref[...]
    ff_pack(CHUNK, w1_ref, w2_ref, ff_ref)


def cross_kernel(half, start_ref, end_ref, empty_ref, nT_ref, first, second, pack_ref, *rest):
    pack_ref[: first.shape[0], :] = first[...]
    pack_ref[first.shape[0] :, :] = second[...]
    attention_forward(half, start_ref, end_ref, empty_ref, nT_ref, pack_ref, *rest)


def early_kernel(x_ref, m0, m1, pa0, pa1, small_ref, base_ref):
    local = m0.shape[0]
    mixed = jnp.concatenate([m[...].astype(BF) for m in (m0, m1)], axis=0)
    weight = jnp.concatenate([p[:D, 3 * local :] for p in (pa0, pa1)], axis=1)
    base_ref[...] = dot(mixed, weight, TT) + small_ref[2:3, :] + x_ref[...].astype(F32)


def out_kernel(base_ref, m2, m3, pa2, pa3, small_ref, hidden_ref, n2_ref, n2T_ref):
    local = m2.shape[0]
    mixed = jnp.concatenate([m[...].astype(BF) for m in (m2, m3)], axis=0)
    weight = jnp.concatenate([p[:D, 3 * local :] for p in (pa2, pa3)], axis=1)
    hidden = dot(mixed, weight, TT) + base_ref[...]
    hidden_ref[...] = hidden
    xhat, _ = norm_terms(hidden)
    n2 = (xhat * small_ref[3:4, :] + small_ref[4:5, :]).astype(BF)
    n2_ref[...] = n2
    n2T_ref[:D, :] = n2.T
    n2T_ref[D:, :] = (lax.broadcasted_iota(jnp.int32, (EXTRA, n2.shape[0]), 0) == 0).astype(F32).astype(BF)


def phi_terms(inner):
    density = jnp.exp2(inner * inner * -0.7213475204444817) * 0.3989422804014327
    t = 1.0 / (1.0 + 0.2316419 * jnp.abs(inner))
    tail = density * (t * (0.31938153 + t * (-0.356563782 + t * (1.781477937 + t * (-1.821255978 + t * 1.330274429)))))
    return jnp.where(inner >= 0, 1.0 - tail, tail), density


def ff_slots(n2, n2T, cot, packs, biases, grad_refs, act_refs, bias_ref, act_buf, gi_buf):
    parts = 2
    piece = n2.shape[0] // parts
    units = [(s, r) for s in range(len(packs)) for r in range(parts)]

    def enter(s, r):
        p = packs[s]
        at = slice(r * piece, (r + 1) * piece)
        w2 = jnp.concatenate([p[D : D + CHUNK, :], p[D + CHUNK : 2 * D, :]], axis=1)
        return dot(n2[at], p[:D, :], NN) + biases[s].astype(F32), dot(cot[at], w2, NT)

    ahead = enter(*units[0])
    for i, (s, r) in enumerate(units):
        inner, grad = ahead
        if i + 1 < len(units):
            ahead = enter(*units[i + 1])
        at = slice(r * piece, (r + 1) * piece)
        lanes = slice(s * CHUNK, (s + 1) * CHUNK)
        cdf, density = phi_terms(inner)
        act = (inner * cdf).astype(BF)
        act_buf[at, lanes] = act
        act_refs[s][at, :] = act
        gi_buf[at, lanes] = (grad * (cdf + inner * density)).astype(BF)
    w1 = jnp.concatenate([p[:D, :] for p in packs], axis=1)

    def rows_back(at):
        return dot(gi_buf[at], w1, NT)

    def first_grad():
        first = dot(n2T, gi_buf[...], NN)
        for s, ref in enumerate(grad_refs):
            at = slice(s * CHUNK, (s + 1) * CHUNK)
            ref[:D, :] = first[:D, at].astype(BF)
            bias_ref[s : s + 1, :] = first[D : D + 1, at]

    def second_grad():
        second = dot(act_buf[...], cot, TN).astype(BF)
        for s, ref in enumerate(grad_refs):
            at = slice(s * CHUNK, (s + 1) * CHUNK)
            ref[D : D + CHUNK, :] = second[at, :CHUNK]
            ref[D + CHUNK : 2 * D, :] = second[at, CHUNK:]

    return rows_back, first_grad, second_grad


def finish_slots(back_ref, back_in, steps):
    rows_back, first_grad, second_grad = steps
    everything = slice(0, back_ref.shape[0])
    back = rows_back(everything)
    back_ref[...] = back if back_in is None else back + back_in[...]
    first_grad()
    second_grad()


def expand_biases(first, *packs):
    return [p[D + 1 : D + 2, first : first + CHUNK] for p in packs]


def ff_kernel(n2_ref, n2T_ref, cot_ref, p0, p1, pa0, pa1, back_in, back_ref, g0, g1, act0, act1, bias_ref, act_buf, gi_buf):
    steps = ff_slots(n2_ref[...], n2T_ref[...], cot_ref[...], (p0, p1), expand_biases(0, pa0, pa1), (g0, g1), (act0, act1), bias_ref,
                     act_buf, gi_buf)
    finish_slots(back_ref, back_in, steps)


def ff_first_kernel(n2_ref, n2T_ref, cot_ref, p0, c0, c1, c2, pa0, pa1, back_ref, g0, d0, d1, act0, act1, bias_ref, act_buf, gi_buf):
    steps = ff_slots(n2_ref[...], n2T_ref[...], cot_ref[...], (p0, Rows(c0, c1, c2)), expand_biases(0, pa0, pa1), (g0, Rows(d0, d1)),
                     (act0, act1), bias_ref, act_buf, gi_buf)
    finish_slots(back_ref, None, steps)


def turn_kernel(n2_ref, n2T_ref, cot_ref, p0, p1, p2, p3, back_in, hidden_ref, m0, m1, m2, m3, pa0, pa1, pa2, pa3, small_in,
                gh_ref, dT0, dT1, dT2, dT3, g0, g1, g2, g3, o0, o2, o_send, act0, act1, act2, act3, bias_ref, small_ref,
                act_buf, gi_buf, low_buf):
    local = m0.shape[0]
    rows_back, first_grad, second_grad = ff_slots(
        n2_ref[...], n2T_ref[...], cot_ref[...], (p0, p1, p2, p3), expand_biases(CHUNK, pa0, pa1, pa2, pa3), (g0, g1, g2, g3),
        (act0, act1, act2, act3), bias_ref, act_buf, gi_buf)
    total = [0.0] * 4
    between = {0: first_grad, 1: second_grad}
    for r in range(hidden_ref.shape[0] // CHUNK):
        at = slice(r * CHUNK, (r + 1) * CHUNK)
        back = rows_back(at) + back_in[at, :]
        if r in between:
            between[r]()
        cot_f = cot_ref[at, :].astype(F32)
        xhat, scale = norm_terms(hidden_ref[at, :])
        grad_hidden = cot_f + norm_back(back, small_in[3:4, :], xhat, scale)
        gh_ref[at, :] = grad_hidden
        low_buf[at, :] = grad_hidden.astype(BF)
        for k, value in enumerate((grad_hidden, back * xhat, back, cot_f)):
            total[k] = total[k] + jnp.sum(value, axis=0, keepdims=True)
    for k in range(4):
        small_ref[k : k + 1, :] = total[k]
    low = low_buf[...]
    weight = jnp.concatenate([p[:D, 3 * local :] for p in (pa0, pa1, pa2, pa3)], axis=1)
    grads_T = dot(weight, low, TT).astype(BF)
    for s, ref in enumerate((dT0, dT1, dT2, dT3)):
        ref[...] = grads_T[s * local : (s + 1) * local]
    mixed = jnp.concatenate([m[...].astype(BF) for m in (m0, m1, m2, m3)], axis=0)
    grad = dot(mixed, low, NN).astype(BF)
    for s, (ref, first) in enumerate(((o0, 0), (o_send, 0), (o2, 0), (o_send, 2 * local))):
        for part in range(2):
            at = first + part * local
            ref[at : at + local, :] = grad[s * local : (s + 1) * local, part * CHUNK : (part + 1) * CHUNK]


def attention_backward(e_ref, dT_ref, inv_ref, mixed_ref, vT_ref, qT_ref, kT_ref, nT_ref, dq_ref, dkv_ref, grad_ref, bias_ref,
                       ds_buf):
    rows = qT_ref.shape[1]
    keys = kT_ref.shape[1]
    local = qT_ref.shape[0]
    heads = local // HEAD
    blocks = [(h, c) for h in range(heads) for c in range(rows // CHUNK)]
    which = lax.broadcasted_iota(jnp.int32, (EXTRA, CHUNK), 0)
    ones2 = (lax.broadcasted_iota(jnp.int32, (EXTRA, 2 * CHUNK), 0) < 2).astype(F32).astype(BF)
    lows = {}

    def enter(i):
        h, c = blocks[i]
        here = slice(h * HEAD, (h + 1) * HEAD)
        columns = slice(c * CHUNK, (c + 1) * CHUNK)
        low = (dT_ref[here, columns].astype(F32) * inv_ref[h : h + 1, columns]).astype(BF)
        delta = jnp.sum(low.astype(F32) * mixed_ref[here, columns], axis=0, keepdims=True)
        high = (-delta).astype(BF).astype(F32)
        extra = jnp.where(which == 0, high, jnp.where(which == 1, -delta - high, 0.0)).astype(BF)
        more = jnp.concatenate([low, extra], axis=0)
        lows[i] = low
        for k in range(keys // (2 * CHUNK)):
            span = slice(k * 2 * CHUNK, (k + 1) * 2 * CHUNK)
            v = jnp.concatenate([vT_ref[here, span], ones2], axis=0)
            ds_buf[i % 2, span, :] = (e_ref[h, c, span, :].astype(F32) * dot(v, more, TN)).astype(BF)

    dv = None
    dk = None
    enter(0)
    for i, (h, c) in enumerate(blocks):
        if i + 1 < len(blocks):
            enter(i + 1)
        here = slice(h * HEAD, (h + 1) * HEAD)
        columns = slice(c * CHUNK, (c + 1) * CHUNK)
        part = dot(lows[i], e_ref[h, c], NT)
        dv = part if c == 0 else dv + part
        dq_ref[here, columns] = (dot(kT_ref[here, :], ds_buf[i % 2], NN) * HEAD**-0.5).astype(BF)
        part = dot(qT_ref[here, columns], ds_buf[i % 2], NT)
        dk = part if c == 0 else dk + part
        if c == rows // CHUNK - 1:
            dkv_ref[here, :] = dk.astype(BF)
            dkv_ref[local + h * HEAD : local + (h + 1) * HEAD, :] = dv.astype(BF)
    for ref, count, columns in ((dq_ref, rows, slice(0, local)), (dkv_ref, keys, slice(local, 3 * local))):
        grad = dot(nT_ref[:, :count], ref[...], NT)
        grad_ref[:, columns] = grad[:D].astype(BF)
        bias_ref[:, columns] = grad[D : D + 1]


def first_kernel(half, x_ref, xs_ref, pa0, pa1, pa2, pa3, *rest):
    sources = rest[:8]
    small_two, b0, b1, b2, b3, f00, f01, f1, own_ref, sib_ref, small_ref = rest[8:]
    local = pa0.shape[1] // TENSOR
    rows = own_ref.shape[0]
    device = lax.axis_index("tensor")
    small_ref[...] = jnp.zeros(small_ref.shape, F32)
    gain_sum = 0.0
    shift_sum = 0.0
    for part, ref in enumerate((x_ref, xs_ref)):
        columns = slice(part * rows, (part + 1) * rows)
        total = None
        for slot, p in enumerate((pa0, pa1, pa2, pa3)):
            for index, lanes in ((0, slice(0, local)), (1, slice(local, 3 * local)))[part:]:
                term = dot(sources[slot * 2 + index][:, columns], p[:D, lanes], TT)
                total = term if total is None else total + term
        if part == 0:
            own_ref[...] = total
        else:
            sib_ref[...] = total.astype(BF)
        xhat, _ = norm_terms(ref[:half, :].astype(F32))
        gain_sum = gain_sum + jnp.sum(total[:half] * xhat, axis=0, keepdims=True)
        shift_sum = shift_sum + jnp.sum(total, axis=0, keepdims=True)
    small_ref[0:4, :] = small_two[...]
    small_ref[4:5, :] = gain_sum
    small_ref[5:6, :] = shift_sum
    for slot, b in enumerate((b0, b1, b2, b3)):
        owner = jnp.bitwise_xor(device, slot)
        small_ref[pl.ds(8 + owner, 1), :] = jnp.concatenate(
            [(f00, f01)[slot // 2][slot % 2 : slot % 2 + 1, :], f1[slot : slot + 1, :]], axis=1
        )
        small_ref[pl.ds(12 + owner, 1), : 3 * local] = b[...]


def branch_kernel(hidden_ref, small_ref, *rest):
    *refs, out_ref = rest
    acts, packs = refs[: 2 * TENSOR], refs[2 * TENSOR :]
    packs = packs[:3] + [Rows(*packs[3:6])] + packs[6:]
    act = jnp.concatenate([a[...] for a in acts], axis=1)
    weight = jnp.concatenate(
        [jnp.concatenate([p[D : D + CHUNK, :], p[D + CHUNK : 2 * D, :]], axis=1) for p in packs], axis=0
    )
    total = hidden_ref[...] + dot(act, weight, NN) + small_ref[5:6, :]
    out_ref[...] = total[: out_ref.shape[0]].astype(BF)


def last_kernel(x_ref, own_ref, got_ref, gh_ref, small_ref, out_ref):
    half = out_ref.shape[0]
    grad = own_ref[:half, :] + got_ref[:half, :].astype(F32)
    xhat, scale = norm_terms(x_ref[:half, :].astype(F32))
    out_ref[...] = gh_ref[:half, :] + norm_back(grad, small_ref[0:1, :], xhat, scale)


def place_of(bit):
    return lax.rem(lax.div(lax.axis_index("dp"), bit), 2)


def merge(kept, got, buf, bit=1):
    rows = kept.shape[0]
    upper = place_of(bit)
    buf[pl.ds(pl.multiple_of(upper * rows, rows), rows), :] = kept[...].astype(F32)
    buf[pl.ds(pl.multiple_of((1 - upper) * rows, rows), rows), :] = got[...].astype(F32)


def finish_ff_kernel(first, kept, got, expand_ref, reduce_ref, out_ref, second):
    local = out_ref.shape[0]
    merge(kept, got, second)
    for index, ref in enumerate((first, second)):
        lanes = slice(index * CHUNK, (index + 1) * CHUNK)
        expand_ref[:, lanes] = ref[:D, :].astype(F32)
        for part in range(2):
            rows = slice(D + part * CHUNK, D + (part + 1) * CHUNK)
            reduce_ref[lanes, part * CHUNK : (part + 1) * CHUNK] = ref[rows, :].astype(F32)
    for part in range(2):
        rows = slice(2 * D + part * local, 2 * D + (part + 1) * local)
        out_ref[:, part * CHUNK : (part + 1) * CHUNK] = second[rows, :]


def finish_qkv_kernel(kept, got, sums_ref, more_ref, q_ref, k_ref, v_ref, bias_q, bias_v, bias_ff, s0, s1, s2, s3, s4, s5, sums):
    half, local = kept.shape[0], q_ref.shape[1]
    upper = place_of(1)
    for index, ref in enumerate((q_ref, k_ref, v_ref)):
        lanes = slice(index * local, (index + 1) * local)
        ref[pl.ds(pl.multiple_of(upper * half, half), half), :] = kept[:, lanes].astype(F32)
        ref[pl.ds(pl.multiple_of((1 - upper) * half, half), half), :] = got[:, lanes].astype(F32)
        ref.flush()
    sums[...] = sums_ref[...] + more_ref[...]
    device = lax.axis_index("tensor")
    for index, ref in enumerate((s0, s1, s2, s3, s4, s5)):
        ref[...] = sums[index : index + 1, :].reshape(D)
    bias_ff[...] = sums[pl.ds(8 + device, 1), :].reshape(D)
    both = sums[pl.ds(12 + device, 1), :]
    bias_q[...] = both[:, :local].reshape(local)
    bias_v[...] = both[:, 2 * local : 3 * local].reshape(local)


class Chain:
    def __init__(self, along, size, halvings, pieces):
        bits = [1 << i for i in range(size.bit_length() - 1)]
        halvings = min(halvings, len(bits))
        self.along = along
        self.plan = [("half", b) for b in bits[:halvings]] + [("full", b) for b in bits[halvings:]]
        self.plan += [("back", b) for b in reversed(bits[:halvings])]
        self.at = -1
        self.pieces = pieces

    def left(self):
        return len(self.plan) - 1 - self.at

    def last(self):
        return tuple(self.pieces[0])

    def due(self):
        kind, bit = self.plan[self.at + 1]
        if kind == "half":
            return "halves", self.pieces, bit
        if self.at >= 0 and self.plan[self.at][0] == "back":
            return ("merge",) + tuple(self.pieces[0]) + (self.plan[self.at][1],)
        return "sum", self.pieces

    def taken(self, *results):
        self.at += 1
        send, keep = results if len(results) == 2 else results * 2
        self.pieces = [(keep, self.along(send, self.plan[self.at][1]))]


def swap(value, axis, size, bit):
    return lax.ppermute(value, axis, [(i, i ^ bit) for i in range(size)])


def on_device(dp, frames, query_weight, query_bias, key_weight, value_weight, value_bias, out_weight, out_bias, first_gain, first_shift,
              expand_weight, expand_bias, reduce_weight, reduce_bias, second_gain, second_shift, span_start, span_end, empty_flag, cotangent):
    half = frames.shape[0]
    rows = -(-half // CHUNK) * CHUNK
    keys = 2 * rows
    local = query_weight.shape[1]
    heads = local // HEAD
    blocks = rows // CHUNK
    line = Line()

    def across(v, bit):
        return swap(v, "tensor", TENSOR, bit)

    def along(v, bit):
        return swap(v, "dp", dp, bit)

    xs = across(frames, 1)
    pa0, small = line.run(
        pack_kernel, (shaped(D + EXTRA, 4 * local), shaped(8, D, dtype=F32)), "f" * 13,
        (query_weight, key_weight, value_weight, out_weight, query_bias, value_bias, expand_bias,
         first_gain, first_shift, out_bias, second_gain, second_shift, reduce_bias), us=2,
    )
    pa2 = across(pa0, 2)
    pa1 = across(pa0, 1)

    forward_outs = (
        (shaped(heads, blocks, keys, CHUNK), "V"), shaped(local, rows), shaped(local, keys), shaped(local, keys),
        shaped(local, rows, dtype=F32), shaped(heads, rows, dtype=F32),
    )
    forward_scratch = (
        pltpu.VMEM((2, keys, CHUNK), F32),
    )
    spans = (span_start, span_end, empty_flag)
    ff_weights = (expand_weight, reduce_weight)
    ff_shape = shaped(2 * D, CHUNK)
    normed, ff0, x, *s0 = line.run(
        functools.partial(start_kernel, half), (shaped(D + EXTRA, keys), ff_shape, shaped(rows, D)) + forward_outs, "sssfvvvff",
        spans + (frames, xs, small, pa0) + ff_weights, forward_scratch + (pltpu.VMEM((2, rows, D), BF),), us=8,
    )
    ff0_far = across(ff0, 2)
    ff0_near = across(ff0, 1)
    cot, ff1, *s1 = line.run(
        functools.partial(near_kernel, half), (shaped(rows, D), ff_shape) + forward_outs, "sssvvfff",
        spans + (normed, pa1, cotangent) + ff_weights, forward_scratch, us=7,
    )
    whole = shaped(rows, D, dtype=F32)
    (base,) = line.run(early_kernel, ((whole, "V"),), "v" * 6, (x, s0[4], s1[4], pa0, pa1, small), us=1)
    pa3 = [across(v, 1) for v in line.tick(("sum", [((pa2, 0, CHUNK),)]), ("sum", [((pa2, CHUNK, D + EXTRA - CHUNK),)]))]
    s2 = line.run(
        functools.partial(attention_forward, half), forward_outs, "sssvv", spans + (normed, pa2), forward_scratch, us=7,
    )
    ff1 = line.touch(ff1)
    ff1_far = across(ff1, 2)
    pa3, *s3 = line.run(
        functools.partial(cross_kernel, half), (shaped(D + EXTRA, 4 * local),) + forward_outs, "sssvvv",
        spans + (normed, *pa3), forward_scratch, us=7,
    )
    slots = (s0, s1, s2, s3)
    mixed = tuple(s[4] for s in slots)
    packs = (pa0, pa1, pa2, pa3)
    cuts = [(0, 384), (384, 320), (704, 320)]
    ff0_cross = [across(v, 1) for v in line.tick(*(("sum", [((ff0_far,) + cut,)]) for cut in cuts))]
    whole = shaped(rows, D, dtype=F32)
    hidden, n2, n2T = line.run(
        out_kernel, (whole, shaped(rows, D), shaped(D + EXTRA, rows)), "V" + "v" * 5, (base,) + mixed[2:] + packs[2:] + (small,), us=8,
    )
    ff1_near = across(ff1, 1)
    ff_scratch = (pltpu.VMEM((rows, TENSOR * CHUNK), BF), pltpu.VMEM((rows, TENSOR * CHUNK), BF))
    bias_shape = shaped(TENSOR, CHUNK, dtype=F32)
    ff_grads = (shaped(2 * D, CHUNK),) * TENSOR
    ff_acts = (shaped(rows, CHUNK),) * TENSOR
    two = (whole,) + ff_grads[:2] + ff_acts[:2] + (shaped(2, CHUNK, dtype=F32),)
    half_scratch = (pltpu.VMEM((rows, 2 * CHUNK), BF), pltpu.VMEM((rows, 2 * CHUNK), BF))
    back, a2, *a3, act2, act3, bias_far = line.run(
        ff_first_kernel, two[:2] + (shaped(D, CHUNK),) * 2 + two[3:], "v" * 9, (n2, n2T, cot, ff0_far, *ff0_cross, pa2, pa3), half_scratch,
        us=4, vmem=10,
    )
    got_a3 = [across(v, 1) for v in a3]
    back, a0, a1, act0, act1, bias_near = line.run(
        ff_kernel, two, "v" * 8, (n2, n2T, cot, ff0, ff0_near, pa0, pa1, back), half_scratch, us=4, vmem=10,
    )
    acts_a, bias_a = (act0, act1, act2, act3), (bias_near, bias_far)
    got_a1 = across(a1, 1)
    spare = jnp.zeros((EXTRA, CHUNK), BF)
    (far_a,) = line.tick(("sum", [((a2, i * D, D), v) for i, v in enumerate(got_a3)] + [(spare,)]))
    y_a = across(far_a, 2)
    ff1_far = line.touch(ff1_far)
    ff1_cross = across(ff1_far, 1)
    size_b = 2 * D + 2 * local
    grad_hidden, *rest = line.run(
        turn_kernel,
        ((whole, "V"),) + (shaped(local, rows),) * TENSOR + ff_grads
        + (shaped(2 * local, CHUNK), shaped(2 * local, CHUNK), shaped(4 * local, CHUNK)) + ff_acts + (bias_shape, shaped(4, D, dtype=F32)),
        "v" * 18,
        (n2, n2T, cot, ff1, ff1_near, ff1_far, ff1_cross, back, hidden) + mixed + packs + (small,),
        ff_scratch + (pltpu.VMEM((rows, D), BF),), us=12, vmem=11,
    )
    dT, (f0, f1, f2, f3, o0, o2, o_send) = rest[:TENSOR], rest[TENSOR : TENSOR + 7]
    acts_b, (bias_b, small_two) = rest[TENSOR + 7 : 2 * TENSOR + 7], rest[2 * TENSOR + 7 :]
    got_f1 = across(f1, 1)
    got_f3 = across(f3, 1)
    got_o = across(o_send, 1)

    backward_outs = (
        shaped(local, rows), shaped(2 * local, keys), shaped(D, 3 * local), shaped(1, 3 * local, dtype=F32),
    )

    def backward(slot):
        e, q, k, v, m, inv = slots[slot]
        return line.run(
            attention_backward, backward_outs, "V" + "v" * 7,
            (e, dT[slot], inv, m, v, q, k, normed), (pltpu.VMEM((2, keys, CHUNK), BF),), us=8, vmem=5,
        )

    def chain(halvings, pieces):
        return Chain(along, dp, halvings, pieces)

    *d3, g3, b3 = backward(3)
    chain_a = chain(1, [(a0, got_a1, (y_a, 0, 2 * D))])
    pair = 2 * local
    far_b, send_3, *halves = line.tick(
        ("sum", [(f2, got_f3), (o2, (got_o, pair, pair))]), ("sum", [(g3,)]), chain_a.due()
    )
    y_b = across(far_b, 2)
    got_3 = across(send_3, 1)
    chain_a.taken(*halves)
    *d2, g2, b2 = backward(2)
    spare = jnp.zeros((EXTRA, 3 * local), BF)
    far_q, whole_a = line.tick(("sum", [(g2, got_3), (spare,)]), chain_a.due())
    y_q = across(far_q, 2)
    chain_a.taken(whole_a)
    *d1, g1, b1 = backward(1)
    chain_b = chain(2, [(f0, got_f1, (y_b, 0, 2 * D)), (o0, (got_o, 0, pair), (y_b, 2 * D, pair))])
    send_1, whole_a, *halves = line.tick(("sum", [(g1,)]), chain_a.due(), chain_b.due())
    got_1 = across(send_1, 1)
    chain_a.taken(whole_a)
    chain_b.taken(*halves)
    *d0, g0, b0 = backward(0)
    chain_q = chain(2, [(g0, got_1, (y_q, 0, D))])
    send_q, keep_q, send_b, keep_b = line.tick(chain_q.due(), chain_b.due())
    chain_q.taken(send_q, keep_q)
    chain_b.taken(send_b, keep_b)
    own, sib, sums = line.run(
        functools.partial(first_kernel, half), (whole, shaped(rows, D), shaped(16, D, dtype=F32)), "v" * 22,
        (x, xs) + packs + (*d0, *d1, *d2, *d3, small_two, b0, b1, b2, b3) + bias_a + (bias_b,), us=6,
    )
    (sums,) = line.tick(("sum", [(sums,)]))
    pending = across(sums, 1)
    chain_q.taken(*line.tick(chain_q.due()))
    part_b, part_a, sums, sib = line.tick(chain_b.due(), chain_a.due(), ("sum", [(sums, pending)]), ("sum", [(sib,)]))
    chain_b.taken(part_b)
    chain_a.taken(part_a)
    pending = across(sums, 2)
    got = across(sib, 1)
    (grad_frames,) = line.run(
        last_kernel, ((shaped(half, D, dtype=F32), "f"),), "vvvVv", (x, own, got, grad_hidden, small), us=4
    )
    bits = [1 << i for i in range(dp.bit_length() - 1)]

    def step(*chains, more=()):
        nonlocal sums, pending
        chains = [c for c in chains if c.left()]
        with_sums = bool(bits)
        jobs = [c.due() for c in chains] + [("sum", [(sums, pending)])] * with_sums + list(more)
        if not jobs:
            return ()
        made = list(line.tick(*jobs))
        for c in chains:
            c.taken(made.pop(0))
        if with_sums:
            sums = made.pop(0)
            pending = along(sums, bits.pop(0))
        return made

    step(chain_q, chain_b, chain_a)
    (output,) = line.run(
        branch_kernel, ((shaped(half, D), "f"),), "v" * 20,
        (hidden, small) + tuple(acts_a) + tuple(acts_b) + (ff0, ff0_near, ff0_far, *ff0_cross, ff1, ff1_near, ff1_far, ff1_cross), us=3,
    )
    while chain_a.left() or chain_b.left() > 1:
        step(chain_q, chain_b, chain_a)
    (whole_a,) = step(chain_q, chain_b, more=(("merge",) + chain_a.last() + (1,),))
    while bits or chain_q.left():
        step(chain_q)
    grad_expand, grad_reduce, grad_out = line.run(
        finish_ff_kernel, tuple((shaped(*o, dtype=F32), "f") for o in ((D, 2 * CHUNK), (2 * CHUNK, D), (local, D))),
        "vvv", (whole_a,) + chain_b.last(), (pltpu.VMEM((size_b, CHUNK), F32),), us=2,
    )
    vector = (shaped(D, dtype=F32), "f")
    short = (shaped(local, dtype=F32), "f")
    grad_q, grad_k, grad_v, bias_q, bias_v, bias_ff, *globals_ = line.run(
        finish_qkv_kernel, ((shaped(D, local, dtype=F32), "f"),) * 3 + (short, short, vector) + (vector,) * 6, "vvvv",
        chain_q.last() + (sums, pending), (pltpu.VMEM(sums.shape, F32),), us=1,
    )
    return (
        output, grad_frames, grad_q, bias_q, grad_k, grad_v, bias_v, grad_out, globals_[0], globals_[4], globals_[5],
        grad_expand, bias_ff, grad_reduce, globals_[3], globals_[1], globals_[2],
    )


def solution(mesh):
    dp = mesh.shape["dp"]
    assert mesh.shape["tensor"] == TENSOR and dp & (dp - 1) == 0
    split = P(("dp", "tensor"), None)
    column = P(None, "tensor")
    return jax.shard_map(
        functools.partial(on_device, dp),
        mesh=mesh,
        in_specs=(
            split, column, P("tensor"), column, column, P("tensor"), P("tensor", None), P(), P(), P(),
            column, P("tensor"), P("tensor", None), P(), P(), P(), P("dp"), P("dp"), P("dp"), split,
        ),
        out_specs=(
            split, split, column, P("tensor"), column, column, P("tensor"), P("tensor", None), P(), P(), P(),
            column, P("tensor"), P("tensor", None), P(), P(), P(),
        ),
        check_vma=False,
    )
```
